32 devices in a mesh: dp: 4 (over y, x), ctx: 8 (over z, core).
Axes of the slice: x: 2, y: 2, z: 4, core: 2. Of those that a mesh axis runs over, the one named last changes fastest.
Arguments:
- queries: bfloat16 [4, 1024, 2048], P('dp', 'ctx'), may hold values from -5 to 5
- key_rows: bfloat16 [4, 1024, 256], P('dp', 'ctx'), may hold values from -5 to 5
- value_stored_rows: bfloat16 [4, 1024, 256], P('dp', 'ctx'), may hold values from -6 to 6
- out_grad: bfloat16 [4, 1024, 2048], P('dp', 'ctx'), may hold values from -6 to 6
- documents: int32 [4, 1024], P('dp', 'ctx'), may hold values from 0 to 15, never falling along the last dimension, each value on 1 to 512 neighbouring positions
- swapped: int32 [4, 8, 4], P('dp', 'ctx'), may hold values from 0 to 1, as said below
Outputs:
- attended: bfloat16 [4, 1024, 2048], P('dp', 'ctx')
- query_grad: bfloat16 [4, 1024, 2048], P('dp', 'ctx')
- key_gradient_store: bfloat16 [4, 1024, 256], P('dp', 'ctx')
- value_gradient_store: bfloat16 [4, 1024, 256], P('dp', 'ctx')
The draws below stay inside these ranges and needn't reach their ends.
Inputs may be any that keep to these rules, and one draw needn't show every extreme that they name: swapped[g, r, b] equals swapped[(g + 2) mod 4, r, b]. `documents`: document numbers never fall along a group's sequence; a document has 1 to 512 positions.
All inputs are finite; a program needn't handle non-finite values.
Results may differ from the reference program's by a relative error of at most 0.024.
Values may be sent and summed in bfloat16 or wider, within the bound.
No kernel may reach another device: no remote copies, remote signals or barrier semaphores. Data moves between devices by JAX's collectives and lax.ppermute only.
A program may use at most 64 MiB of HBM per device.

```python
import math
import jax
import jax.numpy as jnp
import numpy as np
from jax import lax

HEAD_SIZE = 128
QUERY_PER_KEY = 8
KEY_VALUE_HEADS = 2
HQ = 16
PACKED_LENGTH = 1024
DATA_GROUPS = 4
RANKS = 8
NBLK = 4


def draw_queries(key, part):
    key = jax.random.fold_in(key, 3)
    start_offset = jnp.clip(jax.random.normal(key, (DATA_GROUPS, PACKED_LENGTH, HQ * HEAD_SIZE), jnp.float32), -5.0, 5.0)
    return start_offset.astype(jnp.bfloat16)


def draw_key_rows(key, part):
    key = jax.random.fold_in(key, 5)
    start_offset = jnp.clip(jax.random.normal(key, (DATA_GROUPS, PACKED_LENGTH, KEY_VALUE_HEADS * HEAD_SIZE), jnp.float32), -5.0, 5.0)
    return start_offset.astype(jnp.bfloat16)


def draw_swapped(key, part):
    key = jax.random.fold_in(key, 7)
    first_half = jax.random.randint(key, (DATA_GROUPS // 2, RANKS, NBLK), 0, 2, jnp.int32)
    return jnp.concatenate([first_half, first_half], axis=0)


def steps_of(rng, dims, cuts, least, high):
    loudness, own = 1.0, jax.random.fold_in(rng, 6)
    for dim, shards_of in cuts:
        draws = jnp.exp(jax.random.uniform(jax.random.fold_in(own, dim), (shards_of,), jnp.float32, least / len(cuts), high / len(cuts)))
        loudness = loudness * jnp.repeat(draws, dims[dim] // shards_of).reshape([-1 if axis == dim else 1 for axis in range(len(dims))])
    return loudness


def length_profile(count, total, most, slope):
    loads = [(1 << 20) // math.isqrt(standing ** slope) + 1 for standing in range(2, count + 1)]
    spare, given = total - most - (count - 1), [1] * (count - 1)
    while spare > 0:
        free = [i for i in range(count - 1) if given[i] < most]
        whole, remaining = sum([loads[i] for i in free]), spare
        for i in free:
            extra = min(most - given[i], max(1, remaining * loads[i] // whole), spare)
            given[i] = given[i] + extra
            spare = spare - extra
    return np.array([most] + given)


def uneven(rng, count, total, limit, slope):
    if count == 2:
        one = jax.random.randint(rng, (), max(1, total - limit), min(limit, total - 1) + 1)
        return jnp.stack([one, total - one])
    sizes = jnp.asarray(length_profile(count, total, limit, slope), jnp.int32)
    pairs = (count - 1) // 2
    donor, taker = sizes[1:1 + 2 * pairs:2], sizes[2:2 + 2 * pairs:2]
    margin = jnp.minimum(donor - 1, limit - taker)
    shifted = jax.random.randint(jax.random.fold_in(rng, 1), (pairs,), 0, 1 << 20) % (margin + 1)
    sizes = sizes.at[1:1 + 2 * pairs:2].set(donor - shifted).at[2:2 + 2 * pairs:2].set(taker + shifted)
    return sizes[jax.random.permutation(jax.random.fold_in(rng, 2), count)]


def gaussian(stream_key, shape, scale, bound, pieces=(), held_as=jnp.bfloat16):
    values = scale * jax.random.normal(stream_key, shape, jnp.float32)
    if pieces:
        values = values * steps_of(stream_key, shape, pieces, -0.22, 0.18)
    return jnp.clip(values, -bound, bound).astype(held_as)


def setup_inputs(seed: int = 0) -> dict:
    splits = jax.random.split(jax.random.key(seed), 7)
    queries = draw_queries(jax.random.fold_in(splits[6], 71), 0)
    key_rows = draw_key_rows(jax.random.fold_in(splits[6], 71), 0)
    value_stored_rows = gaussian(splits[2], (DATA_GROUPS, PACKED_LENGTH, KEY_VALUE_HEADS * HEAD_SIZE), 1.0, 6.0, ((0, 4), (1, 8)))
    out_grad = gaussian(splits[3], (DATA_GROUPS, PACKED_LENGTH, HQ * HEAD_SIZE), 1.0, 6.0, ((0, 4), (1, 8)))
    documents = jax.vmap(lambda own: jnp.searchsorted(jnp.cumsum(uneven(own, 16, PACKED_LENGTH, PACKED_LENGTH // 2, 2)), jnp.arange(PACKED_LENGTH), side="right"))(jax.random.split(splits[4], DATA_GROUPS)).reshape((DATA_GROUPS, PACKED_LENGTH)).astype(jnp.int32)
    swapped = draw_swapped(jax.random.fold_in(splits[6], 71), 0)
    return dict(queries=queries, key_rows=key_rows, value_stored_rows=value_stored_rows, out_grad=out_grad, documents=documents, swapped=swapped)


def unswap(stacked, swapped):
    groups, sequence_length, feature_width = stacked.shape
    blocked = stacked.reshape(groups, swapped.shape[1], swapped.shape[2], -1, feature_width)
    partner = jnp.roll(blocked, groups // 2, axis=0)
    chosen = (swapped == 1)[:, :, :, None, None]
    return jnp.where(chosen, partner, blocked).reshape(stacked.shape)

def one_head(operands, doc_ids):
    query_head, key_head, value_head, grad_head = operands
    sequence_length, head_width = query_head.shape
    score_scale = 1.0 / math.sqrt(head_width)
    positions = jnp.arange(sequence_length, dtype=jnp.int32)
    raw_scores = jnp.dot(query_head, key_head.T, preferred_element_type=jnp.float32) * score_scale
    allowed = (positions[None, :] <= positions[:, None]) & (doc_ids[None, :] == doc_ids[:, None])
    masked = jnp.where(allowed, raw_scores, -jnp.inf)
    row_max = lax.optimization_barrier(jnp.max(masked, axis=1))
    log_total = row_max + jnp.log(lax.optimization_barrier(jnp.sum(jnp.exp(masked - row_max[:, None]), axis=1)))
    probabilities = jnp.exp(masked - log_total[:, None])
    weights = probabilities.astype(jnp.bfloat16)
    attended = jnp.dot(weights, value_head, preferred_element_type=jnp.float32).astype(jnp.bfloat16)
    row_delta = lax.optimization_barrier(jnp.sum(grad_head.astype(jnp.float32) * attended.astype(jnp.float32), axis=1))
    prob_grad = jnp.dot(grad_head, value_head.T, preferred_element_type=jnp.float32)
    score_grad = (probabilities * (prob_grad - row_delta[:, None])).astype(jnp.bfloat16)
    query_grad = (jnp.dot(score_grad, key_head, preferred_element_type=jnp.float32) * score_scale).astype(jnp.bfloat16)
    key_gradient_store = jnp.dot(score_grad.T, query_head, preferred_element_type=jnp.float32) * score_scale
    value_gradient_store = jnp.dot(weights.T, grad_head, preferred_element_type=jnp.float32)
    return (attended, query_grad, key_gradient_store, value_gradient_store)

def one_group(operands):
    query_rows, key_portion, value_portion, grad_rows, doc_ids = operands
    sequence_length = query_rows.shape[0]

    def head_major_rows(weight_matrix, head_count):
        return weight_matrix.reshape(sequence_length, head_count, HEAD_SIZE).transpose(1, 0, 2)

    def rows_first(stacked):
        return stacked.transpose(1, 0, 2).reshape(sequence_length, -1)
    query_heads = head_major_rows(query_rows, HQ)
    key_head_rows = jnp.repeat(head_major_rows(key_portion, KEY_VALUE_HEADS), QUERY_PER_KEY, axis=0)
    value_head_rows = jnp.repeat(head_major_rows(value_portion, KEY_VALUE_HEADS), QUERY_PER_KEY, axis=0)
    grad_heads = head_major_rows(grad_rows, HQ)
    attended, query_grad, key_gradient_store, value_gradient_store = lax.map(lambda operand: one_head(operand, doc_ids), (query_heads, key_head_rows, value_head_rows, grad_heads))
    key_grad_total = key_gradient_store.reshape(KEY_VALUE_HEADS, QUERY_PER_KEY, sequence_length, HEAD_SIZE).sum(axis=1).astype(jnp.bfloat16)
    value_grad_total = value_gradient_store.reshape(KEY_VALUE_HEADS, QUERY_PER_KEY, sequence_length, HEAD_SIZE).sum(axis=1).astype(jnp.bfloat16)
    return (rows_first(attended), rows_first(query_grad), rows_first(key_grad_total), rows_first(value_grad_total))

def reference(queries, key_rows, value_stored_rows, out_grad, documents, swapped):
    query_home = unswap(queries, swapped)
    key_home = unswap(key_rows, swapped)
    value_home = unswap(value_stored_rows, swapped)
    grad_home = unswap(out_grad, swapped)
    attended, query_grad, key_gradient_store, value_gradient_store = lax.map(one_group, (query_home, key_home, value_home, grad_home, documents))
    return (unswap(attended, swapped), unswap(query_grad, swapped), unswap(key_gradient_store, swapped), unswap(value_gradient_store, swapped))
```

```python
import functools
import math

import jax
import jax.numpy as jnp
from jax import lax
from jax.experimental import pallas as pl
from jax.experimental.pallas import tpu as pltpu
from jax.sharding import Mesh
from jax.sharding import PartitionSpec as P

HEAD_SIZE = 128
QUERY_PER_KEY = 8
KEY_VALUE_HEADS = 2
NBLK = 4
META = 16
FLAG_ROW, TILED_ROW, DOC_ROW = 0, 4, 8
NEG = -1e30
F32, BF16 = jnp.float32, jnp.bfloat16
NT = (((1,), (1,)), ((), ()))


def payload_of(key_rows, value_rows, docs, flags):
    rows, width = key_rows.shape
    per_block = rows // NBLK
    flag_rows = jnp.broadcast_to(flags.astype(BF16)[:, None], (NBLK, width))
    docs = docs.astype(BF16)
    tiled = jnp.tile(docs.reshape(NBLK, per_block), (1, width // per_block))
    doc_row = jnp.tile(docs.reshape(1, rows), (1, width // rows))
    meta = jnp.concatenate(
        [flag_rows, tiled, doc_row, jnp.zeros((META - 2 * NBLK - 1, width), BF16)], axis=0
    )
    return jnp.concatenate([key_rows, value_rows, meta], axis=0)


def attention_kernel(
    window,
    place_ref,
    swap_ref,
    query_ref,
    grad_ref,
    gathered_ref,
    out_ref,
    query_grad_ref,
    partial_ref,
    key_log,
    value_log,
    key_turned,
    value_turned,
    doc_column,
    doc_row,
    key_total,
    value_total,
):
    rows = query_ref.shape[0]
    per_block = rows // NBLK
    lanes = QUERY_PER_KEY * per_block
    half, rank = place_ref[0], place_ref[1]
    ranks = gathered_ref.shape[1]
    scale = 1.0 / math.sqrt(HEAD_SIZE)
    factor = scale * math.log2(math.e)

    key_total[...] = jnp.zeros_like(key_total)
    value_total[...] = jnp.zeros_like(value_total)
    partial_ref[...] = jnp.zeros_like(partial_ref)
    doc_row[...] = jnp.full_like(doc_row, 1e4)

    for slot in range(window):
        source = rank - (window - 1) + slot
        valid = source >= 0
        index = jnp.maximum(source, 0)
        for stored in range(2):
            docs = gathered_ref[stored, index, pl.ds(2 * rows, META), :].astype(F32)
            docs = docs[DOC_ROW : DOC_ROW + 1, :rows]
            docs = jnp.where(valid, docs, -1.0)
            doc_row[stored, slot : slot + 1, :] = docs
            doc_column[stored, slot * rows : (slot + 1) * rows, :] = jnp.broadcast_to(
                docs, (rows, rows)
            ).T
        flags = gathered_ref[0, index, pl.ds(2 * rows, META), :].astype(F32)
        for block in range(NBLK):
            flag = flags[FLAG_ROW + block : FLAG_ROW + block + 1, :]
            mask = jnp.broadcast_to(flag, (per_block, flag.shape[1])) > 0.5
            at = slot * rows + block * per_block
            for which, log in ((0, key_log), (1, value_log)):
                part = pl.ds(which * rows + block * per_block, per_block)
                first = gathered_ref[0, index, part, :].astype(F32)
                second = gathered_ref[1, index, part, :].astype(F32)
                for own, other, logical in ((first, second, 0), (second, first, 1)):
                    merged = jnp.where(mask, other, own).astype(BF16)
                    for head in range(KEY_VALUE_HEADS):
                        log[logical, head, at : at + per_block, :] = merged[
                            :, head * HEAD_SIZE : (head + 1) * HEAD_SIZE
                        ]
    for logical in range(2):
        for head in range(KEY_VALUE_HEADS):
            key_turned[logical, head] = key_log[logical, head].T
            value_turned[logical, head] = value_log[logical, head].T

    def unit(block, logical, head, chunks, doc_lanes):
        first = (window - chunks) * rows
        span = pl.ds(first, chunks * rows)
        at = pl.ds(pl.multiple_of(block * per_block, per_block), per_block)
        columns = [
            slice((head * QUERY_PER_KEY + h) * HEAD_SIZE, (head * QUERY_PER_KEY + h + 1) * HEAD_SIZE)
            for h in range(QUERY_PER_KEY)
        ]
        query = jnp.concatenate([query_ref[at, column] for column in columns], axis=0)
        grad = jnp.concatenate([grad_ref[at, column] for column in columns], axis=0)
        keys = key_log[logical, head, span, :]
        values = value_log[logical, head, span, :]
        scores = lax.dot_general(keys, query, NT, preferred_element_type=F32)
        same = doc_column[logical, span, :] == doc_lanes
        key_place = lax.broadcasted_iota(jnp.int32, same.shape, 0) - (chunks - 1) * rows
        row_place = block * per_block + lax.rem(
            lax.broadcasted_iota(jnp.int32, same.shape, 1), per_block
        )
        allowed = same & (key_place <= row_place)
        width = same.shape[1]
        scores = jnp.concatenate(
            [
                jnp.where(allowed, scores[:, lane : lane + width], NEG)
                for lane in range(0, lanes, width)
            ],
            axis=1,
        )
        peak = jnp.max(scores, axis=0, keepdims=True)
        powers = jnp.exp2((scores - peak) * factor)
        inverse = 1.0 / jnp.sum(powers, axis=0, keepdims=True)
        probs = powers * inverse
        weights = probs.astype(BF16)
        out_turned = jnp.dot(
            value_turned[logical, head, :, span], weights, preferred_element_type=F32
        ).astype(BF16)
        delta = jnp.sum(
            grad.T.astype(F32) * out_turned.astype(F32), axis=0, keepdims=True
        )
        prob_grad = lax.dot_general(values, grad, NT, preferred_element_type=F32)
        score_grad = (probs * (prob_grad - delta)).astype(BF16)
        query_grad_turned = jnp.dot(
            key_turned[logical, head, :, span], score_grad, preferred_element_type=F32
        )
        key_total[logical, head, span, :] += jnp.dot(
            score_grad, query, preferred_element_type=F32
        )
        value_total[logical, head, span, :] += jnp.dot(
            weights, grad, preferred_element_type=F32
        )
        out = out_turned.T
        query_grad = (query_grad_turned * scale).astype(BF16).T
        for h, column in enumerate(columns):
            out_ref[at, column] = out[h * per_block : (h + 1) * per_block, :]
            query_grad_ref[at, column] = query_grad[h * per_block : (h + 1) * per_block, :]

    def row_block(block, carry):
        logical = half ^ swap_ref[block]
        meta = gathered_ref[logical, rank, pl.ds(2 * rows, META), :].astype(F32)
        pick = lax.broadcasted_iota(jnp.int32, meta.shape, 0) == TILED_ROW + block
        doc_lanes = jnp.max(jnp.where(pick, meta, -1.0), axis=0, keepdims=True)
        lowest = jnp.min(doc_lanes)
        skipped = jnp.sum((doc_row[logical] < lowest).astype(F32)).astype(jnp.int32)
        needed = window - skipped // rows
        doc_lanes = doc_lanes[:, :HEAD_SIZE]
        for chunks in range(1, window + 1):

            @pl.when(needed == chunks)
            def _():
                for head in range(KEY_VALUE_HEADS):
                    unit(block, logical, head, chunks, doc_lanes)

        return carry

    lax.fori_loop(0, NBLK, row_block, 0)

    for slot in range(window):
        source = rank - (window - 1) + slot

        @pl.when(source >= 0)
        def _(slot=slot, source=source):
            flags = gathered_ref[0, source, pl.ds(2 * rows, META), :].astype(F32)
            for block in range(NBLK):
                at = slot * rows + block * per_block
                for head in range(KEY_VALUE_HEADS):
                    side = slice(head * HEAD_SIZE, (head + 1) * HEAD_SIZE)
                    flag = flags[FLAG_ROW + block : FLAG_ROW + block + 1, side]
                    mask = jnp.broadcast_to(flag, (per_block, HEAD_SIZE)) > 0.5
                    for which, total, gain in ((0, key_total, scale), (1, value_total, 1.0)):
                        part = pl.ds(which * rows + block * per_block, per_block)
                        first = total[0, head, at : at + per_block, :] * gain
                        second = total[1, head, at : at + per_block, :] * gain
                        partial_ref[0, source, part, side] = jnp.where(
                            mask, second, first
                        ).astype(BF16)
                        partial_ref[1, source, part, side] = jnp.where(
                            mask, first, second
                        ).astype(BF16)


def local(queries, key_rows, value_rows, out_grad, documents, swapped):
    ranks = lax.axis_size("ctx")
    window = ranks // 2 + 1
    rows, width = key_rows.shape[1:]
    payload = payload_of(key_rows[0], value_rows[0], documents[0], swapped[0, 0])
    gathered = lax.all_gather(payload, ("half", "ctx"), axis=0, tiled=False)
    gathered = gathered.reshape(2, ranks, *payload.shape)
    place = jnp.stack([lax.axis_index("half"), lax.axis_index("ctx")]).astype(jnp.int32)
    vmem = pl.BlockSpec(memory_space=pltpu.VMEM)
    smem = pl.BlockSpec(memory_space=pltpu.SMEM)
    heads = KEY_VALUE_HEADS
    keys = window * rows
    out, query_grad, partial = pl.pallas_call(
        functools.partial(attention_kernel, window),
        out_shape=[
            jax.ShapeDtypeStruct(queries.shape[1:], BF16),
            jax.ShapeDtypeStruct(queries.shape[1:], BF16),
            jax.ShapeDtypeStruct((2, ranks, 2 * rows, width), BF16),
        ],
        in_specs=[smem, smem, vmem, vmem, vmem],
        out_specs=[vmem] * 3,
        scratch_shapes=[
            pltpu.VMEM((2, heads, keys, HEAD_SIZE), BF16),
            pltpu.VMEM((2, heads, keys, HEAD_SIZE), BF16),
            pltpu.VMEM((2, heads, HEAD_SIZE, keys), BF16),
            pltpu.VMEM((2, heads, HEAD_SIZE, keys), BF16),
            pltpu.VMEM((2, keys, rows), F32),
            pltpu.VMEM((2, 16, rows), F32),
            pltpu.VMEM((2, heads, keys, HEAD_SIZE), F32),
            pltpu.VMEM((2, heads, keys, HEAD_SIZE), F32),
        ],
        compiler_params=pltpu.CompilerParams(vmem_limit_bytes=48 * 1024 * 1024),
        cost_estimate=pl.CostEstimate(
            flops=12 * rows * keys * 2048, bytes_accessed=8 * 1024 * 1024, transcendentals=rows * keys * 16
        ),
    )(place, swapped[0, 0], queries[0], out_grad[0], gathered)
    summed = lax.psum_scatter(
        partial.reshape(2 * ranks, 2 * rows, width), ("half", "ctx"), scatter_dimension=0, tiled=False
    )
    return (out[None], query_grad[None], summed[None, :rows], summed[None, rows:])


def solution(mesh):
    groups, ranks = mesh.devices.shape
    wide = Mesh(mesh.devices.reshape(2, groups // 2, ranks), ("half", "pair", "ctx"))
    spec3 = P(("half", "pair"), "ctx", None)
    in_specs = (spec3, spec3, spec3, spec3, P(("half", "pair"), "ctx"), spec3)
    return jax.shard_map(
        local, mesh=wide, in_specs=in_specs, out_specs=(spec3,) * 4, check_vma=False
    )
```

```python
import functools
import math

import jax
import jax.numpy as jnp
from jax import lax
from jax.experimental import pallas as pl
from jax.experimental.pallas import tpu as pltpu
from jax.sharding import Mesh
from jax.sharding import PartitionSpec as P

HEAD_SIZE = 128
QUERY_PER_KEY = 8
KEY_VALUE_HEADS = 2
NBLK = 4
META = 16
DOC_ROW = NBLK
NEG = -1e30
F32, BF16 = jnp.float32, jnp.bfloat16
NT = (((1,), (1,)), ((), ()))


def payload_kernel(swap_ref, key_ref, value_ref, docs_ref, payload_ref):
    rows, width = key_ref.shape
    payload_ref[:rows, :] = key_ref[...]
    payload_ref[rows : 2 * rows, :] = value_ref[...]
    docs = jnp.broadcast_to(docs_ref[...].astype(F32), (META, rows))
    docs = jnp.concatenate([docs] * (width // rows), axis=1)
    place = lax.broadcasted_iota(jnp.int32, docs.shape, 0)
    meta = jnp.where(place == DOC_ROW, docs, 0.0)
    for block in range(NBLK):
        meta = jnp.where(place == block, swap_ref[block].astype(F32), meta)
    payload_ref[2 * rows :, :] = meta.astype(BF16)


def attention_kernel(
    hops,
    place_ref,
    swap_ref,
    query_ref,
    grad_ref,
    *refs,
):
    window = 2 * hops + 1
    count = hops + 1
    blocks = refs[: 4 * count]
    out_ref, query_grad_ref, home_ref, home_side_ref, away_ref, away_side_ref = refs[
        4 * count : 4 * count + 6
    ]
    (
        key_log,
        value_log,
        key_turned,
        value_turned,
        doc_column,
        doc_row,
        doc_tiled,
        key_total,
        value_total,
    ) = refs[4 * count + 6 :]
    rows = query_ref.shape[0]
    per_block = rows // NBLK
    lanes = QUERY_PER_KEY * per_block
    core, chip = place_ref[0], place_ref[1]
    scale = 1.0 / math.sqrt(HEAD_SIZE)
    factor = scale * math.log2(math.e)

    key_total[...] = jnp.zeros_like(key_total)
    value_total[...] = jnp.zeros_like(value_total)
    doc_row[...] = jnp.full_like(doc_row, 1e4)

    def place_slot(home, away, valid, slot):
        base = pl.multiple_of(slot * rows, rows)
        for logical, ref in ((0, home), (1, away)):
            meta = ref[2 * rows :, :rows].astype(F32)
            docs = jnp.where(valid, meta[DOC_ROW : DOC_ROW + 1, :], -1.0)
            doc_row[logical, pl.ds(slot, 1), :] = docs
            doc_column[logical, pl.ds(base, rows), :] = jnp.broadcast_to(
                docs, (rows, rows)
            ).T
        flags = home[2 * rows :, :].astype(F32)
        for block in range(NBLK):
            mask = jnp.broadcast_to(flags[block : block + 1, :], (per_block, flags.shape[1])) > 0.5
            at = pl.ds(base + block * per_block, per_block)
            for which, log in ((0, key_log), (1, value_log)):
                part = slice(which * rows + block * per_block, which * rows + (block + 1) * per_block)
                first = home[part, :].astype(F32)
                second = away[part, :].astype(F32)
                for own, other, logical in ((first, second, 0), (second, first, 1)):
                    merged = jnp.where(mask, other, own).astype(BF16)
                    for head in range(KEY_VALUE_HEADS):
                        log[logical, head, at, :] = merged[
                            :, head * HEAD_SIZE : (head + 1) * HEAD_SIZE
                        ]

    for k in range(count):
        home, away, home_side, away_side = (blocks[kind * count + k] for kind in range(4))
        slot = window - 1 - 2 * k
        side_slot = slot + 1 - 2 * core
        place_slot(home, away, chip >= k, slot)

        @pl.when((side_slot >= 0) & (side_slot < window))
        def _(home_side=home_side, away_side=away_side, k=k, side_slot=side_slot):
            place_slot(home_side, away_side, chip >= k, side_slot)

    for logical in range(2):
        for head in range(KEY_VALUE_HEADS):
            key_turned[logical, head] = key_log[logical, head].T
            value_turned[logical, head] = value_log[logical, head].T
        docs = jnp.broadcast_to(doc_row[logical, window - 1 : window, :], (8, rows))
        turns = [docs] + [
            pltpu.roll(docs, t * per_block, 1) for t in range(1, NBLK)
        ]
        group = lax.broadcasted_iota(jnp.int32, docs.shape, 1) // per_block
        for block in range(NBLK):
            tiled = turns[0]
            for t in range(1, NBLK):
                tiled = jnp.where(group == (block + t) % NBLK, turns[t], tiled)
            doc_tiled[logical, block : block + 1, :] = tiled[:1]

    def unit(block, logical, head, chunks, doc_lanes):
        first = (window - chunks) * rows
        span = pl.ds(first, chunks * rows)
        at = pl.ds(pl.multiple_of(block * per_block, per_block), per_block)
        columns = [
            slice((head * QUERY_PER_KEY + h) * HEAD_SIZE, (head * QUERY_PER_KEY + h + 1) * HEAD_SIZE)
            for h in range(QUERY_PER_KEY)
        ]
        query = jnp.concatenate([query_ref[at, column] for column in columns], axis=0)
        grad = jnp.concatenate([grad_ref[at, column] for column in columns], axis=0)
        keys = key_log[logical, head, span, :]
        values = value_log[logical, head, span, :]
        scores = lax.dot_general(keys, query, NT, preferred_element_type=F32)
        same = doc_column[logical, span, :] == doc_lanes
        key_place = lax.broadcasted_iota(jnp.int32, same.shape, 0) - (chunks - 1) * rows
        row_place = block * per_block + lax.rem(
            lax.broadcasted_iota(jnp.int32, same.shape, 1), per_block
        )
        allowed = same & (key_place <= row_place)
        width = same.shape[1]
        scores = jnp.concatenate(
            [
                jnp.where(allowed, scores[:, lane : lane + width], NEG)
                for lane in range(0, lanes, width)
            ],
            axis=1,
        )
        peak = jnp.max(scores, axis=0, keepdims=True)
        powers = jnp.exp2((scores - peak) * factor)
        inverse = 1.0 / jnp.sum(powers, axis=0, keepdims=True)
        probs = powers * inverse
        weights = probs.astype(BF16)
        out_turned = jnp.dot(
            value_turned[logical, head, :, span], weights, preferred_element_type=F32
        ).astype(BF16)
        delta = jnp.sum(
            grad.T.astype(F32) * out_turned.astype(F32), axis=0, keepdims=True
        )
        prob_grad = lax.dot_general(values, grad, NT, preferred_element_type=F32)
        score_grad = (probs * (prob_grad - delta)).astype(BF16)
        query_grad_turned = jnp.dot(
            key_turned[logical, head, :, span], score_grad, preferred_element_type=F32
        )
        key_total[logical, head, span, :] += jnp.dot(
            score_grad, query, preferred_element_type=F32
        )
        value_total[logical, head, span, :] += jnp.dot(
            weights, grad, preferred_element_type=F32
        )
        out = out_turned.T
        query_grad = (query_grad_turned * scale).astype(BF16).T
        for h, column in enumerate(columns):
            out_ref[at, column] = out[h * per_block : (h + 1) * per_block, :]
            query_grad_ref[at, column] = query_grad[h * per_block : (h + 1) * per_block, :]

    def row_block(block, carry):
        logical = swap_ref[block]
        doc_lanes = doc_tiled[logical, pl.ds(block, 1), :]
        lowest = jnp.min(doc_lanes)
        skipped = jnp.sum((doc_row[logical] < lowest).astype(F32)).astype(jnp.int32)
        needed = window - skipped // rows
        for chunks in range(1, window + 1):

            @pl.when(needed == chunks)
            def _():
                for head in range(KEY_VALUE_HEADS):
                    unit(block, logical, head, chunks, doc_lanes)

        return carry

    lax.fori_loop(0, NBLK, row_block, 0)

    def give(slot, k, meta_ref, home_out, away_out):
        base = pl.multiple_of(slot * rows, rows)
        flags = meta_ref[2 * rows :, :].astype(F32)
        for block in range(NBLK):
            at = pl.ds(base + block * per_block, per_block)
            for head in range(KEY_VALUE_HEADS):
                side = slice(head * HEAD_SIZE, (head + 1) * HEAD_SIZE)
                mask = jnp.broadcast_to(flags[block : block + 1, side], (per_block, HEAD_SIZE)) > 0.5
                for which, total, gain in ((0, key_total, scale), (1, value_total, 1.0)):
                    part = slice(
                        which * rows + block * per_block, which * rows + (block + 1) * per_block
                    )
                    first = total[0, head, at, :] * gain
                    second = total[1, head, at, :] * gain
                    home_out[k, part, side] = jnp.where(mask, second, first).astype(BF16)
                    away_out[k, part, side] = jnp.where(mask, first, second).astype(BF16)

    for k in range(count):
        slot = window - 1 - 2 * k
        side_slot = slot + 1 - 2 * core
        give(slot, k, blocks[k], home_ref, away_ref)
        inside = (side_slot >= 0) & (side_slot < window)

        @pl.when(inside)
        def _(k=k, side_slot=side_slot):
            give(side_slot, k, blocks[2 * count + k], home_side_ref, away_side_ref)

        @pl.when(jnp.logical_not(inside))
        def _(k=k):
            home_side_ref[k] = jnp.zeros_like(home_side_ref[k])
            away_side_ref[k] = jnp.zeros_like(away_side_ref[k])


def local(queries, key_rows, value_rows, out_grad, documents, swapped):
    ranks = lax.axis_size("ctx")
    hops = ranks // 4
    count = hops + 1
    window = 2 * hops + 1
    rows, width = key_rows.shape[1:]
    vmem = pl.BlockSpec(memory_space=pltpu.VMEM)
    smem = pl.BlockSpec(memory_space=pltpu.SMEM)
    heads = KEY_VALUE_HEADS
    keys = window * rows
    swap_flags = swapped[0, 0]

    up = [(i, i + 2) for i in range(ranks - 2)]
    down = [(i + 2, i) for i in range(ranks - 2)]
    side = [(i, i ^ 1) for i in range(ranks)]

    def to_partner(block):
        return lax.ppermute(block, "half", [(0, 1), (1, 0)])

    def to_side(block):
        return lax.ppermute(block, "ctx", side)

    payload = pl.pallas_call(
        payload_kernel,
        out_shape=jax.ShapeDtypeStruct((2 * rows + META, width), BF16),
        in_specs=[smem, vmem, vmem, vmem],
        out_specs=vmem,
    )(swap_flags, key_rows[0], value_rows[0], documents)
    home = [payload]
    for _ in range(hops):
        home.append(lax.ppermute(home[-1], "ctx", up))
    away = [to_partner(block) for block in home]
    home_side = [to_side(block) for block in home]
    away_side = [to_side(block) for block in away]
    chunk = jax.ShapeDtypeStruct((count, 2 * rows, width), BF16)
    index = lax.axis_index("ctx")
    place = jnp.stack([lax.rem(index, 2), index // 2]).astype(jnp.int32)
    out, query_grad, home_sum, home_sum_side, away_sum, away_sum_side = pl.pallas_call(
        functools.partial(attention_kernel, hops),
        out_shape=[
            jax.ShapeDtypeStruct(queries.shape[1:], BF16),
            jax.ShapeDtypeStruct(queries.shape[1:], BF16),
            chunk,
            chunk,
            chunk,
            chunk,
        ],
        in_specs=[smem, smem] + [vmem] * (2 + 4 * count),
        out_specs=[vmem] * 6,
        scratch_shapes=[
            pltpu.VMEM((2, heads, keys, HEAD_SIZE), BF16),
            pltpu.VMEM((2, heads, keys, HEAD_SIZE), BF16),
            pltpu.VMEM((2, heads, HEAD_SIZE, keys), BF16),
            pltpu.VMEM((2, heads, HEAD_SIZE, keys), BF16),
            pltpu.VMEM((2, keys, rows), F32),
            pltpu.VMEM((2, 16, rows), F32),
            pltpu.VMEM((2, 8, rows), F32),
            pltpu.VMEM((2, heads, keys, HEAD_SIZE), F32),
            pltpu.VMEM((2, heads, keys, HEAD_SIZE), F32),
        ],
        compiler_params=pltpu.CompilerParams(vmem_limit_bytes=40 * 1024 * 1024),
        cost_estimate=pl.CostEstimate(
            flops=12 * rows * keys * 2048,
            bytes_accessed=8 * 1024 * 1024,
            transcendentals=rows * keys * 16,
        ),
    )(place, swap_flags, queries[0], out_grad[0], *home, *away, *home_side, *away_side)

    away_got = to_side(away_sum_side)
    home_got = to_side(home_sum_side)
    added = [
        (away_sum[k].astype(F32) + away_got[k].astype(F32)).astype(BF16) for k in range(count)
    ]
    crossed = [None] * count
    for k in reversed(range(count)):
        crossed[k] = to_partner(added[k])
    moving = None
    for k in reversed(range(count)):
        total = home_sum[k].astype(F32) + home_got[k].astype(F32) + crossed[k].astype(F32)
        if moving is not None:
            total = total + moving.astype(F32)
        moving = total.astype(BF16)
        if k:
            moving = lax.ppermute(moving, "ctx", down)
    return (out[None], query_grad[None], moving[None, :rows], moving[None, rows:])


def solution(mesh):
    groups, ranks = mesh.devices.shape
    wide = Mesh(mesh.devices.reshape(2, groups // 2, ranks), ("half", "pair", "ctx"))
    spec3 = P(("half", "pair"), "ctx", None)
    in_specs = (spec3, spec3, spec3, spec3, P(("half", "pair"), "ctx"), spec3)
    return jax.shard_map(
        local, mesh=wide, in_specs=in_specs, out_specs=(spec3,) * 4, check_vma=False
    )
```

```python
import functools
import math

import jax
import jax.numpy as jnp
from jax import lax
from jax.experimental import pallas as pl
from jax.experimental.pallas import tpu as pltpu
from jax.sharding import Mesh
from jax.sharding import PartitionSpec as P

HEAD_SIZE = 128
QUERY_PER_KEY = 8
NBLK = 4
META = 16
DOC_ROW = NBLK
DOC_VALUES = 16
GROUPED = 2
HALF = QUERY_PER_KEY * HEAD_SIZE
NEG = -1e30
F32, BF16, I32 = jnp.float32, jnp.bfloat16, jnp.int32
NT = (((1,), (1,)), ((), ()))
VMEM = pl.BlockSpec(memory_space=pltpu.VMEM)
SMEM = pl.BlockSpec(memory_space=pltpu.SMEM)
HBM = pl.BlockSpec(memory_space=pltpu.HBM)


def core_index():
    return lax.rem(lax.axis_index("ctx"), 2)


def payload_kernel(
    swap_ref, key_ref, value_ref, docs_ref, query_ref, grad_ref, own_ref, side_ref, rows_ref, sems
):
    rows = key_ref.shape[0]
    core = core_index()
    away = pl.ds(pl.multiple_of((1 - core) * HALF, HALF), HALF)
    copies = [
        pltpu.make_async_copy(query_ref.at[:, away], rows_ref.at[pl.ds(0, rows), :], sems.at[0]),
        pltpu.make_async_copy(grad_ref.at[:, away], rows_ref.at[pl.ds(rows, rows), :], sems.at[1]),
    ]
    for copy in copies:
        copy.start()
    docs = jnp.broadcast_to(docs_ref[...].astype(F32), (META, rows))
    place = lax.broadcasted_iota(I32, docs.shape, 0)
    meta = jnp.where(place == DOC_ROW, docs, 0.0)
    for block in range(NBLK):
        meta = jnp.where(place == block, swap_ref[block].astype(F32), meta)
    meta = meta.astype(BF16)
    for ref, head in ((own_ref, core), (side_ref, 1 - core)):
        lane = pl.ds(pl.multiple_of(head * HEAD_SIZE, HEAD_SIZE), HEAD_SIZE)
        ref[:rows, :] = key_ref[:, lane]
        ref[rows : 2 * rows, :] = value_ref[:, lane]
        ref[2 * rows :, :] = meta
    for copy in copies:
        copy.wait()


def join_kernel(first_ref, second_ref, both_ref):
    size = first_ref.shape[0]
    both_ref[:size, :] = first_ref[...]
    both_ref[size:, :] = second_ref[...]


def finish_kernel(own_ref, side_ref, out_ref, query_grad_ref, sems):
    rows = out_ref.shape[0]
    core = core_index()
    copies = []
    for at, (source, head) in enumerate(((own_ref, core), (side_ref, 1 - core))):
        lanes = pl.ds(pl.multiple_of(head * HALF, HALF), HALF)
        for part, target in enumerate((out_ref, query_grad_ref)):
            copies.append(
                pltpu.make_async_copy(
                    source.at[pl.ds(part * rows, rows), :], target.at[:, lanes], sems.at[2 * at + part]
                )
            )
    for copy in copies:
        copy.start()
    for copy in copies:
        copy.wait()


def attention_kernel(hops, query_ref, grad_ref, side_rows_ref, *refs):
    count = hops + 1
    slots = 2 * count
    window = slots - 1
    homes, aways = refs[:count], refs[count : 2 * count]
    own_out_ref, side_out_ref = refs[2 * count : 2 * count + 2]
    home_outs = refs[2 * count + 2 : 3 * count + 2]
    away_outs = refs[3 * count + 2 : 4 * count + 2]
    (
        query_all,
        grad_all,
        out_all,
        key_log,
        value_log,
        key_turned,
        value_turned,
        doc_window,
        starts,
        key_total,
        value_total,
        logical_of,
        needed_of,
        sems,
    ) = refs[4 * count + 2 :]
    rows = query_ref.shape[0]
    per_block = rows // NBLK
    lanes = QUERY_PER_KEY * per_block
    size = 2 * rows + META
    core = core_index()
    chip = lax.axis_index("ctx") // 2
    parity = (core, 1 - core)
    scale = 1.0 / math.sqrt(HEAD_SIZE)
    factor = scale * math.log2(math.e)

    mine = pl.ds(pl.multiple_of(core * HALF, HALF), HALF)
    copies = [
        pltpu.make_async_copy(query_ref.at[:, mine], query_all.at[0], sems.at[0]),
        pltpu.make_async_copy(grad_ref.at[:, mine], grad_all.at[0], sems.at[1]),
        pltpu.make_async_copy(side_rows_ref.at[pl.ds(0, rows), :], query_all.at[1], sems.at[2]),
        pltpu.make_async_copy(side_rows_ref.at[pl.ds(rows, rows), :], grad_all.at[1], sems.at[3]),
    ]
    for copy in copies:
        copy.start()

    key_total[...] = jnp.zeros_like(key_total)
    value_total[...] = jnp.zeros_like(value_total)
    doc_window[...] = jnp.full_like(doc_window, 1e4)

    def meta_of(ref, who):
        return ref[who * size + 2 * rows : (who + 1) * size, :].astype(F32)

    for k in range(count):
        for who in range(2):
            slot = 2 * (hops - k) + parity[who]
            base = pl.multiple_of(slot * rows, rows)
            for logical, ref in ((0, homes[k]), (1, aways[k])):
                docs = meta_of(ref, who)[DOC_ROW : DOC_ROW + 1, :]
                doc_window[logical, pl.ds(slot, 1), :] = jnp.where(chip >= k, docs, -1.0)
            flags = meta_of(homes[k], who)
            for block in range(NBLK):
                mask = (
                    jnp.broadcast_to(flags[block : block + 1, :], (per_block, HEAD_SIZE)).astype(BF16)
                    > 0.5
                )
                at = pl.ds(base + block * per_block, per_block)
                for which, log in ((0, key_log), (1, value_log)):
                    first = who * size + which * rows + block * per_block
                    own = homes[k][first : first + per_block, :]
                    other = aways[k][first : first + per_block, :]
                    log[0, at, :] = jnp.where(mask, other, own)
                    log[1, at, :] = jnp.where(mask, own, other)

    for logical in range(2):
        key_turned[logical] = key_log[logical].T
        value_turned[logical] = value_log[logical].T

    values_down = lax.broadcasted_iota(I32, (DOC_VALUES, rows), 0).astype(F32)
    group = lax.broadcasted_iota(I32, (8, rows), 1) // per_block
    meta_rows = [meta_of(homes[0], who) for who in range(2)]
    for logical in range(2):
        lower = jnp.zeros((DOC_VALUES, rows), F32)
        for slot in range(slots):
            docs = jnp.broadcast_to(doc_window[logical, slot : slot + 1, :], lower.shape)
            lower = lower + jnp.where(docs < values_down, 1.0, 0.0)
        lower = jnp.broadcast_to(jnp.sum(lower, axis=1, keepdims=True), lower.shape)
        for who in range(2):
            docs = meta_of((homes, aways)[logical][0], who)[DOC_ROW : DOC_ROW + 1, :]
            docs = jnp.broadcast_to(docs, (8, rows))
            turns = [docs] + [pltpu.roll(docs, t * per_block, 1) for t in range(1, NBLK)]
            for block in range(NBLK):
                tiled = turns[0]
                for t in range(1, NBLK):
                    tiled = jnp.where(group == (block + t) % NBLK, turns[t], tiled)
                tiled = jnp.broadcast_to(tiled[:1], lower.shape)
                start = jnp.sum(jnp.where(tiled == values_down, lower, 0.0), axis=0, keepdims=True)
                starts[logical, who * NBLK + block : who * NBLK + block + 1, :] = start.astype(I32)
    for unit_index in range(2 * NBLK):
        who, block = unit_index // NBLK, unit_index % NBLK
        flag = jnp.max(meta_rows[who][block : block + 1, :]).astype(I32)
        logical_of[unit_index] = flag
        first = jnp.min(starts[flag, unit_index : unit_index + 1, :].astype(F32)).astype(I32)
        needed_of[unit_index] = window + parity[who] - first // rows
    for copy in copies:
        copy.wait()

    def unit(unit_index, chunks):
        who, block = unit_index // NBLK, lax.rem(unit_index, NBLK)
        logical = logical_of[unit_index]
        row_parity = jnp.where(who == 0, core, 1 - core)
        first_slot = window + row_parity - chunks
        first = pl.multiple_of(first_slot * rows, rows)
        span = pl.ds(first, chunks * rows)
        at = pl.ds(pl.multiple_of(block * per_block, per_block), per_block)
        columns = [slice(h * HEAD_SIZE, (h + 1) * HEAD_SIZE) for h in range(QUERY_PER_KEY)]
        query = jnp.concatenate([query_all[who, at, column] for column in columns], axis=0)
        grad = jnp.concatenate([grad_all[who, at, column] for column in columns], axis=0)
        scores = lax.dot_general(key_log[logical, span, :], query, NT, preferred_element_type=F32)
        shape = (chunks * rows, HEAD_SIZE)
        key_place = lax.broadcasted_iota(I32, shape, 0)
        row_first = starts[logical, pl.ds(unit_index, 1), :] - first
        row_last = (
            (chunks - 1) * rows
            + block * per_block
            + lax.rem(lax.broadcasted_iota(I32, (1, HEAD_SIZE), 1), per_block)
        )
        allowed = (key_place >= row_first) & (key_place <= row_last)
        scores = jnp.concatenate(
            [
                jnp.where(allowed, scores[:, lane : lane + HEAD_SIZE], NEG)
                for lane in range(0, lanes, HEAD_SIZE)
            ],
            axis=1,
        )
        peak = jnp.max(scores, axis=0, keepdims=True)
        powers = jnp.exp2((scores - peak) * factor)
        inverse = 1.0 / jnp.sum(powers, axis=0, keepdims=True)
        probs = powers * inverse
        weights = probs.astype(BF16)
        out_turned = jnp.dot(
            value_turned[logical, :, span], weights, preferred_element_type=F32
        ).astype(BF16)
        delta = jnp.sum(grad.T.astype(F32) * out_turned.astype(F32), axis=0, keepdims=True)
        prob_grad = lax.dot_general(
            value_log[logical, span, :], grad, NT, preferred_element_type=F32
        )
        score_grad = (probs * (prob_grad - delta)).astype(BF16)
        query_grad_turned = jnp.dot(
            key_turned[logical, :, span], score_grad, preferred_element_type=F32
        )
        key_add = jnp.dot(score_grad, query, preferred_element_type=F32)
        value_add = jnp.dot(weights, grad, preferred_element_type=F32)
        out = out_turned.T
        query_grad = (query_grad_turned * scale).astype(BF16).T
        return who, at, logical, span, out, query_grad, key_add, value_add

    def step(pair, carry):
        members = [pair * GROUPED + m for m in range(GROUPED)]
        needed = needed_of[members[0]]
        for member in members[1:]:
            needed = jnp.maximum(needed, needed_of[member])
        for chunks in range(1, window + 1):

            @pl.when(needed == chunks)
            def _(chunks=chunks):
                results = [unit(member, chunks) for member in members]
                for who, at, logical, span, out, query_grad, key_add, value_add in results:
                    key_total[logical, span, :] += key_add
                    value_total[logical, span, :] += value_add
                    for h in range(QUERY_PER_KEY):
                        column = slice(h * HEAD_SIZE, (h + 1) * HEAD_SIZE)
                        part = slice(h * per_block, (h + 1) * per_block)
                        out_all[who, 0, at, column] = out[part, :]
                        out_all[who, 1, at, column] = query_grad[part, :]

        return carry

    lax.fori_loop(0, 2 * NBLK // GROUPED, step, 0)
    copies = [
        pltpu.make_async_copy(
            out_all.at[who, which], target.at[pl.ds(which * rows, rows), :], sems.at[2 * who + which]
        )
        for who, target in enumerate((own_out_ref, side_out_ref))
        for which in range(2)
    ]
    for copy in copies:
        copy.start()

    for k in range(count):
        for who in range(2):
            base = pl.multiple_of((2 * (hops - k) + parity[who]) * rows, rows)
            flags = meta_of(homes[k], who)
            for block in range(NBLK):
                at = pl.ds(base + block * per_block, per_block)
                mask = jnp.broadcast_to(flags[block : block + 1, :], (per_block, HEAD_SIZE)) > 0.5
                for which, total, gain in ((0, key_total, scale), (1, value_total, 1.0)):
                    part = (2 * who + which) * rows + block * per_block
                    first = total[0, at, :] * gain
                    second = total[1, at, :] * gain
                    home_outs[k][part : part + per_block, :] = jnp.where(mask, second, first).astype(BF16)
                    away_outs[k][part : part + per_block, :] = jnp.where(mask, first, second).astype(BF16)
    for copy in copies:
        copy.wait()


def local(queries, key_rows, value_rows, out_grad, documents, swapped):
    ranks = lax.axis_size("ctx")
    hops = ranks // 4
    count = hops + 1
    slots = 2 * count
    rows, width = key_rows.shape[1:]
    keys = slots * rows
    size = 2 * rows + META
    queries, out_grad = queries[0], out_grad[0]

    def up(block, k):
        return lax.ppermute(block, "ctx", [(i, i + 2 * k) for i in range(ranks - 2 * k)])

    def down(block, k):
        return lax.ppermute(block, "ctx", [(i + 2 * k, i) for i in range(ranks - 2 * k)])

    def to_partner(block):
        return lax.ppermute(block, "half", [(0, 1), (1, 0)])

    def to_side(block):
        return lax.ppermute(block, "ctx", [(i, i ^ 1) for i in range(ranks)])

    payload, payload_side, rows_side = pl.pallas_call(
        payload_kernel,
        out_shape=[
            jax.ShapeDtypeStruct((size, HEAD_SIZE), BF16),
            jax.ShapeDtypeStruct((size, HEAD_SIZE), BF16),
            jax.ShapeDtypeStruct((2 * rows, HALF), BF16),
        ],
        in_specs=[SMEM, VMEM, VMEM, VMEM, HBM, HBM],
        out_specs=[VMEM, VMEM, HBM],
        scratch_shapes=[pltpu.SemaphoreType.DMA((2,))],
    )(swapped[0, 0], key_rows[0], value_rows[0], documents, queries, out_grad)
    from_side = to_side(payload_side)
    rows_got = to_side(rows_side)
    both = pl.pallas_call(
        join_kernel,
        out_shape=jax.ShapeDtypeStruct((2 * size, HEAD_SIZE), BF16),
        in_specs=[VMEM, VMEM],
        out_specs=VMEM,
    )(payload, from_side)
    home = [both] + [up(both, k) for k in range(1, count)]
    away = [to_partner(block) for block in home]
    chunk = jax.ShapeDtypeStruct((4 * rows, HEAD_SIZE), BF16)
    outs = pl.pallas_call(
        functools.partial(attention_kernel, hops),
        out_shape=[jax.ShapeDtypeStruct((2 * rows, HALF), BF16)] * 2 + [chunk] * (2 * count),
        in_specs=[HBM, HBM, pl.BlockSpec(memory_space=pl.ANY)] + [VMEM] * (2 * count),
        out_specs=[HBM] * 2 + [VMEM] * (2 * count),
        scratch_shapes=[
            pltpu.VMEM((2, rows, HALF), BF16),
            pltpu.VMEM((2, rows, HALF), BF16),
            pltpu.VMEM((2, 2, rows, HALF), BF16),
            pltpu.VMEM((2, keys, HEAD_SIZE), BF16),
            pltpu.VMEM((2, keys, HEAD_SIZE), BF16),
            pltpu.VMEM((2, HEAD_SIZE, keys), BF16),
            pltpu.VMEM((2, HEAD_SIZE, keys), BF16),
            pltpu.VMEM((2, 16, rows), F32),
            pltpu.VMEM((2, 8, rows), I32),
            pltpu.VMEM((2, keys, HEAD_SIZE), F32),
            pltpu.VMEM((2, keys, HEAD_SIZE), F32),
            pltpu.SMEM((2 * NBLK,), I32),
            pltpu.SMEM((2 * NBLK,), I32),
            pltpu.SemaphoreType.DMA((4,)),
        ],
        compiler_params=pltpu.CompilerParams(vmem_limit_bytes=40 * 1024 * 1024),
        cost_estimate=pl.CostEstimate(
            flops=12 * rows * keys * 2048,
            bytes_accessed=4 * 1024 * 1024,
            transcendentals=rows * keys * 16,
        ),
    )(queries, out_grad, rows_got, *home, *away)
    own_out, side_out = outs[:2]
    home_sum, away_sum = outs[2 : 2 + count], outs[2 + count :]

    crossed = [None] * count
    for k in reversed(range(count)):
        crossed[k] = to_partner(away_sum[k])
    parts = []
    for k in reversed(range(count)):
        part = home_sum[k].astype(F32) + crossed[k].astype(F32)
        parts.append(down(part.astype(BF16), k) if k else part)
    out_got = to_side(side_out)
    out, query_grad = pl.pallas_call(
        finish_kernel,
        out_shape=[jax.ShapeDtypeStruct(queries.shape, BF16)] * 2,
        in_specs=[pl.BlockSpec(memory_space=pl.ANY)] * 2,
        out_specs=[HBM] * 2,
        scratch_shapes=[pltpu.SemaphoreType.DMA((4,))],
    )(own_out, out_got)
    parts[0], out, query_grad = lax.optimization_barrier((parts[0], out, query_grad))
    total = sum(part.astype(F32) for part in parts).astype(BF16)
    grads_got = to_side(total[2 * rows :])
    grads = total[: 2 * rows]
    first = core_index() == 0
    grads = jnp.concatenate(
        [jnp.where(first, grads, grads_got), jnp.where(first, grads_got, grads)], axis=1
    )
    return (out[None], query_grad[None], grads[None, :rows], grads[None, rows:])


def solution(mesh):
    groups, ranks = mesh.devices.shape
    wide = Mesh(mesh.devices.reshape(2, groups // 2, ranks), ("half", "pair", "ctx"))
    spec3 = P(("half", "pair"), "ctx", None)
    in_specs = (spec3, spec3, spec3, spec3, P(("half", "pair"), "ctx"), spec3)
    return jax.shard_map(
        local, mesh=wide, in_specs=in_specs, out_specs=(spec3,) * 4, check_vma=False
    )
```

```python
import functools
import math

import jax
import jax.numpy as jnp
from jax import lax
from jax.experimental import pallas as pl
from jax.experimental.pallas import tpu as pltpu
from jax.sharding import Mesh
from jax.sharding import PartitionSpec as P

HEAD_SIZE = 128
QUERY_PER_KEY = 8
NBLK = 4
META = 16
DOC_ROW = NBLK
DOC_VALUES = 16
GROUPED = 4
HALF = QUERY_PER_KEY * HEAD_SIZE
NEG = -1e30
F32, BF16, I32 = jnp.float32, jnp.bfloat16, jnp.int32
NT = (((1,), (1,)), ((), ()))
VMEM = pl.BlockSpec(memory_space=pltpu.VMEM)
SMEM = pl.BlockSpec(memory_space=pltpu.SMEM)
HBM = pl.BlockSpec(memory_space=pltpu.HBM)


def core_index():
    return lax.rem(lax.axis_index("ctx"), 2)


def payload_kernel(swap_ref, key_ref, value_ref, docs_ref, own_ref, side_ref):
    rows = key_ref.shape[0]
    core = core_index()
    docs = jnp.broadcast_to(docs_ref[...].astype(F32), (META, rows))
    place = lax.broadcasted_iota(I32, docs.shape, 0)
    meta = jnp.where(place == DOC_ROW, docs, 0.0)
    for block in range(NBLK):
        meta = jnp.where(place == block, swap_ref[block].astype(F32), meta)
    meta = meta.astype(BF16)
    for ref, head in ((own_ref, core), (side_ref, 1 - core)):
        lane = pl.ds(pl.multiple_of(head * HEAD_SIZE, HEAD_SIZE), HEAD_SIZE)
        ref[:rows, :] = key_ref[:, lane]
        ref[rows : 2 * rows, :] = value_ref[:, lane]
        ref[2 * rows :, :] = meta


def rows_kernel(query_ref, grad_ref, rows_ref, sems):
    rows = query_ref.shape[0]
    away = pl.ds(pl.multiple_of((1 - core_index()) * HALF, HALF), HALF)
    copies = [
        pltpu.make_async_copy(
            source.at[:, away], rows_ref.at[pl.ds(part * rows, rows), :], sems.at[part]
        )
        for part, source in enumerate((query_ref, grad_ref))
    ]
    for copy in copies:
        copy.start()
    for copy in copies:
        copy.wait()


def finish_kernel(own_ref, side_ref, out_ref, query_grad_ref):
    rows = out_ref.shape[0]
    core = core_index()
    for source, head in ((own_ref, core), (side_ref, 1 - core)):
        lanes = pl.ds(pl.multiple_of(head * HALF, HALF), HALF)
        out_ref[:, lanes] = source[:rows, :]
        query_grad_ref[:, lanes] = source[rows:, :]


def attention_kernel(hops, query_ref, grad_ref, side_rows_ref, *refs):
    count = hops + 1
    slots = 2 * count
    window = slots - 1
    homes, aways = refs[:count], refs[count : 2 * count]
    own_out_ref, side_out_ref = refs[2 * count : 2 * count + 2]
    home_outs = refs[2 * count + 2 : 3 * count + 2]
    away_outs = refs[3 * count + 2 : 4 * count + 2]
    (
        query_all,
        grad_all,
        out_all,
        key_log,
        value_log,
        key_turned,
        value_turned,
        doc_window,
        starts,
        key_total,
        value_total,
        logical_of,
        needed_of,
        sems,
    ) = refs[4 * count + 2 :]
    rows = query_ref.shape[0]
    per_block = rows // NBLK
    lanes = QUERY_PER_KEY * per_block
    size = 2 * rows + META
    core = core_index()
    chip = lax.axis_index("ctx") // 2
    parity = (core, 1 - core)
    scale = 1.0 / math.sqrt(HEAD_SIZE)
    factor = scale * math.log2(math.e)

    mine = pl.ds(pl.multiple_of(core * HALF, HALF), HALF)
    copies = [
        pltpu.make_async_copy(query_ref.at[:, mine], query_all.at[0], sems.at[0]),
        pltpu.make_async_copy(grad_ref.at[:, mine], grad_all.at[0], sems.at[1]),
        pltpu.make_async_copy(side_rows_ref.at[pl.ds(0, rows), :], query_all.at[1], sems.at[2]),
        pltpu.make_async_copy(side_rows_ref.at[pl.ds(rows, rows), :], grad_all.at[1], sems.at[3]),
    ]
    for copy in copies:
        copy.start()

    key_total[...] = jnp.zeros_like(key_total)
    value_total[...] = jnp.zeros_like(value_total)
    doc_window[...] = jnp.full_like(doc_window, 1e4)

    def meta_of(ref, who):
        return ref[who * size + 2 * rows : (who + 1) * size, :].astype(F32)

    for k in range(count):
        for who in range(2):
            slot = 2 * (hops - k) + parity[who]
            base = pl.multiple_of(slot * rows, rows)
            for logical, ref in ((0, homes[k]), (1, aways[k])):
                docs = meta_of(ref, who)[DOC_ROW : DOC_ROW + 1, :]
                doc_window[logical, pl.ds(slot, 1), :] = jnp.where(chip >= k, docs, -1.0)
            flags = meta_of(homes[k], who)
            for block in range(NBLK):
                mask = (
                    jnp.broadcast_to(flags[block : block + 1, :], (per_block, HEAD_SIZE)).astype(BF16)
                    > 0.5
                )
                at = pl.ds(base + block * per_block, per_block)
                for which, log in ((0, key_log), (1, value_log)):
                    first = who * size + which * rows + block * per_block
                    own = homes[k][first : first + per_block, :]
                    other = aways[k][first : first + per_block, :]
                    log[0, at, :] = jnp.where(mask, other, own)
                    log[1, at, :] = jnp.where(mask, own, other)

    for logical in range(2):
        key_turned[logical] = key_log[logical].T
        value_turned[logical] = value_log[logical].T

    values_down = lax.broadcasted_iota(I32, (DOC_VALUES, rows), 0).astype(F32)
    group = lax.broadcasted_iota(I32, (8, rows), 1) // per_block
    meta_rows = [meta_of(homes[0], who) for who in range(2)]
    for logical in range(2):
        lower = jnp.zeros((DOC_VALUES, rows), F32)
        for slot in range(slots):
            docs = jnp.broadcast_to(doc_window[logical, slot : slot + 1, :], lower.shape)
            lower = lower + jnp.where(docs < values_down, 1.0, 0.0)
        lower = jnp.broadcast_to(jnp.sum(lower, axis=1, keepdims=True), lower.shape)
        for who in range(2):
            docs = meta_of((homes, aways)[logical][0], who)[DOC_ROW : DOC_ROW + 1, :]
            docs = jnp.broadcast_to(docs, (8, rows))
            turns = [docs] + [pltpu.roll(docs, t * per_block, 1) for t in range(1, NBLK)]
            for block in range(NBLK):
                tiled = turns[0]
                for t in range(1, NBLK):
                    tiled = jnp.where(group == (block + t) % NBLK, turns[t], tiled)
                tiled = jnp.broadcast_to(tiled[:1], lower.shape)
                start = jnp.sum(jnp.where(tiled == values_down, lower, 0.0), axis=0, keepdims=True)
                starts[logical, who * NBLK + block : who * NBLK + block + 1, :] = start.astype(I32)
    for unit_index in range(2 * NBLK):
        who, block = unit_index // NBLK, unit_index % NBLK
        flag = jnp.max(meta_rows[who][block : block + 1, :]).astype(I32)
        logical_of[unit_index] = flag
        first = jnp.min(starts[flag, unit_index : unit_index + 1, :].astype(F32)).astype(I32)
        needed_of[unit_index] = window + parity[who] - first // rows
    for copy in copies:
        copy.wait()

    def unit(unit_index, chunks):
        who, block = unit_index // NBLK, lax.rem(unit_index, NBLK)
        logical = logical_of[unit_index]
        row_parity = jnp.where(who == 0, core, 1 - core)
        first_slot = window + row_parity - chunks
        first = pl.multiple_of(first_slot * rows, rows)
        span = pl.ds(first, chunks * rows)
        at = pl.ds(pl.multiple_of(block * per_block, per_block), per_block)
        columns = [slice(h * HEAD_SIZE, (h + 1) * HEAD_SIZE) for h in range(QUERY_PER_KEY)]
        query = jnp.concatenate([query_all[who, at, column] for column in columns], axis=0)
        grad = jnp.concatenate([grad_all[who, at, column] for column in columns], axis=0)
        scores = lax.dot_general(key_log[logical, span, :], query, NT, preferred_element_type=F32)
        shape = (chunks * rows, HEAD_SIZE)
        key_place = lax.broadcasted_iota(I32, shape, 0)
        row_first = starts[logical, pl.ds(unit_index, 1), :] - first
        row_last = (
            (chunks - 1) * rows
            + block * per_block
            + lax.rem(lax.broadcasted_iota(I32, (1, HEAD_SIZE), 1), per_block)
        )
        allowed = (key_place >= row_first) & (key_place <= row_last)
        scores = jnp.concatenate(
            [
                jnp.where(allowed, scores[:, lane : lane + HEAD_SIZE], NEG)
                for lane in range(0, lanes, HEAD_SIZE)
            ],
            axis=1,
        )
        peak = jnp.max(scores, axis=0, keepdims=True)
        powers = jnp.exp2((scores - peak) * factor)
        inverse = 1.0 / jnp.sum(powers, axis=0, keepdims=True)
        probs = powers * inverse
        weights = probs.astype(BF16)
        out_turned = jnp.dot(
            value_turned[logical, :, span], weights, preferred_element_type=F32
        ).astype(BF16)
        delta = jnp.sum(grad.T.astype(F32) * out_turned.astype(F32), axis=0, keepdims=True)
        prob_grad = lax.dot_general(
            value_log[logical, span, :], grad, NT, preferred_element_type=F32
        )
        score_grad = (probs * (prob_grad - delta)).astype(BF16)
        query_grad_turned = jnp.dot(
            key_turned[logical, :, span], score_grad, preferred_element_type=F32
        )
        key_add = jnp.dot(score_grad, query, preferred_element_type=F32)
        value_add = jnp.dot(weights, grad, preferred_element_type=F32)
        out = out_turned.T
        query_grad = (query_grad_turned * scale).astype(BF16).T
        return who, at, logical, span, out, query_grad, key_add, value_add

    def step(pair, carry):
        members = [pair * GROUPED + m for m in range(GROUPED)]
        needed = needed_of[members[0]]
        for member in members[1:]:
            needed = jnp.maximum(needed, needed_of[member])
        for chunks in range(1, window + 1):

            @pl.when(needed == chunks)
            def _(chunks=chunks):
                results = [unit(member, chunks) for member in members]
                for who, at, logical, span, out, query_grad, key_add, value_add in results:
                    key_total[logical, span, :] += key_add
                    value_total[logical, span, :] += value_add
                    for h in range(QUERY_PER_KEY):
                        column = slice(h * HEAD_SIZE, (h + 1) * HEAD_SIZE)
                        part = slice(h * per_block, (h + 1) * per_block)
                        out_all[who, 0, at, column] = out[part, :]
                        out_all[who, 1, at, column] = query_grad[part, :]

        return carry

    lax.fori_loop(0, 2 * NBLK // GROUPED, step, 0)
    copies = [
        pltpu.make_async_copy(
            out_all.at[who, which], target.at[pl.ds(which * rows, rows), :], sems.at[2 * who + which]
        )
        for who, target in enumerate((own_out_ref, side_out_ref))
        for which in range(2)
    ]
    for copy in copies:
        copy.start()

    for k in range(count):
        for who in range(2):
            base = pl.multiple_of((2 * (hops - k) + parity[who]) * rows, rows)
            flags = meta_of(homes[k], who)
            for block in range(NBLK):
                at = pl.ds(base + block * per_block, per_block)
                mask = jnp.broadcast_to(flags[block : block + 1, :], (per_block, HEAD_SIZE)) > 0.5
                for which, total, gain in ((0, key_total, scale), (1, value_total, 1.0)):
                    part = (2 * who + which) * rows + block * per_block
                    first = total[0, at, :] * gain
                    second = total[1, at, :] * gain
                    home_outs[k][part : part + per_block, :] = jnp.where(mask, second, first).astype(BF16)
                    away_outs[k][part : part + per_block, :] = jnp.where(mask, first, second).astype(BF16)
    for copy in copies:
        copy.wait()


def local(queries, key_rows, value_rows, out_grad, documents, swapped):
    ranks = lax.axis_size("ctx")
    hops = ranks // 4
    count = hops + 1
    slots = 2 * count
    rows, width = key_rows.shape[1:]
    keys = slots * rows
    size = 2 * rows + META
    queries, out_grad = queries[0], out_grad[0]

    def up(block, k):
        return lax.ppermute(block, "ctx", [(i, i + 2 * k) for i in range(ranks - 2 * k)])

    def down(block, k):
        return lax.ppermute(block, "ctx", [(i + 2 * k, i) for i in range(ranks - 2 * k)])

    def to_partner(block):
        return lax.ppermute(block, "half", [(0, 1), (1, 0)])

    def to_side(block):
        return lax.ppermute(block, "ctx", [(i, i ^ 1) for i in range(ranks)])

    payload, payload_side = pl.pallas_call(
        payload_kernel,
        out_shape=[pltpu.VMEM((size, HEAD_SIZE), BF16)] * 2,
        in_specs=[SMEM, VMEM, VMEM, VMEM],
        out_specs=[VMEM, VMEM],
    )(swapped[0, 0], key_rows[0], value_rows[0], documents)
    from_side = to_side(payload_side)
    rows_side = pl.pallas_call(
        rows_kernel,
        out_shape=pltpu.VMEM((2 * rows, HALF), BF16),
        in_specs=[HBM, HBM],
        out_specs=VMEM,
        scratch_shapes=[pltpu.SemaphoreType.DMA((2,))],
    )(queries, out_grad)
    both = jnp.concatenate([payload, from_side], axis=0)
    both, rows_side = lax.optimization_barrier((both, rows_side))
    rows_got = to_side(rows_side)
    home = [both] + [up(both, k) for k in range(1, count)]
    away = [to_partner(block) for block in home]
    chunk = pltpu.VMEM((4 * rows, HEAD_SIZE), BF16)
    outs = pl.pallas_call(
        functools.partial(attention_kernel, hops),
        out_shape=[jax.ShapeDtypeStruct((2 * rows, HALF), BF16)] * 2 + [chunk] * (2 * count),
        in_specs=[HBM, HBM, pl.BlockSpec(memory_space=pl.ANY)] + [VMEM] * (2 * count),
        out_specs=[HBM] * 2 + [VMEM] * (2 * count),
        scratch_shapes=[
            pltpu.VMEM((2, rows, HALF), BF16),
            pltpu.VMEM((2, rows, HALF), BF16),
            pltpu.VMEM((2, 2, rows, HALF), BF16),
            pltpu.VMEM((2, keys, HEAD_SIZE), BF16),
            pltpu.VMEM((2, keys, HEAD_SIZE), BF16),
            pltpu.VMEM((2, HEAD_SIZE, keys), BF16),
            pltpu.VMEM((2, HEAD_SIZE, keys), BF16),
            pltpu.VMEM((2, 16, rows), F32),
            pltpu.VMEM((2, 8, rows), I32),
            pltpu.VMEM((2, keys, HEAD_SIZE), F32),
            pltpu.VMEM((2, keys, HEAD_SIZE), F32),
            pltpu.SMEM((2 * NBLK,), I32),
            pltpu.SMEM((2 * NBLK,), I32),
            pltpu.SemaphoreType.DMA((4,)),
        ],
        compiler_params=pltpu.CompilerParams(vmem_limit_bytes=40 * 1024 * 1024),
        cost_estimate=pl.CostEstimate(
            flops=12 * rows * keys * 2048,
            bytes_accessed=4 * 1024 * 1024,
            transcendentals=rows * keys * 16,
        ),
    )(queries, out_grad, rows_got, *home, *away)
    own_out, side_out = outs[:2]
    home_sum, away_sum = outs[2 : 2 + count], outs[2 + count :]

    crossed = [None] * count
    for k in reversed(range(count)):
        crossed[k] = to_partner(away_sum[k])
    parts = []
    for k in reversed(range(count)):
        part = home_sum[k].astype(F32) + crossed[k].astype(F32)
        if k:
            part = part.astype(BF16)
            if k == hops:
                part, side_out = lax.optimization_barrier((part, side_out))
            part = down(part, k)
        parts.append(part)
    out_got = to_side(side_out)
    out, query_grad = pl.pallas_call(
        finish_kernel,
        out_shape=[jax.ShapeDtypeStruct(queries.shape, BF16)] * 2,
        in_specs=[VMEM] * 2,
        out_specs=[VMEM] * 2,
    )(own_out, out_got)
    parts[0], out, query_grad = lax.optimization_barrier((parts[0], out, query_grad))
    total = sum(part.astype(F32) for part in parts).astype(BF16)
    grads_got = to_side(total[2 * rows :])
    grads = total[: 2 * rows]
    first = core_index() == 0
    grads = jnp.concatenate(
        [jnp.where(first, grads, grads_got), jnp.where(first, grads_got, grads)], axis=1
    )
    return (out[None], query_grad[None], grads[None, :rows], grads[None, rows:])


def solution(mesh):
    groups, ranks = mesh.devices.shape
    wide = Mesh(mesh.devices.reshape(2, groups // 2, ranks), ("half", "pair", "ctx"))
    spec3 = P(("half", "pair"), "ctx", None)
    in_specs = (spec3, spec3, spec3, spec3, P(("half", "pair"), "ctx"), spec3)
    return jax.shard_map(
        local, mesh=wide, in_specs=in_specs, out_specs=(spec3,) * 4, check_vma=False
    )
```

```python
import functools
import math

import jax
import jax.numpy as jnp
from jax import lax
from jax.experimental import pallas as pl
from jax.experimental.pallas import tpu as pltpu
from jax.sharding import Mesh
from jax.sharding import PartitionSpec as P

HEAD_SIZE = 128
QUERY_PER_KEY = 8
NBLK = 4
META = 16
DOC_ROW = NBLK
DOC_VALUES = 16
GROUPED = 4
HALF = QUERY_PER_KEY * HEAD_SIZE
NEG = -1e30
F32, BF16, I32 = jnp.float32, jnp.bfloat16, jnp.int32
NT = (((1,), (1,)), ((), ()))
VMEM = pl.BlockSpec(memory_space=pltpu.VMEM)
SMEM = pl.BlockSpec(memory_space=pltpu.SMEM)
HBM = pl.BlockSpec(memory_space=pltpu.HBM)


def core_index():
    return lax.rem(lax.axis_index("ctx"), 2)


def payload_kernel(swap_ref, key_ref, value_ref, docs_ref, own_ref, side_ref):
    rows = key_ref.shape[0]
    core = core_index()
    docs = jnp.broadcast_to(docs_ref[...].astype(F32), (META, rows))
    place = lax.broadcasted_iota(I32, docs.shape, 0)
    meta = jnp.where(place == DOC_ROW, docs, 0.0)
    for block in range(NBLK):
        meta = jnp.where(place == block, swap_ref[block].astype(F32), meta)
    meta = meta.astype(BF16)
    for ref, head in ((own_ref, core), (side_ref, 1 - core)):
        lane = pl.ds(pl.multiple_of(head * HEAD_SIZE, HEAD_SIZE), HEAD_SIZE)
        ref[:rows, :] = key_ref[:, lane]
        ref[rows : 2 * rows, :] = value_ref[:, lane]
        ref[2 * rows :, :] = meta


def rows_kernel(query_ref, grad_ref, rows_ref, sems):
    rows = query_ref.shape[0]
    away = pl.ds(pl.multiple_of((1 - core_index()) * HALF, HALF), HALF)
    copies = [
        pltpu.make_async_copy(
            source.at[:, away], rows_ref.at[pl.ds(part * rows, rows), :], sems.at[part]
        )
        for part, source in enumerate((query_ref, grad_ref))
    ]
    for copy in copies:
        copy.start()
    for copy in copies:
        copy.wait()


def finish_kernel(side_ref, out_held, query_grad_held, out_ref, query_grad_ref, sems):
    rows = out_ref.shape[0]
    away = pl.ds(pl.multiple_of((1 - core_index()) * HALF, HALF), HALF)
    copies = [
        pltpu.make_async_copy(
            side_ref.at[pl.ds(part * rows, rows), :], target.at[:, away], sems.at[part]
        )
        for part, target in enumerate((out_ref, query_grad_ref))
    ]
    for copy in copies:
        copy.start()
    for copy in copies:
        copy.wait()


def attention_kernel(hops, query_ref, grad_ref, side_rows_ref, *refs):
    count = hops + 1
    slots = 2 * count
    window = slots - 1
    homes, aways = refs[:count], refs[count : 2 * count]
    out_ref, query_grad_ref, side_out_ref = refs[2 * count : 2 * count + 3]
    home_outs = refs[2 * count + 3 : 3 * count + 3]
    away_outs = refs[3 * count + 3 : 4 * count + 3]
    (
        query_all,
        grad_all,
        out_all,
        key_log,
        value_log,
        key_turned,
        value_turned,
        doc_window,
        starts,
        flag_rows,
        key_total,
        value_total,
        logical_of,
        needed_of,
        sems,
    ) = refs[4 * count + 3 :]
    rows = query_ref.shape[0]
    per_block = rows // NBLK
    lanes = QUERY_PER_KEY * per_block
    size = 2 * rows + META
    core = core_index()
    chip = lax.axis_index("ctx") // 2
    parity = (core, 1 - core)
    scale = 1.0 / math.sqrt(HEAD_SIZE)
    factor = scale * math.log2(math.e)

    mine = pl.ds(pl.multiple_of(core * HALF, HALF), HALF)
    copies = [
        pltpu.make_async_copy(query_ref.at[:, mine], query_all.at[0], sems.at[0]),
        pltpu.make_async_copy(grad_ref.at[:, mine], grad_all.at[0], sems.at[1]),
        pltpu.make_async_copy(side_rows_ref.at[pl.ds(0, rows), :], query_all.at[1], sems.at[2]),
        pltpu.make_async_copy(side_rows_ref.at[pl.ds(rows, rows), :], grad_all.at[1], sems.at[3]),
    ]
    for copy in copies:
        copy.start()

    key_total[...] = jnp.zeros_like(key_total)
    value_total[...] = jnp.zeros_like(value_total)
    doc_window[...] = jnp.full_like(doc_window, 1e4)

    def meta_of(ref, who):
        return ref[who * size + 2 * rows : (who + 1) * size, :].astype(F32)

    for k in range(count):
        for who in range(2):
            slot = 2 * (hops - k) + parity[who]
            base = pl.multiple_of(slot * rows, rows)
            for logical, ref in ((0, homes[k]), (1, aways[k])):
                docs = meta_of(ref, who)[DOC_ROW : DOC_ROW + 1, :]
                doc_window[logical, pl.ds(slot, 1), :] = jnp.where(chip >= k, docs, -1.0)
            flags = meta_of(homes[k], who)
            for block in range(NBLK):
                mask = (
                    jnp.broadcast_to(flags[block : block + 1, :], (per_block, HEAD_SIZE)).astype(BF16)
                    > 0.5
                )
                at = pl.ds(base + block * per_block, per_block)
                for which, log in ((0, key_log), (1, value_log)):
                    first = who * size + which * rows + block * per_block
                    own = homes[k][first : first + per_block, :]
                    other = aways[k][first : first + per_block, :]
                    log[0, at, :] = jnp.where(mask, other, own)
                    log[1, at, :] = jnp.where(mask, own, other)

    for logical in range(2):
        key_turned[logical] = key_log[logical].T
        value_turned[logical] = value_log[logical].T

    values_down = lax.broadcasted_iota(I32, (DOC_VALUES, rows), 0).astype(F32)
    group = lax.broadcasted_iota(I32, (8, rows), 1) // per_block
    meta_rows = [meta_of(homes[0], who) for who in range(2)]
    for logical in range(2):
        lower = jnp.zeros((DOC_VALUES, rows), F32)
        for slot in range(slots):
            docs = jnp.broadcast_to(doc_window[logical, slot : slot + 1, :], lower.shape)
            lower = lower + jnp.where(docs < values_down, 1.0, 0.0)
        lower = jnp.broadcast_to(jnp.sum(lower, axis=1, keepdims=True), lower.shape)
        for who in range(2):
            docs = meta_of((homes, aways)[logical][0], who)[DOC_ROW : DOC_ROW + 1, :]
            docs = jnp.broadcast_to(docs, (8, rows))
            turns = [docs] + [pltpu.roll(docs, t * per_block, 1) for t in range(1, NBLK)]
            for block in range(NBLK):
                tiled = turns[0]
                for t in range(1, NBLK):
                    tiled = jnp.where(group == (block + t) % NBLK, turns[t], tiled)
                tiled = jnp.broadcast_to(tiled[:1], lower.shape)
                start = jnp.sum(jnp.where(tiled == values_down, lower, 0.0), axis=0, keepdims=True)
                starts[logical, who * NBLK + block : who * NBLK + block + 1, :] = start.astype(I32)
    for who in range(2):
        flag_rows[who * NBLK : (who + 1) * NBLK, :] = meta_rows[who][:NBLK, :]
    flags = flag_rows[...]
    firsts = [
        jnp.broadcast_to(
            jnp.min(starts[logical].astype(F32), axis=1, keepdims=True), flags.shape
        )
        for logical in range(2)
    ]
    first = jnp.where(flags > 0.5, firsts[1], firsts[0]).astype(I32)
    flags = flags.astype(I32)
    for unit_index in range(2 * NBLK):
        logical_of[unit_index] = flags[unit_index, 0]
        needed_of[unit_index] = window + parity[unit_index // NBLK] - first[unit_index, 0] // rows
    for copy in copies:
        copy.wait()

    def unit(unit_index, chunks):
        who, block = unit_index // NBLK, lax.rem(unit_index, NBLK)
        logical = logical_of[unit_index]
        row_parity = jnp.where(who == 0, core, 1 - core)
        first_slot = window + row_parity - chunks
        first = pl.multiple_of(first_slot * rows, rows)
        span = pl.ds(first, chunks * rows)
        at = pl.ds(pl.multiple_of(block * per_block, per_block), per_block)
        columns = [slice(h * HEAD_SIZE, (h + 1) * HEAD_SIZE) for h in range(QUERY_PER_KEY)]
        query = jnp.concatenate([query_all[who, at, column] for column in columns], axis=0)
        grad = jnp.concatenate([grad_all[who, at, column] for column in columns], axis=0)
        scores = lax.dot_general(key_log[logical, span, :], query, NT, preferred_element_type=F32)
        shape = (chunks * rows, HEAD_SIZE)
        key_place = lax.broadcasted_iota(I32, shape, 0)
        row_first = starts[logical, pl.ds(unit_index, 1), :] - first
        row_last = (
            (chunks - 1) * rows
            + block * per_block
            + lax.rem(lax.broadcasted_iota(I32, (1, HEAD_SIZE), 1), per_block)
        )
        allowed = (key_place >= row_first) & (key_place <= row_last)
        scores = jnp.concatenate(
            [
                jnp.where(allowed, scores[:, lane : lane + HEAD_SIZE], NEG)
                for lane in range(0, lanes, HEAD_SIZE)
            ],
            axis=1,
        )
        peak = jnp.max(scores, axis=0, keepdims=True)
        powers = jnp.exp2((scores - peak) * factor)
        inverse = 1.0 / jnp.sum(powers, axis=0, keepdims=True)
        probs = powers * inverse
        weights = probs.astype(BF16)
        out_turned = jnp.dot(
            value_turned[logical, :, span], weights, preferred_element_type=F32
        ).astype(BF16)
        delta = jnp.sum(grad.T.astype(F32) * out_turned.astype(F32), axis=0, keepdims=True)
        prob_grad = lax.dot_general(
            value_log[logical, span, :], grad, NT, preferred_element_type=F32
        )
        score_grad = (probs * (prob_grad - delta)).astype(BF16)
        query_grad_turned = jnp.dot(
            key_turned[logical, :, span], score_grad, preferred_element_type=F32
        )
        key_add = jnp.dot(score_grad, query, preferred_element_type=F32)
        value_add = jnp.dot(weights, grad, preferred_element_type=F32)
        out = out_turned.T
        query_grad = (query_grad_turned * scale).astype(BF16).T
        return who, at, logical, span, out, query_grad, key_add, value_add

    def step(pair, carry):
        members = [pair * GROUPED + m for m in range(GROUPED)]
        needed = needed_of[members[0]]
        for member in members[1:]:
            needed = jnp.maximum(needed, needed_of[member])
        for chunks in range(1, window + 1):

            @pl.when(needed == chunks)
            def _(chunks=chunks):
                results = [unit(member, chunks) for member in members]
                for who, at, logical, span, out, query_grad, key_add, value_add in results:
                    key_total[logical, span, :] += key_add
                    value_total[logical, span, :] += value_add
                    for h in range(QUERY_PER_KEY):
                        column = slice(h * HEAD_SIZE, (h + 1) * HEAD_SIZE)
                        part = slice(h * per_block, (h + 1) * per_block)
                        out_all[who, 0, at, column] = out[part, :]
                        out_all[who, 1, at, column] = query_grad[part, :]

        return carry

    lax.fori_loop(0, 2 * NBLK // GROUPED, step, 0)
    copies = [
        pltpu.make_async_copy(out_all.at[1, 0], side_out_ref.at[pl.ds(0, rows), :], sems.at[0]),
        pltpu.make_async_copy(out_all.at[1, 1], side_out_ref.at[pl.ds(rows, rows), :], sems.at[1]),
        pltpu.make_async_copy(out_all.at[0, 0], out_ref.at[:, mine], sems.at[2]),
        pltpu.make_async_copy(out_all.at[0, 1], query_grad_ref.at[:, mine], sems.at[3]),
    ]
    for copy in copies:
        copy.start()

    for k in range(count):
        for who in range(2):
            base = pl.multiple_of((2 * (hops - k) + parity[who]) * rows, rows)
            flags = meta_of(homes[k], who)
            for block in range(NBLK):
                at = pl.ds(base + block * per_block, per_block)
                mask = jnp.broadcast_to(flags[block : block + 1, :], (per_block, HEAD_SIZE)) > 0.5
                for which, total, gain in ((0, key_total, scale), (1, value_total, 1.0)):
                    part = (2 * who + which) * rows + block * per_block
                    first = total[0, at, :] * gain
                    second = total[1, at, :] * gain
                    home_outs[k][part : part + per_block, :] = jnp.where(mask, second, first).astype(BF16)
                    away_outs[k][part : part + per_block, :] = jnp.where(mask, first, second).astype(BF16)
    for copy in copies:
        copy.wait()


def local(queries, key_rows, value_rows, out_grad, documents, swapped):
    ranks = lax.axis_size("ctx")
    hops = ranks // 4
    count = hops + 1
    slots = 2 * count
    rows, width = key_rows.shape[1:]
    keys = slots * rows
    size = 2 * rows + META
    queries, out_grad = queries[0], out_grad[0]

    def up(block):
        return lax.ppermute(block, "ctx", [(i, i + 2) for i in range(ranks - 2)])

    def down(block):
        return lax.ppermute(block, "ctx", [(i + 2, i) for i in range(ranks - 2)])

    def to_partner(block):
        return lax.ppermute(block, "half", [(0, 1), (1, 0)])

    def to_side(block):
        return lax.ppermute(block, "ctx", [(i, i ^ 1) for i in range(ranks)])

    payload, payload_side = pl.pallas_call(
        payload_kernel,
        out_shape=[pltpu.VMEM((size, HEAD_SIZE), BF16)] * 2,
        in_specs=[SMEM, VMEM, VMEM, VMEM],
        out_specs=[VMEM, VMEM],
    )(swapped[0, 0], key_rows[0], value_rows[0], documents)
    from_side = to_side(payload_side)
    rows_side = pl.pallas_call(
        rows_kernel,
        out_shape=pltpu.VMEM((2 * rows, HALF), BF16),
        in_specs=[HBM, HBM],
        out_specs=VMEM,
        scratch_shapes=[pltpu.SemaphoreType.DMA((2,))],
    )(queries, out_grad)
    both = jnp.concatenate([payload, from_side], axis=0)
    both, rows_side = lax.optimization_barrier((both, rows_side))
    rows_got = to_side(rows_side)
    home = [both]
    for _ in range(hops):
        home.append(up(home[-1]))
    away = [to_partner(block) for block in home]
    chunk = pltpu.VMEM((4 * rows, HEAD_SIZE), BF16)
    outs = pl.pallas_call(
        functools.partial(attention_kernel, hops),
        out_shape=[jax.ShapeDtypeStruct(queries.shape, BF16)] * 2
        + [pltpu.VMEM((2 * rows, HALF), BF16)]
        + [chunk] * (2 * count),
        in_specs=[HBM, HBM, pl.BlockSpec(memory_space=pl.ANY)] + [VMEM] * (2 * count),
        out_specs=[HBM] * 2 + [VMEM] * (1 + 2 * count),
        scratch_shapes=[
            pltpu.VMEM((2, rows, HALF), BF16),
            pltpu.VMEM((2, rows, HALF), BF16),
            pltpu.VMEM((2, 2, rows, HALF), BF16),
            pltpu.VMEM((2, keys, HEAD_SIZE), BF16),
            pltpu.VMEM((2, keys, HEAD_SIZE), BF16),
            pltpu.VMEM((2, HEAD_SIZE, keys), BF16),
            pltpu.VMEM((2, HEAD_SIZE, keys), BF16),
            pltpu.VMEM((2, 16, rows), F32),
            pltpu.VMEM((2, 8, rows), I32),
            pltpu.VMEM((8, rows), F32),
            pltpu.VMEM((2, keys, HEAD_SIZE), F32),
            pltpu.VMEM((2, keys, HEAD_SIZE), F32),
            pltpu.SMEM((2 * NBLK,), I32),
            pltpu.SMEM((2 * NBLK,), I32),
            pltpu.SemaphoreType.DMA((4,)),
        ],
        compiler_params=pltpu.CompilerParams(vmem_limit_bytes=40 * 1024 * 1024),
        cost_estimate=pl.CostEstimate(
            flops=12 * rows * keys * 2048,
            bytes_accessed=4 * 1024 * 1024,
            transcendentals=rows * keys * 16,
        ),
    )(queries, out_grad, rows_got, *home, *away)
    out, query_grad, side_out = outs[:3]
    home_sum, away_sum = outs[3 : 3 + count], list(outs[3 + count :])

    total = None
    for k in reversed(range(count)):
        part = home_sum[k].astype(F32) + to_partner(away_sum[k]).astype(F32)
        if total is not None:
            part = part + total.astype(F32)
        total = part.astype(BF16)
        if k == hops:
            total, side_out, *away_sum[:k] = lax.optimization_barrier(
                (total, side_out, *away_sum[:k])
            )
            out_got = to_side(side_out)
        if k:
            total = down(total)
        if k == 1:
            out, query_grad = pl.pallas_call(
                finish_kernel,
                out_shape=[jax.ShapeDtypeStruct(queries.shape, BF16)] * 2,
                in_specs=[VMEM, HBM, HBM],
                out_specs=[HBM] * 2,
                input_output_aliases={1: 0, 2: 1},
                scratch_shapes=[pltpu.SemaphoreType.DMA((2,))],
            )(out_got, out, query_grad)
            total, out, query_grad = lax.optimization_barrier((total, out, query_grad))
    grads_got = to_side(total[2 * rows :])
    grads = total[: 2 * rows]
    first = core_index() == 0
    grads = jnp.concatenate(
        [jnp.where(first, grads, grads_got), jnp.where(first, grads_got, grads)], axis=1
    )
    return (out[None], query_grad[None], grads[None, :rows], grads[None, rows:])


def solution(mesh):
    groups, ranks = mesh.devices.shape
    wide = Mesh(mesh.devices.reshape(2, groups // 2, ranks), ("half", "pair", "ctx"))
    spec3 = P(("half", "pair"), "ctx", None)
    in_specs = (spec3, spec3, spec3, spec3, P(("half", "pair"), "ctx"), spec3)
    return jax.shard_map(
        local, mesh=wide, in_specs=in_specs, out_specs=(spec3,) * 4, check_vma=False
    )
```

```python
import functools
import math

import jax
import jax.numpy as jnp
from jax import lax
from jax.experimental import pallas as pl
from jax.experimental.pallas import tpu as pltpu
from jax.sharding import Mesh
from jax.sharding import PartitionSpec as P

HEAD_SIZE = 128
QUERY_PER_KEY = 8
NBLK = 4
META = 16
DOC_ROW = NBLK
DOC_VALUES = 16
GROUPED = 4
HALF = QUERY_PER_KEY * HEAD_SIZE
NEG = -1e30
F32, BF16, I32 = jnp.float32, jnp.bfloat16, jnp.int32
NT = (((1,), (1,)), ((), ()))
VMEM = pl.BlockSpec(memory_space=pltpu.VMEM)
SMEM = pl.BlockSpec(memory_space=pltpu.SMEM)
HBM = pl.BlockSpec(memory_space=pltpu.HBM)


def core_index():
    return lax.rem(lax.axis_index("ctx"), 2)


def payload_kernel(swap_ref, key_ref, value_ref, docs_ref, own_ref, side_ref):
    rows = key_ref.shape[0]
    core = core_index()
    docs = jnp.broadcast_to(docs_ref[...].astype(F32), (META, rows))
    place = lax.broadcasted_iota(I32, docs.shape, 0)
    meta = jnp.where(place == DOC_ROW, docs, 0.0)
    for block in range(NBLK):
        meta = jnp.where(place == block, swap_ref[block].astype(F32), meta)
    meta = meta.astype(BF16)
    for ref, head in ((own_ref, core), (side_ref, 1 - core)):
        lane = pl.ds(pl.multiple_of(head * HEAD_SIZE, HEAD_SIZE), HEAD_SIZE)
        ref[:rows, :] = key_ref[:, lane]
        ref[rows : 2 * rows, :] = value_ref[:, lane]
        ref[2 * rows :, :] = meta


def rows_kernel(query_ref, grad_ref, rows_ref, sems):
    rows = query_ref.shape[0]
    away = pl.ds(pl.multiple_of((1 - core_index()) * HALF, HALF), HALF)
    copies = [
        pltpu.make_async_copy(
            source.at[:, away], rows_ref.at[pl.ds(part * rows, rows), :], sems.at[part]
        )
        for part, source in enumerate((query_ref, grad_ref))
    ]
    for copy in copies:
        copy.start()
    for copy in copies:
        copy.wait()


def finish_kernel(side_ref, out_held, query_grad_held, out_ref, query_grad_ref, sems):
    rows = out_ref.shape[0]
    away = pl.ds(pl.multiple_of((1 - core_index()) * HALF, HALF), HALF)
    copies = [
        pltpu.make_async_copy(
            side_ref.at[pl.ds(part * rows, rows), :], target.at[:, away], sems.at[part]
        )
        for part, target in enumerate((out_ref, query_grad_ref))
    ]
    for copy in copies:
        copy.start()
    for copy in copies:
        copy.wait()


def attention_kernel(hops, query_ref, grad_ref, side_rows_ref, *refs):
    count = hops + 1
    slots = 2 * count
    window = slots - 1
    homes, aways = refs[:count], refs[count : 2 * count]
    out_ref, query_grad_ref, side_out_ref = refs[2 * count : 2 * count + 3]
    home_outs = refs[2 * count + 3 : 3 * count + 3]
    away_outs = refs[3 * count + 3 : 4 * count + 3]
    (
        query_all,
        grad_all,
        out_all,
        key_log,
        value_log,
        key_turned,
        value_turned,
        doc_window,
        starts,
        flag_rows,
        eye,
        key_total,
        value_total,
        logical_of,
        needed_of,
        sems,
    ) = refs[4 * count + 3 :]
    rows = query_ref.shape[0]
    per_block = rows // NBLK
    lanes = QUERY_PER_KEY * per_block
    size = 2 * rows + META
    core = core_index()
    chip = lax.axis_index("ctx") // 2
    parity = (core, 1 - core)
    scale = 1.0 / math.sqrt(HEAD_SIZE)
    factor = scale * math.log2(math.e)

    mine = pl.ds(pl.multiple_of(core * HALF, HALF), HALF)
    copies = [
        pltpu.make_async_copy(query_ref.at[:, mine], query_all.at[0], sems.at[0]),
        pltpu.make_async_copy(grad_ref.at[:, mine], grad_all.at[0], sems.at[1]),
        pltpu.make_async_copy(side_rows_ref.at[pl.ds(0, rows), :], query_all.at[1], sems.at[2]),
        pltpu.make_async_copy(side_rows_ref.at[pl.ds(rows, rows), :], grad_all.at[1], sems.at[3]),
    ]
    for copy in copies:
        copy.start()

    key_total[...] = jnp.zeros_like(key_total)
    value_total[...] = jnp.zeros_like(value_total)
    doc_window[...] = jnp.full_like(doc_window, 1e4)

    def meta_of(ref, who):
        return ref[who * size + 2 * rows : (who + 1) * size, :].astype(F32)

    for k in range(count):
        for who in range(2):
            slot = 2 * (hops - k) + parity[who]
            base = pl.multiple_of(slot * rows, rows)
            for logical, ref in ((0, homes[k]), (1, aways[k])):
                docs = meta_of(ref, who)[DOC_ROW : DOC_ROW + 1, :]
                doc_window[logical, pl.ds(slot, 1), :] = jnp.where(chip >= k, docs, -1.0)
            flags = meta_of(homes[k], who)
            for block in range(NBLK):
                mask = (
                    jnp.broadcast_to(flags[block : block + 1, :], (per_block, HEAD_SIZE)).astype(BF16)
                    > 0.5
                )
                at = pl.ds(base + block * per_block, per_block)
                for which, log in ((0, key_log), (1, value_log)):
                    first = who * size + which * rows + block * per_block
                    own = homes[k][first : first + per_block, :]
                    other = aways[k][first : first + per_block, :]
                    log[0, at, :] = jnp.where(mask, other, own)
                    log[1, at, :] = jnp.where(mask, own, other)

    eye[...] = jnp.where(
        lax.broadcasted_iota(I32, eye.shape, 0) == lax.broadcasted_iota(I32, eye.shape, 1), 1.0, 0.0
    ).astype(BF16)

    def turn(block):
        unit_matrix = eye[: block.shape[1], : block.shape[1]]
        return lax.dot_general(unit_matrix, block, NT, preferred_element_type=F32)

    for logical in range(2):
        key_turned[logical] = turn(key_log[logical]).astype(BF16)
        value_turned[logical] = turn(value_log[logical]).astype(BF16)

    values_down = lax.broadcasted_iota(I32, (DOC_VALUES, rows), 0).astype(F32)
    group = lax.broadcasted_iota(I32, (8, rows), 1) // per_block
    meta_rows = [meta_of(homes[0], who) for who in range(2)]
    for logical in range(2):
        lower = jnp.zeros((DOC_VALUES, rows), F32)
        for slot in range(slots):
            docs = jnp.broadcast_to(doc_window[logical, slot : slot + 1, :], lower.shape)
            lower = lower + jnp.where(docs < values_down, 1.0, 0.0)
        lower = jnp.broadcast_to(jnp.sum(lower, axis=1, keepdims=True), lower.shape)
        for who in range(2):
            docs = meta_of((homes, aways)[logical][0], who)[DOC_ROW : DOC_ROW + 1, :]
            docs = jnp.broadcast_to(docs, (8, rows))
            turns = [docs] + [pltpu.roll(docs, t * per_block, 1) for t in range(1, NBLK)]
            for block in range(NBLK):
                tiled = turns[0]
                for t in range(1, NBLK):
                    tiled = jnp.where(group == (block + t) % NBLK, turns[t], tiled)
                tiled = jnp.broadcast_to(tiled[:1], lower.shape)
                start = jnp.sum(jnp.where(tiled == values_down, lower, 0.0), axis=0, keepdims=True)
                starts[logical, who * NBLK + block : who * NBLK + block + 1, :] = start.astype(I32)
    for who in range(2):
        flag_rows[who * NBLK : (who + 1) * NBLK, :] = meta_rows[who][:NBLK, :]
    flags = flag_rows[...]
    firsts = [
        jnp.broadcast_to(
            jnp.min(starts[logical].astype(F32), axis=1, keepdims=True), flags.shape
        )
        for logical in range(2)
    ]
    first = jnp.where(flags > 0.5, firsts[1], firsts[0]).astype(I32)
    flags = flags.astype(I32)
    for unit_index in range(2 * NBLK):
        logical_of[unit_index] = flags[unit_index, 0]
        needed_of[unit_index] = window + parity[unit_index // NBLK] - first[unit_index, 0] // rows
    for copy in copies:
        copy.wait()

    def unit(unit_index, chunks):
        who, block = unit_index // NBLK, lax.rem(unit_index, NBLK)
        logical = logical_of[unit_index]
        row_parity = jnp.where(who == 0, core, 1 - core)
        first_slot = window + row_parity - chunks
        first = pl.multiple_of(first_slot * rows, rows)
        span = pl.ds(first, chunks * rows)
        at = pl.ds(pl.multiple_of(block * per_block, per_block), per_block)
        columns = [slice(h * HEAD_SIZE, (h + 1) * HEAD_SIZE) for h in range(QUERY_PER_KEY)]
        query = jnp.concatenate([query_all[who, at, column] for column in columns], axis=0)
        grad = jnp.concatenate([grad_all[who, at, column] for column in columns], axis=0)
        scores = lax.dot_general(key_log[logical, span, :], query, NT, preferred_element_type=F32)
        shape = (chunks * rows, HEAD_SIZE)
        key_place = lax.broadcasted_iota(I32, shape, 0)
        row_first = starts[logical, pl.ds(unit_index, 1), :] - first
        row_last = (
            (chunks - 1) * rows
            + block * per_block
            + lax.rem(lax.broadcasted_iota(I32, (1, HEAD_SIZE), 1), per_block)
        )
        allowed = (key_place >= row_first) & (key_place <= row_last)
        scores = jnp.concatenate(
            [
                jnp.where(allowed, scores[:, lane : lane + HEAD_SIZE], NEG)
                for lane in range(0, lanes, HEAD_SIZE)
            ],
            axis=1,
        )
        peak = jnp.max(scores, axis=0, keepdims=True)
        powers = jnp.exp2((scores - peak) * factor)
        inverse = 1.0 / jnp.sum(powers, axis=0, keepdims=True)
        probs = powers * inverse
        weights = probs.astype(BF16)
        out_turned = jnp.dot(
            value_turned[logical, :, span], weights, preferred_element_type=F32
        ).astype(BF16)
        delta = jnp.sum(turn(grad) * out_turned.astype(F32), axis=0, keepdims=True)
        prob_grad = lax.dot_general(
            value_log[logical, span, :], grad, NT, preferred_element_type=F32
        )
        score_grad = (probs * (prob_grad - delta)).astype(BF16)
        query_grad_turned = jnp.dot(
            key_turned[logical, :, span], score_grad, preferred_element_type=F32
        )
        key_add = jnp.dot(score_grad, query, preferred_element_type=F32)
        value_add = jnp.dot(weights, grad, preferred_element_type=F32)
        out = turn(out_turned).astype(BF16)
        query_grad = turn((query_grad_turned * scale).astype(BF16)).astype(BF16)
        return who, at, logical, span, out, query_grad, key_add, value_add

    def step(pair, carry):
        members = [pair * GROUPED + m for m in range(GROUPED)]
        needed = needed_of[members[0]]
        for member in members[1:]:
            needed = jnp.maximum(needed, needed_of[member])
        for chunks in range(1, window + 1):

            @pl.when(needed == chunks)
            def _(chunks=chunks):
                results = [unit(member, chunks) for member in members]
                for who, at, logical, span, out, query_grad, key_add, value_add in results:
                    key_total[logical, span, :] += key_add
                    value_total[logical, span, :] += value_add
                    for h in range(QUERY_PER_KEY):
                        column = slice(h * HEAD_SIZE, (h + 1) * HEAD_SIZE)
                        part = slice(h * per_block, (h + 1) * per_block)
                        out_all[who, 0, at, column] = out[part, :]
                        out_all[who, 1, at, column] = query_grad[part, :]

        return carry

    lax.fori_loop(0, 2 * NBLK // GROUPED, step, 0)
    copies = [
        pltpu.make_async_copy(out_all.at[1, 0], side_out_ref.at[pl.ds(0, rows), :], sems.at[0]),
        pltpu.make_async_copy(out_all.at[1, 1], side_out_ref.at[pl.ds(rows, rows), :], sems.at[1]),
        pltpu.make_async_copy(out_all.at[0, 0], out_ref.at[:, mine], sems.at[2]),
        pltpu.make_async_copy(out_all.at[0, 1], query_grad_ref.at[:, mine], sems.at[3]),
    ]
    for copy in copies:
        copy.start()

    for k in range(count):
        for who in range(2):
            base = pl.multiple_of((2 * (hops - k) + parity[who]) * rows, rows)
            flags = meta_of(homes[k], who)
            for block in range(NBLK):
                at = pl.ds(base + block * per_block, per_block)
                mask = jnp.broadcast_to(flags[block : block + 1, :], (per_block, HEAD_SIZE)) > 0.5
                for which, total, gain in ((0, key_total, scale), (1, value_total, 1.0)):
                    part = (2 * who + which) * rows + block * per_block
                    first = total[0, at, :] * gain
                    second = total[1, at, :] * gain
                    home_outs[k][part : part + per_block, :] = jnp.where(mask, second, first).astype(BF16)
                    away_outs[k][part : part + per_block, :] = jnp.where(mask, first, second).astype(BF16)
    for copy in copies:
        copy.wait()


def local(queries, key_rows, value_rows, out_grad, documents, swapped):
    ranks = lax.axis_size("ctx")
    hops = ranks // 4
    count = hops + 1
    slots = 2 * count
    rows, width = key_rows.shape[1:]
    keys = slots * rows
    size = 2 * rows + META
    queries, out_grad = queries[0], out_grad[0]

    def up(block, k):
        return lax.ppermute(block, "ctx", [(i, i + 2 * k) for i in range(ranks - 2 * k)])

    def down(block, k):
        return lax.ppermute(block, "ctx", [(i + 2 * k, i) for i in range(ranks - 2 * k)])

    def to_partner(block):
        return lax.ppermute(block, "half", [(0, 1), (1, 0)])

    def to_side(block):
        return lax.ppermute(block, "ctx", [(i, i ^ 1) for i in range(ranks)])

    payload, payload_side = pl.pallas_call(
        payload_kernel,
        out_shape=[pltpu.VMEM((size, HEAD_SIZE), BF16)] * 2,
        in_specs=[SMEM, VMEM, VMEM, VMEM],
        out_specs=[VMEM, VMEM],
    )(swapped[0, 0], key_rows[0], value_rows[0], documents)
    from_side = to_side(payload_side)
    rows_side = pl.pallas_call(
        rows_kernel,
        out_shape=pltpu.VMEM((2 * rows, HALF), BF16),
        in_specs=[HBM, HBM],
        out_specs=VMEM,
        scratch_shapes=[pltpu.SemaphoreType.DMA((2,))],
    )(queries, out_grad)
    both = jnp.concatenate([payload, from_side], axis=0)
    both, rows_side = lax.optimization_barrier((both, rows_side))
    rows_got = to_side(rows_side)
    home = [both] + [up(both, k) for k in range(1, count)]
    away = [to_partner(block) for block in home]
    chunk = pltpu.VMEM((4 * rows, HEAD_SIZE), BF16)
    outs = pl.pallas_call(
        functools.partial(attention_kernel, hops),
        out_shape=[jax.ShapeDtypeStruct(queries.shape, BF16)] * 2
        + [pltpu.VMEM((2 * rows, HALF), BF16)]
        + [chunk] * (2 * count),
        in_specs=[HBM, HBM, pl.BlockSpec(memory_space=pl.ANY)] + [VMEM] * (2 * count),
        out_specs=[HBM] * 2 + [VMEM] * (1 + 2 * count),
        scratch_shapes=[
            pltpu.VMEM((2, rows, HALF), BF16),
            pltpu.VMEM((2, rows, HALF), BF16),
            pltpu.VMEM((2, 2, rows, HALF), BF16),
            pltpu.VMEM((2, keys, HEAD_SIZE), BF16),
            pltpu.VMEM((2, keys, HEAD_SIZE), BF16),
            pltpu.VMEM((2, HEAD_SIZE, keys), BF16),
            pltpu.VMEM((2, HEAD_SIZE, keys), BF16),
            pltpu.VMEM((2, 16, rows), F32),
            pltpu.VMEM((2, 8, rows), I32),
            pltpu.VMEM((8, rows), F32),
            pltpu.VMEM((2 * rows, 2 * rows), BF16),
            pltpu.VMEM((2, keys, HEAD_SIZE), F32),
            pltpu.VMEM((2, keys, HEAD_SIZE), F32),
            pltpu.SMEM((2 * NBLK,), I32),
            pltpu.SMEM((2 * NBLK,), I32),
            pltpu.SemaphoreType.DMA((4,)),
        ],
        compiler_params=pltpu.CompilerParams(vmem_limit_bytes=40 * 1024 * 1024),
        cost_estimate=pl.CostEstimate(
            flops=12 * rows * keys * 2048,
            bytes_accessed=4 * 1024 * 1024,
            transcendentals=rows * keys * 16,
        ),
    )(queries, out_grad, rows_got, *home, *away)
    out, query_grad, side_out = outs[:3]
    home_sum, away_sum = outs[3 : 3 + count], list(outs[3 + count :])

    parts = []
    for k in reversed(range(count)):
        part = home_sum[k].astype(F32) + to_partner(away_sum[k]).astype(F32)
        if k:
            part = part.astype(BF16)
            part = down(part, k)
        parts.append(part)
    out_got = to_side(side_out)
    out, query_grad = pl.pallas_call(
        finish_kernel,
        out_shape=[jax.ShapeDtypeStruct(queries.shape, BF16)] * 2,
        in_specs=[VMEM, HBM, HBM],
        out_specs=[HBM] * 2,
        input_output_aliases={1: 0, 2: 1},
        scratch_shapes=[pltpu.SemaphoreType.DMA((2,))],
    )(out_got, out, query_grad)
    parts[0], out, query_grad = lax.optimization_barrier((parts[0], out, query_grad))
    total = sum(part.astype(F32) for part in parts).astype(BF16)
    grads_got = to_side(total[2 * rows :])
    grads = total[: 2 * rows]
    first = core_index() == 0
    grads = jnp.concatenate(
        [jnp.where(first, grads, grads_got), jnp.where(first, grads_got, grads)], axis=1
    )
    return (out[None], query_grad[None], grads[None, :rows], grads[None, rows:])


def solution(mesh):
    groups, ranks = mesh.devices.shape
    wide = Mesh(mesh.devices.reshape(2, groups // 2, ranks), ("half", "pair", "ctx"))
    spec3 = P(("half", "pair"), "ctx", None)
    in_specs = (spec3, spec3, spec3, spec3, P(("half", "pair"), "ctx"), spec3)
    return jax.shard_map(
        local, mesh=wide, in_specs=in_specs, out_specs=(spec3,) * 4, check_vma=False
    )
```

```python
import functools
import math

import jax
import jax.numpy as jnp
from jax import lax
from jax.experimental import pallas as pl
from jax.experimental.pallas import tpu as pltpu
from jax.sharding import Mesh
from jax.sharding import PartitionSpec as P

HEAD_SIZE = 128
QUERY_PER_KEY = 8
NBLK = 4
META = 16
DOC_ROW = NBLK
DOC_VALUES = 16
GROUPED = 4
HALF = QUERY_PER_KEY * HEAD_SIZE
NEG = -1e30
F32, BF16, I32 = jnp.float32, jnp.bfloat16, jnp.int32
NT = (((1,), (1,)), ((), ()))
VMEM = pl.BlockSpec(memory_space=pltpu.VMEM)
SMEM = pl.BlockSpec(memory_space=pltpu.SMEM)
HBM = pl.BlockSpec(memory_space=pltpu.HBM)


def core_index():
    return lax.rem(lax.axis_index("ctx"), 2)


def payload_kernel(swap_ref, key_ref, value_ref, docs_ref, own_ref, side_ref):
    rows = key_ref.shape[0]
    core = core_index()
    docs = jnp.broadcast_to(docs_ref[...].astype(F32), (META, rows))
    place = lax.broadcasted_iota(I32, docs.shape, 0)
    meta = jnp.where(place == DOC_ROW, docs, 0.0)
    for block in range(NBLK):
        meta = jnp.where(place == block, swap_ref[block].astype(F32), meta)
    meta = meta.astype(BF16)
    for ref, head in ((own_ref, core), (side_ref, 1 - core)):
        lane = pl.ds(pl.multiple_of(head * HEAD_SIZE, HEAD_SIZE), HEAD_SIZE)
        ref[:rows, :] = key_ref[:, lane]
        ref[rows : 2 * rows, :] = value_ref[:, lane]
        ref[2 * rows :, :] = meta


def rows_kernel(other, query_ref, grad_ref, rows_ref, sems):
    rows = query_ref.shape[0]
    core = core_index()
    head = 1 - core if other else core
    lanes = pl.ds(pl.multiple_of(head * HALF, HALF), HALF)
    copies = [
        pltpu.make_async_copy(
            source.at[:, lanes], rows_ref.at[pl.ds(part * rows, rows), :], sems.at[part]
        )
        for part, source in enumerate((query_ref, grad_ref))
    ]
    for copy in copies:
        copy.start()
    for copy in copies:
        copy.wait()


def write_heads(source_ref, head, out_ref, query_grad_ref, sems):
    rows = out_ref.shape[0]
    lanes = pl.ds(pl.multiple_of(head * HALF, HALF), HALF)
    copies = [
        pltpu.make_async_copy(
            source_ref.at[pl.ds(part * rows, rows), :], target.at[:, lanes], sems.at[part]
        )
        for part, target in enumerate((out_ref, query_grad_ref))
    ]
    for copy in copies:
        copy.start()
    for copy in copies:
        copy.wait()


def own_kernel(own_ref, out_ref, query_grad_ref, sems):
    write_heads(own_ref, core_index(), out_ref, query_grad_ref, sems)


def finish_kernel(side_ref, out_held, query_grad_held, out_ref, query_grad_ref, sems):
    write_heads(side_ref, 1 - core_index(), out_ref, query_grad_ref, sems)


def merge_hop(home, away, slots_at, rows, logs):
    key_log, value_log, key_turned, value_turned = logs
    per_block = rows // NBLK
    size = 2 * rows + META
    for who in range(2):
        base = pl.multiple_of(slots_at[who] * rows, rows)
        flags = home[who * size + 2 * rows : (who + 1) * size, :].astype(F32)
        for which, log, turned in ((0, key_log, key_turned), (1, value_log, value_turned)):
            merged = ([], [])
            for block in range(NBLK):
                mask = (
                    jnp.broadcast_to(flags[block : block + 1, :], (per_block, HEAD_SIZE)).astype(BF16)
                    > 0.5
                )
                first = who * size + which * rows + block * per_block
                own = home[first : first + per_block, :]
                other = away[first : first + per_block, :]
                merged[0].append(jnp.where(mask, other, own))
                merged[1].append(jnp.where(mask, own, other))
            for logical in range(2):
                whole = jnp.concatenate(merged[logical], axis=0)
                log[logical, pl.ds(base, rows), :] = whole
                turned[logical, :, pl.ds(base, rows)] = whole.T


def prepare_kernel(hops, *refs):
    homes, aways = refs[:hops], refs[hops : 2 * hops]
    logs = refs[2 * hops :]
    rows = (homes[0].shape[0] // 2 - META) // 2
    core = core_index()
    parity = (core, 1 - core)
    for k in range(hops):
        slots_at = [2 * (hops - 1 - k) + parity[who] for who in range(2)]
        merge_hop(homes[k], aways[k], slots_at, rows, logs)


def attention_kernel(hops, rows_ref, *refs):
    count = hops + 1
    slots = 2 * count
    window = slots - 1
    homes, aways = refs[:count], refs[count : 2 * count]
    ready = refs[2 * count : 2 * count + 4]
    out_all = refs[2 * count + 4]
    home_outs = refs[2 * count + 5 : 3 * count + 5]
    away_outs = refs[3 * count + 5 : 4 * count + 5]
    (
        key_log,
        value_log,
        key_turned,
        value_turned,
        doc_window,
        starts,
        flag_rows,
        key_total,
        value_total,
        logical_of,
        needed_of,
    ) = refs[4 * count + 5 :]
    rows = rows_ref.shape[0] // 4
    per_block = rows // NBLK
    lanes = QUERY_PER_KEY * per_block
    size = 2 * rows + META
    core = core_index()
    chip = lax.axis_index("ctx") // 2
    parity = (core, 1 - core)
    scale = 1.0 / math.sqrt(HEAD_SIZE)
    factor = scale * math.log2(math.e)

    key_total[...] = jnp.zeros_like(key_total)
    value_total[...] = jnp.zeros_like(value_total)
    doc_window[...] = jnp.full_like(doc_window, 1e4)

    def meta_of(ref, who):
        return ref[who * size + 2 * rows : (who + 1) * size, :].astype(F32)

    for k in range(count):
        for who in range(2):
            slot = 2 * (hops - k) + parity[who]
            base = pl.multiple_of(slot * rows, rows)
            for logical, ref in ((0, homes[k]), (1, aways[k])):
                docs = meta_of(ref, who)[DOC_ROW : DOC_ROW + 1, :]
                doc_window[logical, pl.ds(slot, 1), :] = jnp.where(chip >= k, docs, -1.0)
    logs = (key_log, value_log, key_turned, value_turned)
    for log, held in zip(logs[:2], ready[:2]):
        log[:, pl.ds(2 * rows, 2 * rows * hops), :] = held[...]
    for log, held in zip(logs[2:], ready[2:]):
        log[:, :, pl.ds(2 * rows, 2 * rows * hops)] = held[...]
    merge_hop(homes[hops], aways[hops], parity, rows, logs)

    values_down = lax.broadcasted_iota(I32, (DOC_VALUES, rows), 0).astype(F32)
    group = lax.broadcasted_iota(I32, (8, rows), 1) // per_block
    meta_rows = [meta_of(homes[0], who) for who in range(2)]
    for logical in range(2):
        lower = jnp.zeros((DOC_VALUES, rows), F32)
        for slot in range(slots):
            docs = jnp.broadcast_to(doc_window[logical, slot : slot + 1, :], lower.shape)
            lower = lower + jnp.where(docs < values_down, 1.0, 0.0)
        lower = jnp.broadcast_to(jnp.sum(lower, axis=1, keepdims=True), lower.shape)
        for who in range(2):
            docs = meta_of((homes, aways)[logical][0], who)[DOC_ROW : DOC_ROW + 1, :]
            docs = jnp.broadcast_to(docs, (8, rows))
            turns = [docs] + [pltpu.roll(docs, t * per_block, 1) for t in range(1, NBLK)]
            for block in range(NBLK):
                tiled = turns[0]
                for t in range(1, NBLK):
                    tiled = jnp.where(group == (block + t) % NBLK, turns[t], tiled)
                tiled = jnp.broadcast_to(tiled[:1], lower.shape)
                start = jnp.sum(jnp.where(tiled == values_down, lower, 0.0), axis=0, keepdims=True)
                starts[logical, who * NBLK + block : who * NBLK + block + 1, :] = start.astype(I32)
    for who in range(2):
        flag_rows[who * NBLK : (who + 1) * NBLK, :] = meta_rows[who][:NBLK, :]
    flags = flag_rows[...]
    firsts = [
        jnp.broadcast_to(
            jnp.min(starts[logical].astype(F32), axis=1, keepdims=True), flags.shape
        )
        for logical in range(2)
    ]
    first = jnp.where(flags > 0.5, firsts[1], firsts[0]).astype(I32)
    flags = flags.astype(I32)
    for unit_index in range(2 * NBLK):
        logical_of[unit_index] = flags[unit_index, 0]
        needed_of[unit_index] = window + parity[unit_index // NBLK] - first[unit_index, 0] // rows

    def unit(unit_index, chunks):
        who, block = unit_index // NBLK, lax.rem(unit_index, NBLK)
        logical = logical_of[unit_index]
        row_parity = jnp.where(who == 0, core, 1 - core)
        first_slot = window + row_parity - chunks
        first = pl.multiple_of(first_slot * rows, rows)
        span = pl.ds(first, chunks * rows)
        columns = [slice(h * HEAD_SIZE, (h + 1) * HEAD_SIZE) for h in range(QUERY_PER_KEY)]
        query_at = pl.ds(pl.multiple_of(2 * who * rows + block * per_block, per_block), per_block)
        grad_at = pl.ds(
            pl.multiple_of((2 * who + 1) * rows + block * per_block, per_block), per_block
        )
        query = jnp.concatenate([rows_ref[query_at, column] for column in columns], axis=0)
        grad = jnp.concatenate([rows_ref[grad_at, column] for column in columns], axis=0)
        scores = lax.dot_general(key_log[logical, span, :], query, NT, preferred_element_type=F32)
        shape = (chunks * rows, HEAD_SIZE)
        key_place = lax.broadcasted_iota(I32, shape, 0)
        row_first = starts[logical, pl.ds(unit_index, 1), :] - first
        row_last = (
            (chunks - 1) * rows
            + block * per_block
            + lax.rem(lax.broadcasted_iota(I32, (1, HEAD_SIZE), 1), per_block)
        )
        allowed = (key_place >= row_first) & (key_place <= row_last)
        scores = jnp.concatenate(
            [
                jnp.where(allowed, scores[:, lane : lane + HEAD_SIZE], NEG)
                for lane in range(0, lanes, HEAD_SIZE)
            ],
            axis=1,
        )
        peak = jnp.max(scores, axis=0, keepdims=True)
        powers = jnp.exp2((scores - peak) * factor)
        inverse = 1.0 / jnp.sum(powers, axis=0, keepdims=True)
        probs = powers * inverse
        weights = probs.astype(BF16)
        out_turned = jnp.dot(
            value_turned[logical, :, span], weights, preferred_element_type=F32
        ).astype(BF16)
        delta = jnp.sum(grad.T.astype(F32) * out_turned.astype(F32), axis=0, keepdims=True)
        prob_grad = lax.dot_general(
            value_log[logical, span, :], grad, NT, preferred_element_type=F32
        )
        score_grad = (probs * (prob_grad - delta)).astype(BF16)
        query_grad_turned = jnp.dot(
            key_turned[logical, :, span], score_grad, preferred_element_type=F32
        )
        key_add = jnp.dot(score_grad, query, preferred_element_type=F32)
        value_add = jnp.dot(weights, grad, preferred_element_type=F32)
        out = out_turned.T
        query_grad = (query_grad_turned * scale).astype(BF16).T
        return query_at, grad_at, logical, span, out, query_grad, key_add, value_add

    def step(pair, carry):
        members = [pair * GROUPED + m for m in range(GROUPED)]
        needed = needed_of[members[0]]
        for member in members[1:]:
            needed = jnp.maximum(needed, needed_of[member])
        for chunks in range(1, window + 1):

            @pl.when(needed == chunks)
            def _(chunks=chunks):
                results = [unit(member, chunks) for member in members]
                for query_at, grad_at, logical, span, out, query_grad, key_add, value_add in results:
                    key_total[logical, span, :] += key_add
                    value_total[logical, span, :] += value_add
                    for h in range(QUERY_PER_KEY):
                        column = slice(h * HEAD_SIZE, (h + 1) * HEAD_SIZE)
                        part = slice(h * per_block, (h + 1) * per_block)
                        out_all[query_at, column] = out[part, :]
                        out_all[grad_at, column] = query_grad[part, :]

        return carry

    lax.fori_loop(0, 2 * NBLK // GROUPED, step, 0)
    for k in range(count):
        for who in range(2):
            base = pl.multiple_of((2 * (hops - k) + parity[who]) * rows, rows)
            flags = meta_of(homes[k], who)
            for block in range(NBLK):
                at = pl.ds(base + block * per_block, per_block)
                mask = jnp.broadcast_to(flags[block : block + 1, :], (per_block, HEAD_SIZE)) > 0.5
                for which, total, gain in ((0, key_total, scale), (1, value_total, 1.0)):
                    part = (2 * who + which) * rows + block * per_block
                    first = total[0, at, :] * gain
                    second = total[1, at, :] * gain
                    home_outs[k][part : part + per_block, :] = jnp.where(mask, second, first).astype(BF16)
                    away_outs[k][part : part + per_block, :] = jnp.where(mask, first, second).astype(BF16)


def local(queries, key_rows, value_rows, out_grad, documents, swapped):
    ranks = lax.axis_size("ctx")
    hops = ranks // 4
    count = hops + 1
    slots = 2 * count
    rows, width = key_rows.shape[1:]
    keys = slots * rows
    size = 2 * rows + META
    queries, out_grad = queries[0], out_grad[0]

    def up(block, k):
        return lax.ppermute(block, "ctx", [(i, i + 2 * k) for i in range(ranks - 2 * k)])

    def down(block, k):
        return lax.ppermute(block, "ctx", [(i + 2 * k, i) for i in range(ranks - 2 * k)])

    def to_partner(block):
        return lax.ppermute(block, "half", [(0, 1), (1, 0)])

    def to_side(block):
        return lax.ppermute(block, "ctx", [(i, i ^ 1) for i in range(ranks)])

    payload, payload_side = pl.pallas_call(
        payload_kernel,
        out_shape=[pltpu.VMEM((size, HEAD_SIZE), BF16)] * 2,
        in_specs=[SMEM, VMEM, VMEM, VMEM],
        out_specs=[VMEM, VMEM],
    )(swapped[0, 0], key_rows[0], value_rows[0], documents)
    from_side = to_side(payload_side)

    def rows_of(other, queries, out_grad):
        return pl.pallas_call(
            functools.partial(rows_kernel, other),
            out_shape=pltpu.VMEM((2 * rows, HALF), BF16),
            in_specs=[HBM, HBM],
            out_specs=VMEM,
            scratch_shapes=[pltpu.SemaphoreType.DMA((2,))],
        )(queries, out_grad)

    both = jnp.concatenate([payload, from_side], axis=0)
    rows_side = rows_of(True, queries, out_grad)
    both, rows_side = lax.optimization_barrier((both, rows_side))
    rows_got = to_side(rows_side)
    home = [both] + [up(both, k) for k in range(1, count)]
    away = [to_partner(block) for block in home]
    *early, home[hops], queries, out_grad = lax.optimization_barrier(
        (*home[:hops], *away[:hops], home[hops], queries, out_grad)
    )
    rows_all = jnp.concatenate([rows_of(False, queries, out_grad), rows_got], axis=0)
    ready = pl.pallas_call(
        functools.partial(prepare_kernel, hops),
        out_shape=[pltpu.VMEM((2, 2 * rows * hops, HEAD_SIZE), BF16)] * 2
        + [pltpu.VMEM((2, HEAD_SIZE, 2 * rows * hops), BF16)] * 2,
        in_specs=[VMEM] * (2 * hops),
        out_specs=[VMEM] * 4,
        cost_estimate=pl.CostEstimate(flops=0, bytes_accessed=4 * 1024 * 1024, transcendentals=0),
    )(*early)
    chunk = pltpu.VMEM((4 * rows, HEAD_SIZE), BF16)
    outs = pl.pallas_call(
        functools.partial(attention_kernel, hops),
        out_shape=[pltpu.VMEM((4 * rows, HALF), BF16)] + [chunk] * (2 * count),
        in_specs=[VMEM] * (5 + 2 * count),
        out_specs=[VMEM] * (1 + 2 * count),
        scratch_shapes=[
            pltpu.VMEM((2, keys, HEAD_SIZE), BF16),
            pltpu.VMEM((2, keys, HEAD_SIZE), BF16),
            pltpu.VMEM((2, HEAD_SIZE, keys), BF16),
            pltpu.VMEM((2, HEAD_SIZE, keys), BF16),
            pltpu.VMEM((2, 16, rows), F32),
            pltpu.VMEM((2, 8, rows), I32),
            pltpu.VMEM((8, rows), F32),
            pltpu.VMEM((2, keys, HEAD_SIZE), F32),
            pltpu.VMEM((2, keys, HEAD_SIZE), F32),
            pltpu.SMEM((2 * NBLK,), I32),
            pltpu.SMEM((2 * NBLK,), I32),
        ],
        compiler_params=pltpu.CompilerParams(vmem_limit_bytes=40 * 1024 * 1024),
        cost_estimate=pl.CostEstimate(
            flops=12 * rows * keys * 2048,
            bytes_accessed=4 * 1024 * 1024,
            transcendentals=rows * keys * 16,
        ),
    )(rows_all, *home, *away, *ready)
    home_sum, away_sum = outs[1 : 1 + count], outs[1 + count :]
    side_out = outs[0][2 * rows :]
    out, query_grad = pl.pallas_call(
        own_kernel,
        out_shape=[jax.ShapeDtypeStruct(queries.shape, BF16)] * 2,
        in_specs=[VMEM],
        out_specs=[HBM] * 2,
        scratch_shapes=[pltpu.SemaphoreType.DMA((2,))],
        cost_estimate=pl.CostEstimate(flops=0, bytes_accessed=4 * 1024 * 1024, transcendentals=0),
    )(outs[0])

    parts = []
    for k in reversed(range(count)):
        crossed = to_partner(away_sum[k])
        if k == hops:
            crossed, out, query_grad = lax.optimization_barrier((crossed, out, query_grad))
        part = home_sum[k].astype(F32) + crossed.astype(F32)
        if k:
            part = part.astype(BF16)
            part = down(part, k)
        parts.append(part)
    out_got = to_side(side_out)
    out, query_grad = pl.pallas_call(
        finish_kernel,
        out_shape=[jax.ShapeDtypeStruct(queries.shape, BF16)] * 2,
        in_specs=[VMEM, HBM, HBM],
        out_specs=[HBM] * 2,
        input_output_aliases={1: 0, 2: 1},
        scratch_shapes=[pltpu.SemaphoreType.DMA((2,))],
    )(out_got, out, query_grad)
    parts[0], out, query_grad = lax.optimization_barrier((parts[0], out, query_grad))
    total = sum(part.astype(F32) for part in parts).astype(BF16)
    grads_got = to_side(total[2 * rows :])
    grads = total[: 2 * rows]
    first = core_index() == 0
    grads = jnp.concatenate(
        [jnp.where(first, grads, grads_got), jnp.where(first, grads_got, grads)], axis=1
    )
    return (out[None], query_grad[None], grads[None, :rows], grads[None, rows:])


def solution(mesh):
    groups, ranks = mesh.devices.shape
    wide = Mesh(mesh.devices.reshape(2, groups // 2, ranks), ("half", "pair", "ctx"))
    spec3 = P(("half", "pair"), "ctx", None)
    in_specs = (spec3, spec3, spec3, spec3, P(("half", "pair"), "ctx"), spec3)
    return jax.shard_map(
        local, mesh=wide, in_specs=in_specs, out_specs=(spec3,) * 4, check_vma=False
    )
```

```python
import functools
import math

import jax
import jax.numpy as jnp
from jax import lax
from jax.experimental import pallas as pl
from jax.experimental.pallas import tpu as pltpu
from jax.sharding import Mesh
from jax.sharding import PartitionSpec as P

HEAD_SIZE = 128
QUERY_PER_KEY = 8
NBLK = 4
META = 16
DOC_ROW = NBLK
DOC_VALUES = 16
GROUPED = 4
HALF = QUERY_PER_KEY * HEAD_SIZE
NEG = -1e30
F32, BF16, I32 = jnp.float32, jnp.bfloat16, jnp.int32
NT = (((1,), (1,)), ((), ()))
VMEM = pl.BlockSpec(memory_space=pltpu.VMEM)
SMEM = pl.BlockSpec(memory_space=pltpu.SMEM)
HBM = pl.BlockSpec(memory_space=pltpu.HBM)
SMALL = pltpu.CompilerParams(vmem_limit_bytes=8 * 1024 * 1024)


def core_index():
    return lax.rem(lax.axis_index("ctx"), 2)


def payload_kernel(swap_ref, key_ref, value_ref, docs_ref, own_ref, side_ref):
    rows = key_ref.shape[0]
    core = core_index()
    docs = jnp.broadcast_to(docs_ref[...].astype(F32), (META, rows))
    place = lax.broadcasted_iota(I32, docs.shape, 0)
    meta = jnp.where(place == DOC_ROW, docs, 0.0)
    for block in range(NBLK):
        meta = jnp.where(place == block, swap_ref[block].astype(F32), meta)
    meta = meta.astype(BF16)
    for ref, head in ((own_ref, core), (side_ref, 1 - core)):
        lane = pl.ds(pl.multiple_of(head * HEAD_SIZE, HEAD_SIZE), HEAD_SIZE)
        ref[:rows, :] = key_ref[:, lane]
        ref[rows : 2 * rows, :] = value_ref[:, lane]
        ref[2 * rows :, :] = meta


def rows_kernel(other, query_ref, grad_ref, rows_ref, sems):
    rows = query_ref.shape[0]
    core = core_index()
    head = 1 - core if other else core
    lanes = pl.ds(pl.multiple_of(head * HALF, HALF), HALF)
    copies = [
        pltpu.make_async_copy(
            source.at[:, lanes], rows_ref.at[pl.ds(part * rows, rows), :], sems.at[part]
        )
        for part, source in enumerate((query_ref, grad_ref))
    ]
    for copy in copies:
        copy.start()
    for copy in copies:
        copy.wait()


def write_heads(source_ref, head, out_ref, query_grad_ref, sems):
    rows = out_ref.shape[0]
    lanes = pl.ds(pl.multiple_of(head * HALF, HALF), HALF)
    copies = [
        pltpu.make_async_copy(
            source_ref.at[pl.ds(part * rows, rows), :], target.at[:, lanes], sems.at[part]
        )
        for part, target in enumerate((out_ref, query_grad_ref))
    ]
    for copy in copies:
        copy.start()
    for copy in copies:
        copy.wait()


def own_kernel(own_ref, out_ref, query_grad_ref, sems):
    write_heads(own_ref, core_index(), out_ref, query_grad_ref, sems)


def finish_kernel(side_ref, out_held, query_grad_held, out_ref, query_grad_ref, sems):
    write_heads(side_ref, 1 - core_index(), out_ref, query_grad_ref, sems)


def merge_hop(home, away, slots_at, rows, logs):
    key_log, value_log, key_turned, value_turned = logs
    per_block = rows // NBLK
    size = 2 * rows + META
    for who in range(2):
        base = pl.multiple_of(slots_at[who] * rows, rows)
        flags = home[who * size + 2 * rows : (who + 1) * size, :].astype(F32)
        for which, log, turned in ((0, key_log, key_turned), (1, value_log, value_turned)):
            merged = ([], [])
            for block in range(NBLK):
                mask = (
                    jnp.broadcast_to(flags[block : block + 1, :], (per_block, HEAD_SIZE)).astype(BF16)
                    > 0.5
                )
                first = who * size + which * rows + block * per_block
                own = home[first : first + per_block, :]
                other = away[first : first + per_block, :]
                merged[0].append(jnp.where(mask, other, own))
                merged[1].append(jnp.where(mask, own, other))
            for logical in range(2):
                whole = jnp.concatenate(merged[logical], axis=0)
                log[logical, pl.ds(base, rows), :] = whole
                turned[logical, :, pl.ds(base, rows)] = whole.T


def prepare_kernel(hops, *refs):
    homes, aways = refs[:hops], refs[hops : 2 * hops]
    logs = refs[2 * hops :]
    rows = (homes[0].shape[0] // 2 - META) // 2
    core = core_index()
    parity = (core, 1 - core)
    for k in range(hops):
        slots_at = [2 * (hops - 1 - k) + parity[who] for who in range(2)]
        merge_hop(homes[k], aways[k], slots_at, rows, logs)


def attention_kernel(hops, rows_ref, *refs):
    count = hops + 1
    slots = 2 * count
    window = slots - 1
    homes, aways = refs[:count], refs[count : 2 * count]
    ready = refs[2 * count : 2 * count + 4]
    out_all = refs[2 * count + 4]
    home_outs = refs[2 * count + 5 : 3 * count + 5]
    away_outs = refs[3 * count + 5 : 4 * count + 5]
    (
        key_log,
        value_log,
        key_turned,
        value_turned,
        doc_window,
        starts,
        flag_rows,
        key_total,
        value_total,
        logical_of,
        needed_of,
    ) = refs[4 * count + 5 :]
    rows = rows_ref.shape[0] // 4
    per_block = rows // NBLK
    lanes = QUERY_PER_KEY * per_block
    size = 2 * rows + META
    core = core_index()
    chip = lax.axis_index("ctx") // 2
    parity = (core, 1 - core)
    scale = 1.0 / math.sqrt(HEAD_SIZE)
    factor = scale * math.log2(math.e)

    key_total[...] = jnp.zeros_like(key_total)
    value_total[...] = jnp.zeros_like(value_total)
    doc_window[...] = jnp.full_like(doc_window, 1e4)

    def meta_of(ref, who):
        return ref[who * size + 2 * rows : (who + 1) * size, :].astype(F32)

    for k in range(count):
        for who in range(2):
            slot = 2 * (hops - k) + parity[who]
            base = pl.multiple_of(slot * rows, rows)
            for logical, ref in ((0, homes[k]), (1, aways[k])):
                docs = meta_of(ref, who)[DOC_ROW : DOC_ROW + 1, :]
                doc_window[logical, pl.ds(slot, 1), :] = jnp.where(chip >= k, docs, -1.0)
    logs = (key_log, value_log, key_turned, value_turned)
    for log, held in zip(logs[:2], ready[:2]):
        log[:, pl.ds(2 * rows, 2 * rows * hops), :] = held[...]
    for log, held in zip(logs[2:], ready[2:]):
        log[:, :, pl.ds(2 * rows, 2 * rows * hops)] = held[...]
    merge_hop(homes[hops], aways[hops], parity, rows, logs)

    values_down = lax.broadcasted_iota(I32, (DOC_VALUES, rows), 0).astype(F32)
    group = lax.broadcasted_iota(I32, (8, rows), 1) // per_block
    meta_rows = [meta_of(homes[0], who) for who in range(2)]
    for logical in range(2):
        lower = jnp.zeros((DOC_VALUES, rows), F32)
        for slot in range(slots):
            docs = jnp.broadcast_to(doc_window[logical, slot : slot + 1, :], lower.shape)
            lower = lower + jnp.where(docs < values_down, 1.0, 0.0)
        lower = jnp.broadcast_to(jnp.sum(lower, axis=1, keepdims=True), lower.shape)
        for who in range(2):
            docs = meta_of((homes, aways)[logical][0], who)[DOC_ROW : DOC_ROW + 1, :]
            docs = jnp.broadcast_to(docs, (8, rows))
            turns = [docs] + [pltpu.roll(docs, t * per_block, 1) for t in range(1, NBLK)]
            for block in range(NBLK):
                tiled = turns[0]
                for t in range(1, NBLK):
                    tiled = jnp.where(group == (block + t) % NBLK, turns[t], tiled)
                tiled = jnp.broadcast_to(tiled[:1], lower.shape)
                start = jnp.sum(jnp.where(tiled == values_down, lower, 0.0), axis=0, keepdims=True)
                starts[logical, who * NBLK + block : who * NBLK + block + 1, :] = start.astype(I32)
    for who in range(2):
        flag_rows[who * NBLK : (who + 1) * NBLK, :] = meta_rows[who][:NBLK, :]
    flags = flag_rows[...]
    firsts = [
        jnp.broadcast_to(
            jnp.min(starts[logical].astype(F32), axis=1, keepdims=True), flags.shape
        )
        for logical in range(2)
    ]
    first = jnp.where(flags > 0.5, firsts[1], firsts[0]).astype(I32)
    flags = flags.astype(I32)
    for unit_index in range(2 * NBLK):
        logical_of[unit_index] = flags[unit_index, 0]
        needed_of[unit_index] = window + parity[unit_index // NBLK] - first[unit_index, 0] // rows

    def unit(unit_index, chunks):
        who, block = unit_index // NBLK, lax.rem(unit_index, NBLK)
        logical = logical_of[unit_index]
        row_parity = jnp.where(who == 0, core, 1 - core)
        first_slot = window + row_parity - chunks
        first = pl.multiple_of(first_slot * rows, rows)
        span = pl.ds(first, chunks * rows)
        columns = [slice(h * HEAD_SIZE, (h + 1) * HEAD_SIZE) for h in range(QUERY_PER_KEY)]
        query_at = pl.ds(pl.multiple_of(2 * who * rows + block * per_block, per_block), per_block)
        grad_at = pl.ds(
            pl.multiple_of((2 * who + 1) * rows + block * per_block, per_block), per_block
        )
        query = jnp.concatenate([rows_ref[query_at, column] for column in columns], axis=0)
        grad = jnp.concatenate([rows_ref[grad_at, column] for column in columns], axis=0)
        scores = lax.dot_general(key_log[logical, span, :], query, NT, preferred_element_type=F32)
        shape = (chunks * rows, HEAD_SIZE)
        key_place = lax.broadcasted_iota(I32, shape, 0)
        row_first = starts[logical, pl.ds(unit_index, 1), :] - first
        row_last = (
            (chunks - 1) * rows
            + block * per_block
            + lax.rem(lax.broadcasted_iota(I32, (1, HEAD_SIZE), 1), per_block)
        )
        allowed = (key_place >= row_first) & (key_place <= row_last)
        scores = jnp.concatenate(
            [
                jnp.where(allowed, scores[:, lane : lane + HEAD_SIZE], NEG)
                for lane in range(0, lanes, HEAD_SIZE)
            ],
            axis=1,
        )
        peak = jnp.max(scores, axis=0, keepdims=True)
        powers = jnp.exp2((scores - peak) * factor)
        inverse = 1.0 / jnp.sum(powers, axis=0, keepdims=True)
        probs = powers * inverse
        weights = probs.astype(BF16)
        out_turned = jnp.dot(
            value_turned[logical, :, span], weights, preferred_element_type=F32
        ).astype(BF16)
        delta = jnp.sum(grad.T.astype(F32) * out_turned.astype(F32), axis=0, keepdims=True)
        prob_grad = lax.dot_general(
            value_log[logical, span, :], grad, NT, preferred_element_type=F32
        )
        score_grad = (probs * (prob_grad - delta)).astype(BF16)
        query_grad_turned = jnp.dot(
            key_turned[logical, :, span], score_grad, preferred_element_type=F32
        )
        key_add = jnp.dot(score_grad, query, preferred_element_type=F32)
        value_add = jnp.dot(weights, grad, preferred_element_type=F32)
        out = out_turned.T
        query_grad = (query_grad_turned * scale).astype(BF16).T
        return query_at, grad_at, logical, span, out, query_grad, key_add, value_add

    def step(pair, carry):
        members = [pair * GROUPED + m for m in range(GROUPED)]
        needed = needed_of[members[0]]
        for member in members[1:]:
            needed = jnp.maximum(needed, needed_of[member])
        for chunks in range(1, window + 1):

            @pl.when(needed == chunks)
            def _(chunks=chunks):
                results = [unit(member, chunks) for member in members]
                for query_at, grad_at, logical, span, out, query_grad, key_add, value_add in results:
                    key_total[logical, span, :] += key_add
                    value_total[logical, span, :] += value_add
                    for h in range(QUERY_PER_KEY):
                        column = slice(h * HEAD_SIZE, (h + 1) * HEAD_SIZE)
                        part = slice(h * per_block, (h + 1) * per_block)
                        out_all[query_at, column] = out[part, :]
                        out_all[grad_at, column] = query_grad[part, :]

        return carry

    lax.fori_loop(0, 2 * NBLK // GROUPED, step, 0)
    for k in range(count):
        for who in range(2):
            base = pl.multiple_of((2 * (hops - k) + parity[who]) * rows, rows)
            flags = meta_of(homes[k], who)
            for block in range(NBLK):
                at = pl.ds(base + block * per_block, per_block)
                mask = jnp.broadcast_to(flags[block : block + 1, :], (per_block, HEAD_SIZE)) > 0.5
                for which, total, gain in ((0, key_total, scale), (1, value_total, 1.0)):
                    part = (2 * who + which) * rows + block * per_block
                    first = total[0, at, :] * gain
                    second = total[1, at, :] * gain
                    home_outs[k][part : part + per_block, :] = jnp.where(mask, second, first).astype(BF16)
                    away_outs[k][part : part + per_block, :] = jnp.where(mask, first, second).astype(BF16)


def local(queries, key_rows, value_rows, out_grad, documents, swapped):
    ranks = lax.axis_size("ctx")
    hops = ranks // 4
    count = hops + 1
    slots = 2 * count
    rows, width = key_rows.shape[1:]
    keys = slots * rows
    size = 2 * rows + META
    queries, out_grad = queries[0], out_grad[0]

    def up(block, k):
        return lax.ppermute(block, "ctx", [(i, i + 2 * k) for i in range(ranks - 2 * k)])

    def down(block, k):
        return lax.ppermute(block, "ctx", [(i + 2 * k, i) for i in range(ranks - 2 * k)])

    def to_partner(block):
        return lax.ppermute(block, "half", [(0, 1), (1, 0)])

    def to_side(block):
        return lax.ppermute(block, "ctx", [(i, i ^ 1) for i in range(ranks)])

    payload, payload_side = pl.pallas_call(
        payload_kernel,
        out_shape=[pltpu.VMEM((size, HEAD_SIZE), BF16)] * 2,
        in_specs=[SMEM, VMEM, VMEM, VMEM],
        out_specs=[VMEM, VMEM],
        compiler_params=SMALL,
    )(swapped[0, 0], key_rows[0], value_rows[0], documents)
    from_side = to_side(payload_side)

    def rows_of(other, queries, out_grad):
        return pl.pallas_call(
            functools.partial(rows_kernel, other),
            out_shape=pltpu.VMEM((2 * rows, HALF), BF16),
            in_specs=[HBM, HBM],
            out_specs=VMEM,
            scratch_shapes=[pltpu.SemaphoreType.DMA((2,))],
            compiler_params=SMALL,
        )(queries, out_grad)

    both = jnp.concatenate([payload, from_side], axis=0)
    rows_side = rows_of(True, queries, out_grad)
    both, rows_side = lax.optimization_barrier((both, rows_side))
    rows_got = to_side(rows_side)
    home = [both] + [up(both, k) for k in range(1, count)]
    away = [to_partner(block) for block in home]
    *early, home[hops], queries, out_grad = lax.optimization_barrier(
        (*home[:hops], *away[:hops], home[hops], queries, out_grad)
    )
    rows_all = jnp.concatenate([rows_of(False, queries, out_grad), rows_got], axis=0)
    ready = pl.pallas_call(
        functools.partial(prepare_kernel, hops),
        out_shape=[pltpu.VMEM((2, 2 * rows * hops, HEAD_SIZE), BF16)] * 2
        + [pltpu.VMEM((2, HEAD_SIZE, 2 * rows * hops), BF16)] * 2,
        in_specs=[VMEM] * (2 * hops),
        out_specs=[VMEM] * 4,
        compiler_params=SMALL,
        cost_estimate=pl.CostEstimate(flops=0, bytes_accessed=4 * 1024 * 1024, transcendentals=0),
    )(*early)
    chunk = pltpu.VMEM((4 * rows, HEAD_SIZE), BF16)
    outs = pl.pallas_call(
        functools.partial(attention_kernel, hops),
        out_shape=[pltpu.VMEM((4 * rows, HALF), BF16)] + [chunk] * (2 * count),
        in_specs=[VMEM] * (5 + 2 * count),
        out_specs=[VMEM] * (1 + 2 * count),
        scratch_shapes=[
            pltpu.VMEM((2, keys, HEAD_SIZE), BF16),
            pltpu.VMEM((2, keys, HEAD_SIZE), BF16),
            pltpu.VMEM((2, HEAD_SIZE, keys), BF16),
            pltpu.VMEM((2, HEAD_SIZE, keys), BF16),
            pltpu.VMEM((2, 16, rows), F32),
            pltpu.VMEM((2, 8, rows), I32),
            pltpu.VMEM((8, rows), F32),
            pltpu.VMEM((2, keys, HEAD_SIZE), F32),
            pltpu.VMEM((2, keys, HEAD_SIZE), F32),
            pltpu.SMEM((2 * NBLK,), I32),
            pltpu.SMEM((2 * NBLK,), I32),
        ],
        compiler_params=pltpu.CompilerParams(vmem_limit_bytes=32 * 1024 * 1024),
        cost_estimate=pl.CostEstimate(
            flops=12 * rows * keys * 2048,
            bytes_accessed=4 * 1024 * 1024,
            transcendentals=rows * keys * 16,
        ),
    )(rows_all, *home, *away, *ready)
    home_sum, away_sum = outs[1 : 1 + count], outs[1 + count :]
    side_out = outs[0][2 * rows :]
    out, query_grad = pl.pallas_call(
        own_kernel,
        out_shape=[jax.ShapeDtypeStruct(queries.shape, BF16)] * 2,
        in_specs=[VMEM],
        out_specs=[HBM] * 2,
        compiler_params=SMALL,
        scratch_shapes=[pltpu.SemaphoreType.DMA((2,))],
        cost_estimate=pl.CostEstimate(flops=0, bytes_accessed=4 * 1024 * 1024, transcendentals=0),
    )(outs[0])

    parts = []
    for k in reversed(range(count)):
        crossed = to_partner(away_sum[k])
        part = home_sum[k].astype(F32) + crossed.astype(F32)
        if k:
            part = part.astype(BF16)
            part = down(part, k)
        parts.append(part)
    out_got = to_side(side_out)
    out, query_grad = pl.pallas_call(
        finish_kernel,
        out_shape=[jax.ShapeDtypeStruct(queries.shape, BF16)] * 2,
        in_specs=[VMEM, HBM, HBM],
        out_specs=[HBM] * 2,
        compiler_params=SMALL,
        input_output_aliases={1: 0, 2: 1},
        scratch_shapes=[pltpu.SemaphoreType.DMA((2,))],
    )(out_got, out, query_grad)
    parts[0], out, query_grad = lax.optimization_barrier((parts[0], out, query_grad))
    total = sum(part.astype(F32) for part in parts).astype(BF16)
    grads_got = to_side(total[2 * rows :])
    grads = total[: 2 * rows]
    first = core_index() == 0
    grads = jnp.concatenate(
        [jnp.where(first, grads, grads_got), jnp.where(first, grads_got, grads)], axis=1
    )
    return (out[None], query_grad[None], grads[None, :rows], grads[None, rows:])


def solution(mesh):
    groups, ranks = mesh.devices.shape
    wide = Mesh(mesh.devices.reshape(2, groups // 2, ranks), ("half", "pair", "ctx"))
    spec3 = P(("half", "pair"), "ctx", None)
    in_specs = (spec3, spec3, spec3, spec3, P(("half", "pair"), "ctx"), spec3)
    return jax.shard_map(
        local, mesh=wide, in_specs=in_specs, out_specs=(spec3,) * 4, check_vma=False
    )
```

```python
import functools
import math

import jax
import jax.numpy as jnp
from jax import lax
from jax.experimental import pallas as pl
from jax.experimental.pallas import tpu as pltpu
from jax.sharding import Mesh
from jax.sharding import PartitionSpec as P

HEAD_SIZE = 128
QUERY_PER_KEY = 8
NBLK = 4
META = 16
DOC_ROW = NBLK
DOC_VALUES = 16
GROUPED = 4
HALF = QUERY_PER_KEY * HEAD_SIZE
NEG = -1e30
F32, BF16, I32 = jnp.float32, jnp.bfloat16, jnp.int32
NT = (((1,), (1,)), ((), ()))
VMEM = pl.BlockSpec(memory_space=pltpu.VMEM)
SMEM = pl.BlockSpec(memory_space=pltpu.SMEM)
HBM = pl.BlockSpec(memory_space=pltpu.HBM)
SMALL = pltpu.CompilerParams(vmem_limit_bytes=8 * 1024 * 1024)


def core_index():
    return lax.rem(lax.axis_index("ctx"), 2)


def payload_kernel(swap_ref, key_ref, value_ref, docs_ref, own_ref, side_ref):
    rows = key_ref.shape[0]
    core = core_index()
    docs = jnp.broadcast_to(docs_ref[...].astype(F32), (META, rows))
    place = lax.broadcasted_iota(I32, docs.shape, 0)
    meta = jnp.where(place == DOC_ROW, docs, 0.0)
    for block in range(NBLK):
        meta = jnp.where(place == block, swap_ref[block].astype(F32), meta)
    meta = meta.astype(BF16)
    for ref, head in ((own_ref, core), (side_ref, 1 - core)):
        lane = pl.ds(pl.multiple_of(head * HEAD_SIZE, HEAD_SIZE), HEAD_SIZE)
        ref[:rows, :] = key_ref[:, lane]
        ref[rows : 2 * rows, :] = value_ref[:, lane]
        ref[2 * rows :, :] = meta


def rows_kernel(other, query_ref, grad_ref, rows_ref, sems):
    rows = query_ref.shape[0]
    core = core_index()
    head = 1 - core if other else core
    lanes = pl.ds(pl.multiple_of(head * HALF, HALF), HALF)
    copies = [
        pltpu.make_async_copy(
            source.at[:, lanes], rows_ref.at[pl.ds(part * rows, rows), :], sems.at[part]
        )
        for part, source in enumerate((query_ref, grad_ref))
    ]
    for copy in copies:
        copy.start()
    for copy in copies:
        copy.wait()


def write_heads(source_ref, head, out_ref, query_grad_ref, sems):
    rows = out_ref.shape[0]
    lanes = pl.ds(pl.multiple_of(head * HALF, HALF), HALF)
    copies = [
        pltpu.make_async_copy(
            source_ref.at[pl.ds(part * rows, rows), :], target.at[:, lanes], sems.at[part]
        )
        for part, target in enumerate((out_ref, query_grad_ref))
    ]
    for copy in copies:
        copy.start()
    for copy in copies:
        copy.wait()


def own_kernel(own_ref, out_ref, query_grad_ref, sems):
    write_heads(own_ref, core_index(), out_ref, query_grad_ref, sems)


def finish_kernel(side_ref, out_held, query_grad_held, out_ref, query_grad_ref, sems):
    write_heads(side_ref, 1 - core_index(), out_ref, query_grad_ref, sems)


def merge_hop(home, away, slots_at, rows, logs):
    key_log, value_log, key_turned, value_turned = logs
    per_block = rows // NBLK
    size = 2 * rows + META
    for who in range(2):
        base = pl.multiple_of(slots_at[who] * rows, rows)
        flags = home[who * size + 2 * rows : (who + 1) * size, :].astype(F32)
        for which, log, turned in ((0, key_log, key_turned), (1, value_log, value_turned)):
            merged = ([], [])
            for block in range(NBLK):
                mask = (
                    jnp.broadcast_to(flags[block : block + 1, :], (per_block, HEAD_SIZE)).astype(BF16)
                    > 0.5
                )
                first = who * size + which * rows + block * per_block
                own = home[first : first + per_block, :]
                other = away[first : first + per_block, :]
                merged[0].append(jnp.where(mask, other, own))
                merged[1].append(jnp.where(mask, own, other))
            for logical in range(2):
                whole = jnp.concatenate(merged[logical], axis=0)
                log[logical, pl.ds(base, rows), :] = whole
                turned[logical, :, pl.ds(base, rows)] = whole.T


def prepare_kernel(hops, *refs):
    homes, aways = refs[:hops], refs[hops : 2 * hops]
    logs = refs[2 * hops :]
    rows = (homes[0].shape[0] // 2 - META) // 2
    core = core_index()
    parity = (core, 1 - core)
    for k in range(hops):
        slots_at = [2 * (hops - 1 - k) + parity[who] for who in range(2)]
        merge_hop(homes[k], aways[k], slots_at, rows, logs)


def attention_kernel(hops, rows_ref, *refs):
    count = hops + 1
    slots = 2 * count
    window = slots - 1
    homes, aways = refs[:count], refs[count : 2 * count]
    ready = refs[2 * count : 2 * count + 4]
    out_all = refs[2 * count + 4]
    home_outs = refs[2 * count + 5 : 3 * count + 5]
    away_outs = refs[3 * count + 5 : 4 * count + 5]
    (
        key_log,
        value_log,
        key_turned,
        value_turned,
        doc_window,
        starts,
        flag_rows,
        key_total,
        value_total,
        logical_of,
        needed_of,
    ) = refs[4 * count + 5 :]
    rows = rows_ref.shape[0] // 4
    per_block = rows // NBLK
    lanes = QUERY_PER_KEY * per_block
    size = 2 * rows + META
    core = core_index()
    chip = lax.axis_index("ctx") // 2
    parity = (core, 1 - core)
    scale = 1.0 / math.sqrt(HEAD_SIZE)
    factor = scale * math.log2(math.e)

    key_total[...] = jnp.zeros_like(key_total)
    value_total[...] = jnp.zeros_like(value_total)
    doc_window[...] = jnp.full_like(doc_window, 1e4)

    def meta_of(ref, who):
        return ref[who * size + 2 * rows : (who + 1) * size, :].astype(F32)

    for k in range(count):
        for who in range(2):
            slot = 2 * (hops - k) + parity[who]
            base = pl.multiple_of(slot * rows, rows)
            for logical, ref in ((0, homes[k]), (1, aways[k])):
                docs = meta_of(ref, who)[DOC_ROW : DOC_ROW + 1, :]
                doc_window[logical, pl.ds(slot, 1), :] = jnp.where(chip >= k, docs, -1.0)
    logs = (key_log, value_log, key_turned, value_turned)
    for log, held in zip(logs[:2], ready[:2]):
        log[:, pl.ds(2 * rows, 2 * rows * hops), :] = held[...]
    for log, held in zip(logs[2:], ready[2:]):
        log[:, :, pl.ds(2 * rows, 2 * rows * hops)] = held[...]
    merge_hop(homes[hops], aways[hops], parity, rows, logs)

    values_down = lax.broadcasted_iota(I32, (DOC_VALUES, rows), 0).astype(F32)
    group = lax.broadcasted_iota(I32, (8, rows), 1) // per_block
    meta_rows = [meta_of(homes[0], who) for who in range(2)]
    for logical in range(2):
        lower = jnp.zeros((DOC_VALUES, rows), F32)
        for slot in range(slots):
            docs = jnp.broadcast_to(doc_window[logical, slot : slot + 1, :], lower.shape)
            lower = lower + jnp.where(docs < values_down, 1.0, 0.0)
        lower = jnp.broadcast_to(jnp.sum(lower, axis=1, keepdims=True), lower.shape)
        for who in range(2):
            docs = meta_of((homes, aways)[logical][0], who)[DOC_ROW : DOC_ROW + 1, :]
            docs = jnp.broadcast_to(docs, (8, rows))
            turns = [docs] + [pltpu.roll(docs, t * per_block, 1) for t in range(1, NBLK)]
            for block in range(NBLK):
                tiled = turns[0]
                for t in range(1, NBLK):
                    tiled = jnp.where(group == (block + t) % NBLK, turns[t], tiled)
                tiled = jnp.broadcast_to(tiled[:1], lower.shape)
                start = jnp.sum(jnp.where(tiled == values_down, lower, 0.0), axis=0, keepdims=True)
                starts[logical, who * NBLK + block : who * NBLK + block + 1, :] = start.astype(I32)
    for who in range(2):
        flag_rows[who * NBLK : (who + 1) * NBLK, :] = meta_rows[who][:NBLK, :]
    flags = flag_rows[...]
    firsts = [
        jnp.broadcast_to(
            jnp.min(starts[logical].astype(F32), axis=1, keepdims=True), flags.shape
        )
        for logical in range(2)
    ]
    first = jnp.where(flags > 0.5, firsts[1], firsts[0]).astype(I32)
    flags = flags.astype(I32)
    for unit_index in range(2 * NBLK):
        logical_of[unit_index] = flags[unit_index, 0]
        needed_of[unit_index] = window + parity[unit_index // NBLK] - first[unit_index, 0] // rows

    def unit(unit_index, chunks):
        who, block = unit_index // NBLK, lax.rem(unit_index, NBLK)
        logical = logical_of[unit_index]
        row_parity = jnp.where(who == 0, core, 1 - core)
        first_slot = window + row_parity - chunks
        first = pl.multiple_of(first_slot * rows, rows)
        span = pl.ds(first, chunks * rows)
        columns = [slice(h * HEAD_SIZE, (h + 1) * HEAD_SIZE) for h in range(QUERY_PER_KEY)]
        query_at = pl.ds(pl.multiple_of(2 * who * rows + block * per_block, per_block), per_block)
        grad_at = pl.ds(
            pl.multiple_of((2 * who + 1) * rows + block * per_block, per_block), per_block
        )
        query = jnp.concatenate([rows_ref[query_at, column] for column in columns], axis=0)
        grad = jnp.concatenate([rows_ref[grad_at, column] for column in columns], axis=0)
        scores = lax.dot_general(key_log[logical, span, :], query, NT, preferred_element_type=F32)
        shape = (chunks * rows, HEAD_SIZE)
        key_place = lax.broadcasted_iota(I32, shape, 0)
        row_first = starts[logical, pl.ds(unit_index, 1), :] - first
        row_last = (
            (chunks - 1) * rows
            + block * per_block
            + lax.rem(lax.broadcasted_iota(I32, (1, HEAD_SIZE), 1), per_block)
        )
        allowed = (key_place >= row_first) & (key_place <= row_last)
        scores = jnp.concatenate(
            [
                jnp.where(allowed, scores[:, lane : lane + HEAD_SIZE], NEG)
                for lane in range(0, lanes, HEAD_SIZE)
            ],
            axis=1,
        )
        peak = jnp.max(scores, axis=0, keepdims=True)
        powers = jnp.exp2((scores - peak) * factor)
        inverse = 1.0 / jnp.sum(powers, axis=0, keepdims=True)
        probs = powers * inverse
        weights = probs.astype(BF16)
        out_turned = jnp.dot(
            value_turned[logical, :, span], weights, preferred_element_type=F32
        ).astype(BF16)
        delta = jnp.sum(grad.T.astype(F32) * out_turned.astype(F32), axis=0, keepdims=True)
        prob_grad = lax.dot_general(
            value_log[logical, span, :], grad, NT, preferred_element_type=F32
        )
        score_grad = (probs * (prob_grad - delta)).astype(BF16)
        query_grad_turned = jnp.dot(
            key_turned[logical, :, span], score_grad, preferred_element_type=F32
        )
        key_add = jnp.dot(score_grad, query, preferred_element_type=F32)
        value_add = jnp.dot(weights, grad, preferred_element_type=F32)
        out = out_turned.T
        query_grad = (query_grad_turned * scale).astype(BF16).T
        return query_at, grad_at, logical, span, out, query_grad, key_add, value_add

    def step(pair, carry):
        members = [pair * GROUPED + m for m in range(GROUPED)]
        needed = needed_of[members[0]]
        for member in members[1:]:
            needed = jnp.maximum(needed, needed_of[member])
        for chunks in range(1, window + 1):

            @pl.when(needed == chunks)
            def _(chunks=chunks):
                results = [unit(member, chunks) for member in members]
                for query_at, grad_at, logical, span, out, query_grad, key_add, value_add in results:
                    key_total[logical, span, :] += key_add
                    value_total[logical, span, :] += value_add
                    for h in range(QUERY_PER_KEY):
                        column = slice(h * HEAD_SIZE, (h + 1) * HEAD_SIZE)
                        part = slice(h * per_block, (h + 1) * per_block)
                        out_all[query_at, column] = out[part, :]
                        out_all[grad_at, column] = query_grad[part, :]

        return carry

    lax.fori_loop(0, 2 * NBLK // GROUPED, step, 0)
    for k in range(count):
        for who in range(2):
            base = pl.multiple_of((2 * (hops - k) + parity[who]) * rows, rows)
            flags = meta_of(homes[k], who)
            for block in range(NBLK):
                at = pl.ds(base + block * per_block, per_block)
                mask = jnp.broadcast_to(flags[block : block + 1, :], (per_block, HEAD_SIZE)) > 0.5
                for which, total, gain in ((0, key_total, scale), (1, value_total, 1.0)):
                    part = (2 * who + which) * rows + block * per_block
                    first = total[0, at, :] * gain
                    second = total[1, at, :] * gain
                    home_outs[k][part : part + per_block, :] = jnp.where(mask, second, first).astype(BF16)
                    away_outs[k][part : part + per_block, :] = jnp.where(mask, first, second).astype(BF16)


def local(queries, key_rows, value_rows, out_grad, documents, swapped):
    ranks = lax.axis_size("ctx")
    hops = ranks // 4
    count = hops + 1
    slots = 2 * count
    rows, width = key_rows.shape[1:]
    keys = slots * rows
    size = 2 * rows + META
    queries, out_grad = queries[0], out_grad[0]

    def up(block, k):
        return lax.ppermute(block, "ctx", [(i, i + 2 * k) for i in range(ranks - 2 * k)])

    def down(block, k):
        return lax.ppermute(block, "ctx", [(i + 2 * k, i) for i in range(ranks - 2 * k)])

    def to_partner(block):
        return lax.ppermute(block, "half", [(0, 1), (1, 0)])

    def to_side(block):
        return lax.ppermute(block, "ctx", [(i, i ^ 1) for i in range(ranks)])

    payload, payload_side = pl.pallas_call(
        payload_kernel,
        out_shape=[pltpu.VMEM((size, HEAD_SIZE), BF16)] * 2,
        in_specs=[SMEM, VMEM, VMEM, VMEM],
        out_specs=[VMEM, VMEM],
    )(swapped[0, 0], key_rows[0], value_rows[0], documents)
    from_side = to_side(payload_side)

    def rows_of(other, queries, out_grad):
        return pl.pallas_call(
            functools.partial(rows_kernel, other),
            out_shape=pltpu.VMEM((2 * rows, HALF), BF16),
            in_specs=[HBM, HBM],
            out_specs=VMEM,
            scratch_shapes=[pltpu.SemaphoreType.DMA((2,))],
            compiler_params=None if other else SMALL,
        )(queries, out_grad)

    both = jnp.concatenate([payload, from_side], axis=0)
    rows_side = rows_of(True, queries, out_grad)
    both, rows_side = lax.optimization_barrier((both, rows_side))
    rows_got = to_side(rows_side)
    home = [both] + [up(both, k) for k in range(1, count)]
    away = [to_partner(block) for block in home]
    *early, home[hops], queries, out_grad = lax.optimization_barrier(
        (*home[:hops], *away[:hops], home[hops], queries, out_grad)
    )
    rows_all = jnp.concatenate([rows_of(False, queries, out_grad), rows_got], axis=0)
    ready = pl.pallas_call(
        functools.partial(prepare_kernel, hops),
        out_shape=[pltpu.VMEM((2, 2 * rows * hops, HEAD_SIZE), BF16)] * 2
        + [pltpu.VMEM((2, HEAD_SIZE, 2 * rows * hops), BF16)] * 2,
        in_specs=[VMEM] * (2 * hops),
        out_specs=[VMEM] * 4,
        compiler_params=SMALL,
        cost_estimate=pl.CostEstimate(flops=0, bytes_accessed=4 * 1024 * 1024, transcendentals=0),
    )(*early)
    chunk = pltpu.VMEM((4 * rows, HEAD_SIZE), BF16)
    outs = pl.pallas_call(
        functools.partial(attention_kernel, hops),
        out_shape=[pltpu.VMEM((4 * rows, HALF), BF16)] + [chunk] * (2 * count),
        in_specs=[VMEM] * (5 + 2 * count),
        out_specs=[VMEM] * (1 + 2 * count),
        scratch_shapes=[
            pltpu.VMEM((2, keys, HEAD_SIZE), BF16),
            pltpu.VMEM((2, keys, HEAD_SIZE), BF16),
            pltpu.VMEM((2, HEAD_SIZE, keys), BF16),
            pltpu.VMEM((2, HEAD_SIZE, keys), BF16),
            pltpu.VMEM((2, 16, rows), F32),
            pltpu.VMEM((2, 8, rows), I32),
            pltpu.VMEM((8, rows), F32),
            pltpu.VMEM((2, keys, HEAD_SIZE), F32),
            pltpu.VMEM((2, keys, HEAD_SIZE), F32),
            pltpu.SMEM((2 * NBLK,), I32),
            pltpu.SMEM((2 * NBLK,), I32),
        ],
        compiler_params=pltpu.CompilerParams(vmem_limit_bytes=32 * 1024 * 1024),
        cost_estimate=pl.CostEstimate(
            flops=12 * rows * keys * 2048,
            bytes_accessed=4 * 1024 * 1024,
            transcendentals=rows * keys * 16,
        ),
    )(rows_all, *home, *away, *ready)
    home_sum, away_sum = outs[1 : 1 + count], outs[1 + count :]
    side_out = outs[0][2 * rows :]
    out, query_grad = pl.pallas_call(
        own_kernel,
        out_shape=[jax.ShapeDtypeStruct(queries.shape, BF16)] * 2,
        in_specs=[VMEM],
        out_specs=[HBM] * 2,
        compiler_params=SMALL,
        scratch_shapes=[pltpu.SemaphoreType.DMA((2,))],
        cost_estimate=pl.CostEstimate(flops=0, bytes_accessed=4 * 1024 * 1024, transcendentals=0),
    )(outs[0])

    parts = []
    for k in reversed(range(count)):
        crossed = to_partner(away_sum[k])
        part = home_sum[k].astype(F32) + crossed.astype(F32)
        if k:
            part = part.astype(BF16)
            part = down(part, k)
        parts.append(part)
    out_got = to_side(side_out)
    out, query_grad = pl.pallas_call(
        finish_kernel,
        out_shape=[jax.ShapeDtypeStruct(queries.shape, BF16)] * 2,
        in_specs=[VMEM, HBM, HBM],
        out_specs=[HBM] * 2,
        compiler_params=SMALL,
        input_output_aliases={1: 0, 2: 1},
        scratch_shapes=[pltpu.SemaphoreType.DMA((2,))],
    )(out_got, out, query_grad)
    parts[0], out, query_grad = lax.optimization_barrier((parts[0], out, query_grad))
    total = sum(part.astype(F32) for part in parts).astype(BF16)
    grads_got = to_side(total[2 * rows :])
    grads = total[: 2 * rows]
    first = core_index() == 0
    grads = jnp.concatenate(
        [jnp.where(first, grads, grads_got), jnp.where(first, grads_got, grads)], axis=1
    )
    return (out[None], query_grad[None], grads[None, :rows], grads[None, rows:])


def solution(mesh):
    groups, ranks = mesh.devices.shape
    wide = Mesh(mesh.devices.reshape(2, groups // 2, ranks), ("half", "pair", "ctx"))
    spec3 = P(("half", "pair"), "ctx", None)
    in_specs = (spec3, spec3, spec3, spec3, P(("half", "pair"), "ctx"), spec3)
    return jax.shard_map(
        local, mesh=wide, in_specs=in_specs, out_specs=(spec3,) * 4, check_vma=False
    )
```

```python
import functools
import math

import jax
import jax.numpy as jnp
from jax import lax
from jax.experimental import pallas as pl
from jax.experimental.pallas import tpu as pltpu
from jax.sharding import Mesh
from jax.sharding import PartitionSpec as P

HEAD_SIZE = 128
QUERY_PER_KEY = 8
NBLK = 4
META = 16
DOC_ROW = NBLK
DOC_VALUES = 16
GROUPED = 4
HALF = QUERY_PER_KEY * HEAD_SIZE
NEG = -1e30
F32, BF16, I32 = jnp.float32, jnp.bfloat16, jnp.int32
NT = (((1,), (1,)), ((), ()))
VMEM = pl.BlockSpec(memory_space=pltpu.VMEM)
SMEM = pl.BlockSpec(memory_space=pltpu.SMEM)
HBM = pl.BlockSpec(memory_space=pltpu.HBM)
SMALL = pltpu.CompilerParams(vmem_limit_bytes=8 * 1024 * 1024)


def core_index():
    return lax.rem(lax.axis_index("ctx"), 2)


def payload_kernel(swap_ref, key_ref, value_ref, docs_ref, own_ref, side_ref):
    rows = key_ref.shape[0]
    core = core_index()
    docs = jnp.broadcast_to(docs_ref[...].astype(F32), (META, rows))
    place = lax.broadcasted_iota(I32, docs.shape, 0)
    meta = jnp.where(place == DOC_ROW, docs, 0.0)
    for block in range(NBLK):
        meta = jnp.where(place == block, swap_ref[block].astype(F32), meta)
    meta = meta.astype(BF16)
    for ref, head in ((own_ref, core), (side_ref, 1 - core)):
        lane = pl.ds(pl.multiple_of(head * HEAD_SIZE, HEAD_SIZE), HEAD_SIZE)
        ref[:rows, :] = key_ref[:, lane]
        ref[rows : 2 * rows, :] = value_ref[:, lane]
        ref[2 * rows :, :] = meta


def rows_kernel(other, query_ref, grad_ref, rows_ref, sems):
    rows = query_ref.shape[0]
    core = core_index()
    head = 1 - core if other else core
    lanes = pl.ds(pl.multiple_of(head * HALF, HALF), HALF)
    copies = [
        pltpu.make_async_copy(
            source.at[:, lanes], rows_ref.at[pl.ds(part * rows, rows), :], sems.at[part]
        )
        for part, source in enumerate((query_ref, grad_ref))
    ]
    for copy in copies:
        copy.start()
    for copy in copies:
        copy.wait()


def write_heads(source_ref, head, out_ref, query_grad_ref, sems):
    rows = out_ref.shape[0]
    lanes = pl.ds(pl.multiple_of(head * HALF, HALF), HALF)
    copies = [
        pltpu.make_async_copy(
            source_ref.at[pl.ds(part * rows, rows), :], target.at[:, lanes], sems.at[part]
        )
        for part, target in enumerate((out_ref, query_grad_ref))
    ]
    for copy in copies:
        copy.start()
    for copy in copies:
        copy.wait()


def own_kernel(own_ref, out_ref, query_grad_ref, sems):
    write_heads(own_ref, core_index(), out_ref, query_grad_ref, sems)


def finish_kernel(side_ref, out_held, query_grad_held, out_ref, query_grad_ref, sems):
    write_heads(side_ref, 1 - core_index(), out_ref, query_grad_ref, sems)


def merge_hop(home, away, slots_at, rows, logs):
    key_log, value_log, key_turned, value_turned = logs
    per_block = rows // NBLK
    size = 2 * rows + META
    for who in range(2):
        base = pl.multiple_of(slots_at[who] * rows, rows)
        flags = home[who * size + 2 * rows : (who + 1) * size, :].astype(F32)
        for which, log, turned in ((0, key_log, key_turned), (1, value_log, value_turned)):
            merged = ([], [])
            for block in range(NBLK):
                mask = (
                    jnp.broadcast_to(flags[block : block + 1, :], (per_block, HEAD_SIZE)).astype(BF16)
                    > 0.5
                )
                first = who * size + which * rows + block * per_block
                own = home[first : first + per_block, :]
                other = away[first : first + per_block, :]
                merged[0].append(jnp.where(mask, other, own))
                merged[1].append(jnp.where(mask, own, other))
            for logical in range(2):
                whole = jnp.concatenate(merged[logical], axis=0)
                log[logical, pl.ds(base, rows), :] = whole
                turned[logical, :, pl.ds(base, rows)] = whole.T


def prepare_kernel(hops, *refs):
    homes, aways = refs[:hops], refs[hops : 2 * hops]
    logs = refs[2 * hops :]
    rows = (homes[0].shape[0] // 2 - META) // 2
    core = core_index()
    parity = (core, 1 - core)
    for k in range(hops):
        slots_at = [2 * (hops - 1 - k) + parity[who] for who in range(2)]
        merge_hop(homes[k], aways[k], slots_at, rows, logs)


def attention_kernel(hops, rows_ref, *refs):
    count = hops + 1
    slots = 2 * count
    window = slots - 1
    homes, aways = refs[:count], refs[count : 2 * count]
    ready = refs[2 * count : 2 * count + 4]
    out_all = refs[2 * count + 4]
    home_outs = refs[2 * count + 5 : 3 * count + 5]
    away_outs = refs[3 * count + 5 : 4 * count + 5]
    (
        key_log,
        value_log,
        key_turned,
        value_turned,
        doc_window,
        starts,
        flag_rows,
        key_total,
        value_total,
        logical_of,
        needed_of,
    ) = refs[4 * count + 5 :]
    rows = rows_ref.shape[0] // 4
    per_block = rows // NBLK
    lanes = QUERY_PER_KEY * per_block
    size = 2 * rows + META
    core = core_index()
    chip = lax.axis_index("ctx") // 2
    parity = (core, 1 - core)
    scale = 1.0 / math.sqrt(HEAD_SIZE)
    factor = scale * math.log2(math.e)

    key_total[...] = jnp.zeros_like(key_total)
    value_total[...] = jnp.zeros_like(value_total)
    doc_window[...] = jnp.full_like(doc_window, 1e4)

    def meta_of(ref, who):
        return ref[who * size + 2 * rows : (who + 1) * size, :].astype(F32)

    for k in range(count):
        for who in range(2):
            slot = 2 * (hops - k) + parity[who]
            base = pl.multiple_of(slot * rows, rows)
            for logical, ref in ((0, homes[k]), (1, aways[k])):
                docs = meta_of(ref, who)[DOC_ROW : DOC_ROW + 1, :]
                doc_window[logical, pl.ds(slot, 1), :] = jnp.where(chip >= k, docs, -1.0)
    logs = (key_log, value_log, key_turned, value_turned)
    for log, held in zip(logs[:2], ready[:2]):
        log[:, pl.ds(2 * rows, 2 * rows * hops), :] = held[...]
    for log, held in zip(logs[2:], ready[2:]):
        log[:, :, pl.ds(2 * rows, 2 * rows * hops)] = held[...]
    merge_hop(homes[hops], aways[hops], parity, rows, logs)

    values_down = lax.broadcasted_iota(I32, (DOC_VALUES, rows), 0).astype(F32)
    group = lax.broadcasted_iota(I32, (8, rows), 1) // per_block
    meta_rows = [meta_of(homes[0], who) for who in range(2)]
    for logical in range(2):
        lower = jnp.zeros((DOC_VALUES, rows), F32)
        for slot in range(slots):
            docs = jnp.broadcast_to(doc_window[logical, slot : slot + 1, :], lower.shape)
            lower = lower + jnp.where(docs < values_down, 1.0, 0.0)
        lower = jnp.broadcast_to(jnp.sum(lower, axis=1, keepdims=True), lower.shape)
        for who in range(2):
            docs = meta_of((homes, aways)[logical][0], who)[DOC_ROW : DOC_ROW + 1, :]
            docs = jnp.broadcast_to(docs, (8, rows))
            turns = [docs] + [pltpu.roll(docs, t * per_block, 1) for t in range(1, NBLK)]
            for block in range(NBLK):
                tiled = turns[0]
                for t in range(1, NBLK):
                    tiled = jnp.where(group == (block + t) % NBLK, turns[t], tiled)
                tiled = jnp.broadcast_to(tiled[:1], lower.shape)
                start = jnp.sum(jnp.where(tiled == values_down, lower, 0.0), axis=0, keepdims=True)
                starts[logical, who * NBLK + block : who * NBLK + block + 1, :] = start.astype(I32)
    for who in range(2):
        flag_rows[who * NBLK : (who + 1) * NBLK, :] = meta_rows[who][:NBLK, :]
    flags = flag_rows[...]
    firsts = [
        jnp.broadcast_to(
            jnp.min(starts[logical].astype(F32), axis=1, keepdims=True), flags.shape
        )
        for logical in range(2)
    ]
    first = jnp.where(flags > 0.5, firsts[1], firsts[0]).astype(I32)
    flags = flags.astype(I32)
    for unit_index in range(2 * NBLK):
        logical_of[unit_index] = flags[unit_index, 0]
        needed_of[unit_index] = window + parity[unit_index // NBLK] - first[unit_index, 0] // rows

    def unit(unit_index, chunks):
        who, block = unit_index // NBLK, lax.rem(unit_index, NBLK)
        logical = logical_of[unit_index]
        row_parity = jnp.where(who == 0, core, 1 - core)
        first_slot = window + row_parity - chunks
        first = pl.multiple_of(first_slot * rows, rows)
        span = pl.ds(first, chunks * rows)
        columns = [slice(h * HEAD_SIZE, (h + 1) * HEAD_SIZE) for h in range(QUERY_PER_KEY)]
        query_at = pl.ds(pl.multiple_of(2 * who * rows + block * per_block, per_block), per_block)
        grad_at = pl.ds(
            pl.multiple_of((2 * who + 1) * rows + block * per_block, per_block), per_block
        )
        query = jnp.concatenate([rows_ref[query_at, column] for column in columns], axis=0)
        grad = jnp.concatenate([rows_ref[grad_at, column] for column in columns], axis=0)
        scores = lax.dot_general(key_log[logical, span, :], query, NT, preferred_element_type=F32)
        shape = (chunks * rows, HEAD_SIZE)
        key_place = lax.broadcasted_iota(I32, shape, 0)
        row_first = starts[logical, pl.ds(unit_index, 1), :] - first
        row_last = (
            (chunks - 1) * rows
            + block * per_block
            + lax.rem(lax.broadcasted_iota(I32, (1, HEAD_SIZE), 1), per_block)
        )
        early = (chunks - 1) * rows
        allowed = [
            (slice(early, None), (key_place[early:] >= row_first) & (key_place[early:] <= row_last))
        ]
        if early:
            allowed.insert(0, (slice(0, early), key_place[:early] >= row_first))
        scores = jnp.concatenate(
            [
                jnp.concatenate(
                    [
                        jnp.where(keep, scores[part, lane : lane + HEAD_SIZE], NEG)
                        for lane in range(0, lanes, HEAD_SIZE)
                    ],
                    axis=1,
                )
                for part, keep in allowed
            ],
            axis=0,
        )
        peak = jnp.max(scores, axis=0, keepdims=True)
        powers = jnp.exp2((scores - peak) * factor)
        inverse = 1.0 / jnp.sum(powers, axis=0, keepdims=True)
        probs = powers * inverse
        weights = probs.astype(BF16)
        out_turned = jnp.dot(
            value_turned[logical, :, span], weights, preferred_element_type=F32
        ).astype(BF16)
        delta = jnp.sum(grad.T.astype(F32) * out_turned.astype(F32), axis=0, keepdims=True)
        prob_grad = lax.dot_general(
            value_log[logical, span, :], grad, NT, preferred_element_type=F32
        )
        score_grad = (probs * (prob_grad - delta)).astype(BF16)
        query_grad_turned = jnp.dot(
            key_turned[logical, :, span], score_grad, preferred_element_type=F32
        )
        key_add = jnp.dot(score_grad, query, preferred_element_type=F32)
        value_add = jnp.dot(weights, grad, preferred_element_type=F32)
        out = out_turned.T
        query_grad = (query_grad_turned * scale).astype(BF16).T
        return query_at, grad_at, logical, span, out, query_grad, key_add, value_add

    def step(pair, carry):
        members = [pair * GROUPED + m for m in range(GROUPED)]
        needed = needed_of[members[0]]
        for member in members[1:]:
            needed = jnp.maximum(needed, needed_of[member])
        for chunks in range(1, window + 1):

            @pl.when(needed == chunks)
            def _(chunks=chunks):
                results = [unit(member, chunks) for member in members]
                for query_at, grad_at, logical, span, out, query_grad, key_add, value_add in results:
                    key_total[logical, span, :] += key_add
                    value_total[logical, span, :] += value_add
                    for h in range(QUERY_PER_KEY):
                        column = slice(h * HEAD_SIZE, (h + 1) * HEAD_SIZE)
                        part = slice(h * per_block, (h + 1) * per_block)
                        out_all[query_at, column] = out[part, :]
                        out_all[grad_at, column] = query_grad[part, :]

        return carry

    lax.fori_loop(0, 2 * NBLK // GROUPED, step, 0)
    for k in range(count):
        for who in range(2):
            base = pl.multiple_of((2 * (hops - k) + parity[who]) * rows, rows)
            flags = meta_of(homes[k], who)
            for block in range(NBLK):
                at = pl.ds(base + block * per_block, per_block)
                mask = (
                    jnp.broadcast_to(flags[block : block + 1, :], (per_block, HEAD_SIZE)).astype(BF16)
                    > 0.5
                )
                for which, total, gain in ((0, key_total, scale), (1, value_total, 1.0)):
                    part = (2 * who + which) * rows + block * per_block
                    first = (total[0, at, :] * gain).astype(BF16)
                    second = (total[1, at, :] * gain).astype(BF16)
                    home_outs[k][part : part + per_block, :] = jnp.where(mask, second, first)
                    away_outs[k][part : part + per_block, :] = jnp.where(mask, first, second)


def local(queries, key_rows, value_rows, out_grad, documents, swapped):
    ranks = lax.axis_size("ctx")
    hops = ranks // 4
    count = hops + 1
    slots = 2 * count
    rows, width = key_rows.shape[1:]
    keys = slots * rows
    size = 2 * rows + META
    queries, out_grad = queries[0], out_grad[0]

    def up(block, k):
        return lax.ppermute(block, "ctx", [(i, i + 2 * k) for i in range(ranks - 2 * k)])

    def down(block, k):
        return lax.ppermute(block, "ctx", [(i + 2 * k, i) for i in range(ranks - 2 * k)])

    def to_partner(block):
        return lax.ppermute(block, "half", [(0, 1), (1, 0)])

    def to_side(block):
        return lax.ppermute(block, "ctx", [(i, i ^ 1) for i in range(ranks)])

    payload, payload_side = pl.pallas_call(
        payload_kernel,
        out_shape=[pltpu.VMEM((size, HEAD_SIZE), BF16)] * 2,
        in_specs=[SMEM, VMEM, VMEM, VMEM],
        out_specs=[VMEM, VMEM],
    )(swapped[0, 0], key_rows[0], value_rows[0], documents)
    from_side = to_side(payload_side)

    def rows_of(other, queries, out_grad):
        return pl.pallas_call(
            functools.partial(rows_kernel, other),
            out_shape=pltpu.VMEM((2 * rows, HALF), BF16),
            in_specs=[HBM, HBM],
            out_specs=VMEM,
            scratch_shapes=[pltpu.SemaphoreType.DMA((2,))],
            compiler_params=None if other else SMALL,
        )(queries, out_grad)

    both = jnp.concatenate([payload, from_side], axis=0)
    rows_side = rows_of(True, queries, out_grad)
    both, rows_side = lax.optimization_barrier((both, rows_side))
    rows_got = to_side(rows_side)
    home = [both] + [up(both, k) for k in range(1, count)]
    away = [to_partner(block) for block in home]
    *early, home[hops], queries, out_grad = lax.optimization_barrier(
        (*home[:hops], *away[:hops], home[hops], queries, out_grad)
    )
    rows_all = jnp.concatenate([rows_of(False, queries, out_grad), rows_got], axis=0)
    ready = pl.pallas_call(
        functools.partial(prepare_kernel, hops),
        out_shape=[pltpu.VMEM((2, 2 * rows * hops, HEAD_SIZE), BF16)] * 2
        + [pltpu.VMEM((2, HEAD_SIZE, 2 * rows * hops), BF16)] * 2,
        in_specs=[VMEM] * (2 * hops),
        out_specs=[VMEM] * 4,
        compiler_params=SMALL,
        cost_estimate=pl.CostEstimate(flops=0, bytes_accessed=4 * 1024 * 1024, transcendentals=0),
    )(*early)
    chunk = pltpu.VMEM((4 * rows, HEAD_SIZE), BF16)
    outs = pl.pallas_call(
        functools.partial(attention_kernel, hops),
        out_shape=[pltpu.VMEM((4 * rows, HALF), BF16)] + [chunk] * (2 * count),
        in_specs=[VMEM] * (5 + 2 * count),
        out_specs=[VMEM] * (1 + 2 * count),
        scratch_shapes=[
            pltpu.VMEM((2, keys, HEAD_SIZE), BF16),
            pltpu.VMEM((2, keys, HEAD_SIZE), BF16),
            pltpu.VMEM((2, HEAD_SIZE, keys), BF16),
            pltpu.VMEM((2, HEAD_SIZE, keys), BF16),
            pltpu.VMEM((2, 16, rows), F32),
            pltpu.VMEM((2, 8, rows), I32),
            pltpu.VMEM((8, rows), F32),
            pltpu.VMEM((2, keys, HEAD_SIZE), F32),
            pltpu.VMEM((2, keys, HEAD_SIZE), F32),
            pltpu.SMEM((2 * NBLK,), I32),
            pltpu.SMEM((2 * NBLK,), I32),
        ],
        compiler_params=pltpu.CompilerParams(vmem_limit_bytes=32 * 1024 * 1024),
        cost_estimate=pl.CostEstimate(
            flops=12 * rows * keys * 2048,
            bytes_accessed=4 * 1024 * 1024,
            transcendentals=rows * keys * 16,
        ),
    )(rows_all, *home, *away, *ready)
    home_sum, away_sum = outs[1 : 1 + count], outs[1 + count :]
    side_out = outs[0][2 * rows :]
    out, query_grad = pl.pallas_call(
        own_kernel,
        out_shape=[jax.ShapeDtypeStruct(queries.shape, BF16)] * 2,
        in_specs=[VMEM],
        out_specs=[HBM] * 2,
        compiler_params=SMALL,
        scratch_shapes=[pltpu.SemaphoreType.DMA((2,))],
        cost_estimate=pl.CostEstimate(flops=0, bytes_accessed=4 * 1024 * 1024, transcendentals=0),
    )(outs[0])

    parts = []
    for k in reversed(range(count)):
        crossed = to_partner(away_sum[k])
        part = home_sum[k].astype(F32) + crossed.astype(F32)
        if k:
            part = part.astype(BF16)
            part = down(part, k)
        parts.append(part)
    out_got = to_side(side_out)
    out, query_grad = pl.pallas_call(
        finish_kernel,
        out_shape=[jax.ShapeDtypeStruct(queries.shape, BF16)] * 2,
        in_specs=[VMEM, HBM, HBM],
        out_specs=[HBM] * 2,
        compiler_params=SMALL,
        input_output_aliases={1: 0, 2: 1},
        scratch_shapes=[pltpu.SemaphoreType.DMA((2,))],
    )(out_got, out, query_grad)
    parts[0], out, query_grad = lax.optimization_barrier((parts[0], out, query_grad))
    total = sum(part.astype(F32) for part in parts).astype(BF16)
    grads_got = to_side(total[2 * rows :])
    grads = total[: 2 * rows]
    first = core_index() == 0
    grads = jnp.concatenate(
        [jnp.where(first, grads, grads_got), jnp.where(first, grads_got, grads)], axis=1
    )
    return (out[None], query_grad[None], grads[None, :rows], grads[None, rows:])


def solution(mesh):
    groups, ranks = mesh.devices.shape
    wide = Mesh(mesh.devices.reshape(2, groups // 2, ranks), ("half", "pair", "ctx"))
    spec3 = P(("half", "pair"), "ctx", None)
    in_specs = (spec3, spec3, spec3, spec3, P(("half", "pair"), "ctx"), spec3)
    return jax.shard_map(
        local, mesh=wide, in_specs=in_specs, out_specs=(spec3,) * 4, check_vma=False
    )
```

```python
import functools
import math

import jax
import jax.numpy as jnp
from jax import lax
from jax.experimental import pallas as pl
from jax.experimental.pallas import tpu as pltpu
from jax.sharding import Mesh
from jax.sharding import PartitionSpec as P

HEAD_SIZE = 128
QUERY_PER_KEY = 8
NBLK = 4
META = 16
DOC_ROW = NBLK
DOC_VALUES = 16
GROUPED = 4
HALF = QUERY_PER_KEY * HEAD_SIZE
NEG = -1e30
F32, BF16, I32 = jnp.float32, jnp.bfloat16, jnp.int32
NT = (((1,), (1,)), ((), ()))
VMEM = pl.BlockSpec(memory_space=pltpu.VMEM)
SMEM = pl.BlockSpec(memory_space=pltpu.SMEM)
HBM = pl.BlockSpec(memory_space=pltpu.HBM)
SMALL = pltpu.CompilerParams(vmem_limit_bytes=8 * 1024 * 1024)


def core_index():
    return lax.rem(lax.axis_index("ctx"), 2)


def payload_kernel(swap_ref, key_ref, value_ref, docs_ref, own_ref, side_ref):
    rows = key_ref.shape[0]
    core = core_index()
    docs = jnp.broadcast_to(docs_ref[...].astype(F32), (META, rows))
    place = lax.broadcasted_iota(I32, docs.shape, 0)
    meta = jnp.where(place == DOC_ROW, docs, 0.0)
    for block in range(NBLK):
        meta = jnp.where(place == block, swap_ref[block].astype(F32), meta)
    meta = meta.astype(BF16)
    for ref, head in ((own_ref, core), (side_ref, 1 - core)):
        lane = pl.ds(pl.multiple_of(head * HEAD_SIZE, HEAD_SIZE), HEAD_SIZE)
        ref[:rows, :] = key_ref[:, lane]
        ref[rows : 2 * rows, :] = value_ref[:, lane]
        ref[2 * rows :, :] = meta


def rows_kernel(other, query_ref, grad_ref, rows_ref, sems):
    rows = query_ref.shape[0]
    core = core_index()
    head = 1 - core if other else core
    lanes = pl.ds(pl.multiple_of(head * HALF, HALF), HALF)
    copies = [
        pltpu.make_async_copy(
            source.at[:, lanes], rows_ref.at[pl.ds(part * rows, rows), :], sems.at[part]
        )
        for part, source in enumerate((query_ref, grad_ref))
    ]
    for copy in copies:
        copy.start()
    for copy in copies:
        copy.wait()


def write_heads(source_ref, head, out_ref, query_grad_ref, sems):
    rows = out_ref.shape[0]
    lanes = pl.ds(pl.multiple_of(head * HALF, HALF), HALF)
    copies = [
        pltpu.make_async_copy(
            source_ref.at[pl.ds(part * rows, rows), :], target.at[:, lanes], sems.at[part]
        )
        for part, target in enumerate((out_ref, query_grad_ref))
    ]
    for copy in copies:
        copy.start()
    for copy in copies:
        copy.wait()


def own_kernel(own_ref, out_ref, query_grad_ref, sems):
    write_heads(own_ref, core_index(), out_ref, query_grad_ref, sems)


def finish_kernel(side_ref, out_held, query_grad_held, out_ref, query_grad_ref, sems):
    write_heads(side_ref, 1 - core_index(), out_ref, query_grad_ref, sems)


def merge_hop(home, away, slots_at, rows, logs):
    key_log, value_log, key_turned, value_turned = logs
    per_block = rows // NBLK
    size = 2 * rows + META
    for who in range(2):
        base = pl.multiple_of(slots_at[who] * rows, rows)
        flags = home[who * size + 2 * rows : (who + 1) * size, :].astype(F32)
        for which, log, turned in ((0, key_log, key_turned), (1, value_log, value_turned)):
            merged = ([], [])
            for block in range(NBLK):
                mask = (
                    jnp.broadcast_to(flags[block : block + 1, :], (per_block, HEAD_SIZE)).astype(BF16)
                    > 0.5
                )
                first = who * size + which * rows + block * per_block
                own = home[first : first + per_block, :]
                other = away[first : first + per_block, :]
                merged[0].append(jnp.where(mask, other, own))
                merged[1].append(jnp.where(mask, own, other))
            for logical in range(2):
                whole = jnp.concatenate(merged[logical], axis=0)
                log[logical, pl.ds(base, rows), :] = whole
                turned[logical, :, pl.ds(base, rows)] = whole.T


def prepare_kernel(hops, *refs):
    homes, aways = refs[:hops], refs[hops : 2 * hops]
    logs = refs[2 * hops :]
    rows = (homes[0].shape[0] // 2 - META) // 2
    core = core_index()
    parity = (core, 1 - core)
    for k in range(hops):
        slots_at = [2 * (hops - 1 - k) + parity[who] for who in range(2)]
        merge_hop(homes[k], aways[k], slots_at, rows, logs)


def attention_kernel(hops, rows_ref, *refs):
    count = hops + 1
    slots = 2 * count
    window = slots - 1
    homes, aways = refs[:count], refs[count : 2 * count]
    ready = refs[2 * count : 2 * count + 4]
    out_all = refs[2 * count + 4]
    home_outs = refs[2 * count + 5 : 3 * count + 5]
    away_outs = refs[3 * count + 5 : 4 * count + 5]
    (
        key_log,
        value_log,
        key_turned,
        value_turned,
        doc_window,
        starts,
        flag_rows,
        key_total,
        value_total,
        logical_of,
        needed_of,
    ) = refs[4 * count + 5 :]
    rows = rows_ref.shape[0] // 4
    per_block = rows // NBLK
    lanes = QUERY_PER_KEY * per_block
    size = 2 * rows + META
    core = core_index()
    chip = lax.axis_index("ctx") // 2
    parity = (core, 1 - core)
    scale = 1.0 / math.sqrt(HEAD_SIZE)
    factor = scale * math.log2(math.e)

    key_total[...] = jnp.zeros_like(key_total)
    value_total[...] = jnp.zeros_like(value_total)
    doc_window[...] = jnp.full_like(doc_window, 1e4)

    def meta_of(ref, who):
        return ref[who * size + 2 * rows : (who + 1) * size, :].astype(F32)

    for k in range(count):
        for who in range(2):
            slot = 2 * (hops - k) + parity[who]
            base = pl.multiple_of(slot * rows, rows)
            for logical, ref in ((0, homes[k]), (1, aways[k])):
                docs = meta_of(ref, who)[DOC_ROW : DOC_ROW + 1, :]
                doc_window[logical, pl.ds(slot, 1), :] = jnp.where(chip >= k, docs, -1.0)
    logs = (key_log, value_log, key_turned, value_turned)
    for log, held in zip(logs[:2], ready[:2]):
        log[:, pl.ds(2 * rows, 2 * rows * hops), :] = held[...]
    for log, held in zip(logs[2:], ready[2:]):
        log[:, :, pl.ds(2 * rows, 2 * rows * hops)] = held[...]
    merge_hop(homes[hops], aways[hops], parity, rows, logs)

    values_down = lax.broadcasted_iota(I32, (DOC_VALUES, rows), 0).astype(F32)
    group = lax.broadcasted_iota(I32, (8, rows), 1) // per_block
    meta_rows = [meta_of(homes[0], who) for who in range(2)]
    for logical in range(2):
        lower = jnp.zeros((DOC_VALUES, rows), F32)
        for slot in range(slots):
            docs = jnp.broadcast_to(doc_window[logical, slot : slot + 1, :], lower.shape)
            lower = lower + jnp.where(docs < values_down, 1.0, 0.0)
        lower = jnp.broadcast_to(jnp.sum(lower, axis=1, keepdims=True), lower.shape)
        for who in range(2):
            docs = meta_of((homes, aways)[logical][0], who)[DOC_ROW : DOC_ROW + 1, :]
            docs = jnp.broadcast_to(docs, (8, rows))
            turns = [docs] + [pltpu.roll(docs, t * per_block, 1) for t in range(1, NBLK)]
            for block in range(NBLK):
                tiled = turns[0]
                for t in range(1, NBLK):
                    tiled = jnp.where(group == (block + t) % NBLK, turns[t], tiled)
                tiled = jnp.broadcast_to(tiled[:1], lower.shape)
                start = jnp.sum(jnp.where(tiled == values_down, lower, 0.0), axis=0, keepdims=True)
                starts[logical, who * NBLK + block : who * NBLK + block + 1, :] = start.astype(I32)
    for who in range(2):
        flag_rows[who * NBLK : (who + 1) * NBLK, :] = meta_rows[who][:NBLK, :]
    flags = flag_rows[...]
    firsts = [
        jnp.broadcast_to(
            jnp.min(starts[logical].astype(F32), axis=1, keepdims=True), flags.shape
        )
        for logical in range(2)
    ]
    first = jnp.where(flags > 0.5, firsts[1], firsts[0]).astype(I32)
    flags = flags.astype(I32)
    for unit_index in range(2 * NBLK):
        logical_of[unit_index] = flags[unit_index, 0]
        needed_of[unit_index] = window + parity[unit_index // NBLK] - first[unit_index, 0] // rows

    def unit(unit_index, chunks):
        who, block = unit_index // NBLK, lax.rem(unit_index, NBLK)
        logical = logical_of[unit_index]
        row_parity = jnp.where(who == 0, core, 1 - core)
        first_slot = window + row_parity - chunks
        first = pl.multiple_of(first_slot * rows, rows)
        span = pl.ds(first, chunks * rows)
        columns = [slice(h * HEAD_SIZE, (h + 1) * HEAD_SIZE) for h in range(QUERY_PER_KEY)]
        query_at = pl.ds(pl.multiple_of(2 * who * rows + block * per_block, per_block), per_block)
        grad_at = pl.ds(
            pl.multiple_of((2 * who + 1) * rows + block * per_block, per_block), per_block
        )
        query = jnp.concatenate([rows_ref[query_at, column] for column in columns], axis=0)
        grad = jnp.concatenate([rows_ref[grad_at, column] for column in columns], axis=0)
        scores = lax.dot_general(key_log[logical, span, :], query, NT, preferred_element_type=F32)
        shape = (chunks * rows, HEAD_SIZE)
        key_place = lax.broadcasted_iota(I32, shape, 0)
        row_first = starts[logical, pl.ds(unit_index, 1), :] - first
        row_last = (
            (chunks - 1) * rows
            + block * per_block
            + lax.rem(lax.broadcasted_iota(I32, (1, HEAD_SIZE), 1), per_block)
        )
        allowed = (key_place >= row_first) & (key_place <= row_last)
        scores = jnp.concatenate(
            [
                jnp.where(allowed, scores[:, lane : lane + HEAD_SIZE], NEG)
                for lane in range(0, lanes, HEAD_SIZE)
            ],
            axis=1,
        )
        peak = jnp.max(scores, axis=0, keepdims=True)
        powers = jnp.exp2((scores - peak) * factor)
        inverse = 1.0 / jnp.sum(powers, axis=0, keepdims=True)
        probs = powers * inverse
        weights = probs.astype(BF16)
        out_turned = jnp.dot(
            value_turned[logical, :, span], weights, preferred_element_type=F32
        ).astype(BF16)
        delta = jnp.sum(grad.T.astype(F32) * out_turned.astype(F32), axis=0, keepdims=True)
        prob_grad = lax.dot_general(
            value_log[logical, span, :], grad, NT, preferred_element_type=F32
        )
        score_grad = (probs * (prob_grad - delta)).astype(BF16)
        query_grad_turned = jnp.dot(
            key_turned[logical, :, span], score_grad, preferred_element_type=F32
        )
        key_add = jnp.dot(score_grad, query, preferred_element_type=F32)
        value_add = jnp.dot(weights, grad, preferred_element_type=F32)
        out = out_turned.T
        query_grad = (query_grad_turned * scale).astype(BF16).T
        return query_at, grad_at, logical, span, out, query_grad, key_add, value_add

    def step(pair, carry):
        members = [pair * GROUPED + m for m in range(GROUPED)]
        needed = needed_of[members[0]]
        for member in members[1:]:
            needed = jnp.maximum(needed, needed_of[member])
        for chunks in range(1, window + 1):

            @pl.when(needed == chunks)
            def _(chunks=chunks):
                results = [unit(member, chunks) for member in members]
                for query_at, grad_at, logical, span, out, query_grad, key_add, value_add in results:
                    key_total[logical, span, :] += key_add
                    value_total[logical, span, :] += value_add
                    for h in range(QUERY_PER_KEY):
                        column = slice(h * HEAD_SIZE, (h + 1) * HEAD_SIZE)
                        part = slice(h * per_block, (h + 1) * per_block)
                        out_all[query_at, column] = out[part, :]
                        out_all[grad_at, column] = query_grad[part, :]

        return carry

    lax.fori_loop(0, 2 * NBLK // GROUPED, step, 0)
    for k in range(count):
        for who in range(2):
            base = pl.multiple_of((2 * (hops - k) + parity[who]) * rows, rows)
            flags = meta_of(homes[k], who)
            for block in range(NBLK):
                at = pl.ds(base + block * per_block, per_block)
                mask = jnp.broadcast_to(flags[block : block + 1, :], (per_block, HEAD_SIZE)) > 0.5
                for which, total, gain in ((0, key_total, scale), (1, value_total, 1.0)):
                    part = (2 * who + which) * rows + block * per_block
                    first = total[0, at, :] * gain
                    second = total[1, at, :] * gain
                    home_outs[k][part : part + per_block, :] = jnp.where(mask, second, first).astype(BF16)
                    away_outs[k][part : part + per_block, :] = jnp.where(mask, first, second).astype(BF16)


def local(queries, key_rows, value_rows, out_grad, documents, swapped):
    ranks = lax.axis_size("ctx")
    hops = ranks // 4
    count = hops + 1
    slots = 2 * count
    rows, width = key_rows.shape[1:]
    keys = slots * rows
    size = 2 * rows + META
    queries, out_grad = queries[0], out_grad[0]

    def up(block, k):
        return lax.ppermute(block, "ctx", [(i, i + 2 * k) for i in range(ranks - 2 * k)])

    def down(block, k):
        return lax.ppermute(block, "ctx", [(i + 2 * k, i) for i in range(ranks - 2 * k)])

    def down_across(block, k):
        return lax.ppermute(block, "ctx", [(i + 2 * k, i ^ 1) for i in range(ranks - 2 * k)])

    def to_partner(block):
        return lax.ppermute(block, "half", [(0, 1), (1, 0)])

    def to_side(block):
        return lax.ppermute(block, "ctx", [(i, i ^ 1) for i in range(ranks)])

    payload, payload_side = pl.pallas_call(
        payload_kernel,
        out_shape=[pltpu.VMEM((size, HEAD_SIZE), BF16)] * 2,
        in_specs=[SMEM, VMEM, VMEM, VMEM],
        out_specs=[VMEM, VMEM],
    )(swapped[0, 0], key_rows[0], value_rows[0], documents)
    from_side = to_side(payload_side)

    def rows_of(other, queries, out_grad):
        return pl.pallas_call(
            functools.partial(rows_kernel, other),
            out_shape=pltpu.VMEM((2 * rows, HALF), BF16),
            in_specs=[HBM, HBM],
            out_specs=VMEM,
            scratch_shapes=[pltpu.SemaphoreType.DMA((2,))],
            compiler_params=None if other else SMALL,
        )(queries, out_grad)

    both = jnp.concatenate([payload, from_side], axis=0)
    rows_side = rows_of(True, queries, out_grad)
    both, rows_side = lax.optimization_barrier((both, rows_side))
    rows_got = to_side(rows_side)
    home = [both] + [up(both, k) for k in range(1, count)]
    away = [to_partner(block) for block in home]
    *early, home[hops], queries, out_grad = lax.optimization_barrier(
        (*home[:hops], *away[:hops], home[hops], queries, out_grad)
    )
    rows_all = jnp.concatenate([rows_of(False, queries, out_grad), rows_got], axis=0)
    ready = pl.pallas_call(
        functools.partial(prepare_kernel, hops),
        out_shape=[pltpu.VMEM((2, 2 * rows * hops, HEAD_SIZE), BF16)] * 2
        + [pltpu.VMEM((2, HEAD_SIZE, 2 * rows * hops), BF16)] * 2,
        in_specs=[VMEM] * (2 * hops),
        out_specs=[VMEM] * 4,
        compiler_params=SMALL,
        cost_estimate=pl.CostEstimate(flops=0, bytes_accessed=4 * 1024 * 1024, transcendentals=0),
    )(*early)
    chunk = pltpu.VMEM((4 * rows, HEAD_SIZE), BF16)
    outs = pl.pallas_call(
        functools.partial(attention_kernel, hops),
        out_shape=[pltpu.VMEM((4 * rows, HALF), BF16)] + [chunk] * (2 * count),
        in_specs=[VMEM] * (5 + 2 * count),
        out_specs=[VMEM] * (1 + 2 * count),
        scratch_shapes=[
            pltpu.VMEM((2, keys, HEAD_SIZE), BF16),
            pltpu.VMEM((2, keys, HEAD_SIZE), BF16),
            pltpu.VMEM((2, HEAD_SIZE, keys), BF16),
            pltpu.VMEM((2, HEAD_SIZE, keys), BF16),
            pltpu.VMEM((2, 16, rows), F32),
            pltpu.VMEM((2, 8, rows), I32),
            pltpu.VMEM((8, rows), F32),
            pltpu.VMEM((2, keys, HEAD_SIZE), F32),
            pltpu.VMEM((2, keys, HEAD_SIZE), F32),
            pltpu.SMEM((2 * NBLK,), I32),
            pltpu.SMEM((2 * NBLK,), I32),
        ],
        compiler_params=pltpu.CompilerParams(vmem_limit_bytes=32 * 1024 * 1024),
        cost_estimate=pl.CostEstimate(
            flops=12 * rows * keys * 2048,
            bytes_accessed=4 * 1024 * 1024,
            transcendentals=rows * keys * 16,
        ),
    )(rows_all, *home, *away, *ready)
    home_sum, away_sum = outs[1 : 1 + count], outs[1 + count :]
    side_out = outs[0][2 * rows :]
    out, query_grad = pl.pallas_call(
        own_kernel,
        out_shape=[jax.ShapeDtypeStruct(queries.shape, BF16)] * 2,
        in_specs=[VMEM],
        out_specs=[HBM] * 2,
        compiler_params=SMALL,
        scratch_shapes=[pltpu.SemaphoreType.DMA((2,))],
        cost_estimate=pl.CostEstimate(flops=0, bytes_accessed=4 * 1024 * 1024, transcendentals=0),
    )(outs[0])

    parts, side_parts = [], []
    for k in reversed(range(count)):
        crossed = to_partner(away_sum[k])
        part = home_sum[k].astype(F32) + crossed.astype(F32)
        near, far = part[: 2 * rows], part[2 * rows :].astype(BF16)
        if k:
            parts.append(down(near.astype(BF16), k))
            side_parts.append(down_across(far, k))
        else:
            parts.append(near)
            side_parts.append(to_side(far))
    out_got = to_side(side_out)
    out, query_grad = pl.pallas_call(
        finish_kernel,
        out_shape=[jax.ShapeDtypeStruct(queries.shape, BF16)] * 2,
        in_specs=[VMEM, HBM, HBM],
        out_specs=[HBM] * 2,
        compiler_params=SMALL,
        input_output_aliases={1: 0, 2: 1},
        scratch_shapes=[pltpu.SemaphoreType.DMA((2,))],
    )(out_got, out, query_grad)
    parts[0], out, query_grad = lax.optimization_barrier((parts[0], out, query_grad))
    grads, grads_got = (
        sum(part.astype(F32) for part in group).astype(BF16) for group in (parts, side_parts)
    )
    first = core_index() == 0
    grads = jnp.concatenate(
        [jnp.where(first, grads, grads_got), jnp.where(first, grads_got, grads)], axis=1
    )
    return (out[None], query_grad[None], grads[None, :rows], grads[None, rows:])


def solution(mesh):
    groups, ranks = mesh.devices.shape
    wide = Mesh(mesh.devices.reshape(2, groups // 2, ranks), ("half", "pair", "ctx"))
    spec3 = P(("half", "pair"), "ctx", None)
    in_specs = (spec3, spec3, spec3, spec3, P(("half", "pair"), "ctx"), spec3)
    return jax.shard_map(
        local, mesh=wide, in_specs=in_specs, out_specs=(spec3,) * 4, check_vma=False
    )
```

```python
import functools
import math

import jax
import jax.numpy as jnp
from jax import lax
from jax.experimental import pallas as pl
from jax.experimental.pallas import tpu as pltpu
from jax.sharding import Mesh
from jax.sharding import PartitionSpec as P

HEAD_SIZE = 128
QUERY_PER_KEY = 8
NBLK = 4
META = 16
DOC_ROW = NBLK
DOC_VALUES = 16
GROUPED = 4
HALF = QUERY_PER_KEY * HEAD_SIZE
NEG = -1e30
F32, BF16, I32 = jnp.float32, jnp.bfloat16, jnp.int32
NT = (((1,), (1,)), ((), ()))
VMEM = pl.BlockSpec(memory_space=pltpu.VMEM)
SMEM = pl.BlockSpec(memory_space=pltpu.SMEM)
HBM = pl.BlockSpec(memory_space=pltpu.HBM)
SMALL = pltpu.CompilerParams(vmem_limit_bytes=8 * 1024 * 1024)


def core_index():
    return lax.rem(lax.axis_index("ctx"), 2)


def payload_kernel(swap_ref, key_ref, value_ref, docs_ref, own_ref, side_ref):
    rows = key_ref.shape[0]
    core = core_index()
    docs = jnp.broadcast_to(docs_ref[...].astype(F32), (META, rows))
    place = lax.broadcasted_iota(I32, docs.shape, 0)
    meta = jnp.where(place == DOC_ROW, docs, 0.0)
    for block in range(NBLK):
        meta = jnp.where(place == block, swap_ref[block].astype(F32), meta)
    meta = meta.astype(BF16)
    for ref, head in ((own_ref, core), (side_ref, 1 - core)):
        lane = pl.ds(pl.multiple_of(head * HEAD_SIZE, HEAD_SIZE), HEAD_SIZE)
        ref[:rows, :] = key_ref[:, lane]
        ref[rows : 2 * rows, :] = value_ref[:, lane]
        ref[2 * rows :, :] = meta


def rows_kernel(other, query_ref, grad_ref, rows_ref, sems):
    rows = query_ref.shape[0]
    core = core_index()
    head = 1 - core if other else core
    lanes = pl.ds(pl.multiple_of(head * HALF, HALF), HALF)
    copies = [
        pltpu.make_async_copy(
            source.at[:, lanes], rows_ref.at[pl.ds(part * rows, rows), :], sems.at[part]
        )
        for part, source in enumerate((query_ref, grad_ref))
    ]
    for copy in copies:
        copy.start()
    for copy in copies:
        copy.wait()


def write_heads(source_ref, head, out_ref, query_grad_ref, sems):
    rows = out_ref.shape[0]
    lanes = pl.ds(pl.multiple_of(head * HALF, HALF), HALF)
    copies = [
        pltpu.make_async_copy(
            source_ref.at[pl.ds(part * rows, rows), :], target.at[:, lanes], sems.at[part]
        )
        for part, target in enumerate((out_ref, query_grad_ref))
    ]
    for copy in copies:
        copy.start()
    for copy in copies:
        copy.wait()


def own_kernel(own_ref, out_ref, query_grad_ref, sems):
    write_heads(own_ref, core_index(), out_ref, query_grad_ref, sems)


def finish_kernel(side_ref, out_held, query_grad_held, out_ref, query_grad_ref, sems):
    write_heads(side_ref, 1 - core_index(), out_ref, query_grad_ref, sems)


def merge_hop(home, away, slots_at, rows, logs):
    key_log, value_log, key_turned, value_turned = logs
    per_block = rows // NBLK
    size = 2 * rows + META
    for who in range(2):
        base = pl.multiple_of(slots_at[who] * rows, rows)
        flags = home[who * size + 2 * rows : (who + 1) * size, :].astype(F32)
        for which, log, turned in ((0, key_log, key_turned), (1, value_log, value_turned)):
            merged = ([], [])
            for block in range(NBLK):
                mask = (
                    jnp.broadcast_to(flags[block : block + 1, :], (per_block, HEAD_SIZE)).astype(BF16)
                    > 0.5
                )
                first = who * size + which * rows + block * per_block
                own = home[first : first + per_block, :]
                other = away[first : first + per_block, :]
                merged[0].append(jnp.where(mask, other, own))
                merged[1].append(jnp.where(mask, own, other))
            for logical in range(2):
                whole = jnp.concatenate(merged[logical], axis=0)
                log[logical, pl.ds(base, rows), :] = whole
                turned[logical, :, pl.ds(base, rows)] = whole.T


def prepare_kernel(hops, *refs):
    homes, aways = refs[:hops], refs[hops : 2 * hops]
    logs = refs[2 * hops :]
    rows = (homes[0].shape[0] // 2 - META) // 2
    core = core_index()
    parity = (core, 1 - core)
    for k in range(hops):
        slots_at = [2 * (hops - 1 - k) + parity[who] for who in range(2)]
        merge_hop(homes[k], aways[k], slots_at, rows, logs)


def attention_kernel(hops, rows_ref, *refs):
    count = hops + 1
    slots = 2 * count
    window = slots - 1
    homes, aways = refs[:count], refs[count : 2 * count]
    ready = refs[2 * count : 2 * count + 4]
    out_all = refs[2 * count + 4]
    home_outs = refs[2 * count + 5 : 3 * count + 5]
    away_outs = refs[3 * count + 5 : 4 * count + 5]
    (
        key_log,
        value_log,
        key_turned,
        value_turned,
        doc_window,
        starts,
        flag_rows,
        key_total,
        value_total,
        logical_of,
        needed_of,
        order_of,
    ) = refs[4 * count + 5 :]
    rows = rows_ref.shape[0] // 4
    per_block = rows // NBLK
    lanes = QUERY_PER_KEY * per_block
    size = 2 * rows + META
    core = core_index()
    chip = lax.axis_index("ctx") // 2
    parity = (core, 1 - core)
    scale = 1.0 / math.sqrt(HEAD_SIZE)
    factor = scale * math.log2(math.e)

    key_total[...] = jnp.zeros_like(key_total)
    value_total[...] = jnp.zeros_like(value_total)
    doc_window[...] = jnp.full_like(doc_window, 1e4)

    def meta_of(ref, who):
        return ref[who * size + 2 * rows : (who + 1) * size, :].astype(F32)

    for k in range(count):
        for who in range(2):
            slot = 2 * (hops - k) + parity[who]
            base = pl.multiple_of(slot * rows, rows)
            for logical, ref in ((0, homes[k]), (1, aways[k])):
                docs = meta_of(ref, who)[DOC_ROW : DOC_ROW + 1, :]
                doc_window[logical, pl.ds(slot, 1), :] = jnp.where(chip >= k, docs, -1.0)
    logs = (key_log, value_log, key_turned, value_turned)
    for log, held in zip(logs[:2], ready[:2]):
        log[:, pl.ds(2 * rows, 2 * rows * hops), :] = held[...]
    for log, held in zip(logs[2:], ready[2:]):
        log[:, :, pl.ds(2 * rows, 2 * rows * hops)] = held[...]
    merge_hop(homes[hops], aways[hops], parity, rows, logs)

    values_down = lax.broadcasted_iota(I32, (DOC_VALUES, rows), 0).astype(F32)
    group = lax.broadcasted_iota(I32, (8, rows), 1) // per_block
    meta_rows = [meta_of(homes[0], who) for who in range(2)]
    for logical in range(2):
        lower = jnp.zeros((DOC_VALUES, rows), F32)
        for slot in range(slots):
            docs = jnp.broadcast_to(doc_window[logical, slot : slot + 1, :], lower.shape)
            lower = lower + jnp.where(docs < values_down, 1.0, 0.0)
        lower = jnp.broadcast_to(jnp.sum(lower, axis=1, keepdims=True), lower.shape)
        for who in range(2):
            docs = meta_of((homes, aways)[logical][0], who)[DOC_ROW : DOC_ROW + 1, :]
            docs = jnp.broadcast_to(docs, (8, rows))
            turns = [docs] + [pltpu.roll(docs, t * per_block, 1) for t in range(1, NBLK)]
            for block in range(NBLK):
                tiled = turns[0]
                for t in range(1, NBLK):
                    tiled = jnp.where(group == (block + t) % NBLK, turns[t], tiled)
                tiled = jnp.broadcast_to(tiled[:1], lower.shape)
                start = jnp.sum(jnp.where(tiled == values_down, lower, 0.0), axis=0, keepdims=True)
                starts[logical, who * NBLK + block : who * NBLK + block + 1, :] = start.astype(I32)
    for who in range(2):
        flag_rows[who * NBLK : (who + 1) * NBLK, :] = meta_rows[who][:NBLK, :]
    flags = flag_rows[...]
    firsts = [
        jnp.broadcast_to(
            jnp.min(starts[logical].astype(F32), axis=1, keepdims=True), flags.shape
        )
        for logical in range(2)
    ]
    first = jnp.where(flags > 0.5, firsts[1], firsts[0]).astype(I32)
    flags = flags.astype(I32)
    needs = [
        window + parity[index // NBLK] - first[index, 0] // rows for index in range(2 * NBLK)
    ]
    for index, need in enumerate(needs):
        place = jnp.int32(0)
        for other, its_need in enumerate(needs):
            if other != index:
                ahead = its_need >= need if other < index else its_need > need
                place = place + ahead.astype(I32)
        order_of[place] = index
        logical_of[index] = flags[index, 0]
        needed_of[index] = need

    def unit(unit_index, chunks):
        who, block = unit_index // NBLK, lax.rem(unit_index, NBLK)
        logical = logical_of[unit_index]
        row_parity = jnp.where(who == 0, core, 1 - core)
        first_slot = window + row_parity - chunks
        first = pl.multiple_of(first_slot * rows, rows)
        span = pl.ds(first, chunks * rows)
        columns = [slice(h * HEAD_SIZE, (h + 1) * HEAD_SIZE) for h in range(QUERY_PER_KEY)]
        query_at = pl.ds(pl.multiple_of(2 * who * rows + block * per_block, per_block), per_block)
        grad_at = pl.ds(
            pl.multiple_of((2 * who + 1) * rows + block * per_block, per_block), per_block
        )
        query = jnp.concatenate([rows_ref[query_at, column] for column in columns], axis=0)
        grad = jnp.concatenate([rows_ref[grad_at, column] for column in columns], axis=0)
        scores = lax.dot_general(key_log[logical, span, :], query, NT, preferred_element_type=F32)
        shape = (chunks * rows, HEAD_SIZE)
        key_place = lax.broadcasted_iota(I32, shape, 0)
        row_first = starts[logical, pl.ds(unit_index, 1), :] - first
        row_last = (
            (chunks - 1) * rows
            + block * per_block
            + lax.rem(lax.broadcasted_iota(I32, (1, HEAD_SIZE), 1), per_block)
        )
        allowed = (key_place >= row_first) & (key_place <= row_last)
        scores = jnp.concatenate(
            [
                jnp.where(allowed, scores[:, lane : lane + HEAD_SIZE], NEG)
                for lane in range(0, lanes, HEAD_SIZE)
            ],
            axis=1,
        )
        peak = jnp.max(scores, axis=0, keepdims=True)
        powers = jnp.exp2((scores - peak) * factor)
        inverse = 1.0 / jnp.sum(powers, axis=0, keepdims=True)
        probs = powers * inverse
        weights = probs.astype(BF16)
        out_turned = jnp.dot(
            value_turned[logical, :, span], weights, preferred_element_type=F32
        ).astype(BF16)
        delta = jnp.sum(grad.T.astype(F32) * out_turned.astype(F32), axis=0, keepdims=True)
        prob_grad = lax.dot_general(
            value_log[logical, span, :], grad, NT, preferred_element_type=F32
        )
        score_grad = (probs * (prob_grad - delta)).astype(BF16)
        query_grad_turned = jnp.dot(
            key_turned[logical, :, span], score_grad, preferred_element_type=F32
        )
        key_add = jnp.dot(score_grad, query, preferred_element_type=F32)
        value_add = jnp.dot(weights, grad, preferred_element_type=F32)
        out = out_turned.T
        query_grad = (query_grad_turned * scale).astype(BF16).T
        return query_at, grad_at, logical, span, out, query_grad, key_add, value_add

    def step(pair, carry):
        members = [order_of[pair * GROUPED + m] for m in range(GROUPED)]
        needed = needed_of[members[0]]
        for chunks in range(1, window + 1):

            @pl.when(needed == chunks)
            def _(chunks=chunks):
                results = [unit(member, chunks) for member in members]
                for query_at, grad_at, logical, span, out, query_grad, key_add, value_add in results:
                    key_total[logical, span, :] += key_add
                    value_total[logical, span, :] += value_add
                    for h in range(QUERY_PER_KEY):
                        column = slice(h * HEAD_SIZE, (h + 1) * HEAD_SIZE)
                        part = slice(h * per_block, (h + 1) * per_block)
                        out_all[query_at, column] = out[part, :]
                        out_all[grad_at, column] = query_grad[part, :]

        return carry

    lax.fori_loop(0, 2 * NBLK // GROUPED, step, 0)
    for k in range(count):
        for who in range(2):
            base = pl.multiple_of((2 * (hops - k) + parity[who]) * rows, rows)
            flags = meta_of(homes[k], who)
            for block in range(NBLK):
                at = pl.ds(base + block * per_block, per_block)
                mask = jnp.broadcast_to(flags[block : block + 1, :], (per_block, HEAD_SIZE)) > 0.5
                for which, total, gain in ((0, key_total, scale), (1, value_total, 1.0)):
                    part = (2 * who + which) * rows + block * per_block
                    first = total[0, at, :] * gain
                    second = total[1, at, :] * gain
                    home_outs[k][part : part + per_block, :] = jnp.where(mask, second, first).astype(BF16)
                    away_outs[k][part : part + per_block, :] = jnp.where(mask, first, second).astype(BF16)


def local(queries, key_rows, value_rows, out_grad, documents, swapped):
    ranks = lax.axis_size("ctx")
    hops = ranks // 4
    count = hops + 1
    slots = 2 * count
    rows, width = key_rows.shape[1:]
    keys = slots * rows
    size = 2 * rows + META
    queries, out_grad = queries[0], out_grad[0]

    def up(block, k):
        return lax.ppermute(block, "ctx", [(i, i + 2 * k) for i in range(ranks - 2 * k)])

    def down(block, k):
        return lax.ppermute(block, "ctx", [(i + 2 * k, i) for i in range(ranks - 2 * k)])

    def to_partner(block):
        return lax.ppermute(block, "half", [(0, 1), (1, 0)])

    def to_side(block):
        return lax.ppermute(block, "ctx", [(i, i ^ 1) for i in range(ranks)])

    payload, payload_side = pl.pallas_call(
        payload_kernel,
        out_shape=[pltpu.VMEM((size, HEAD_SIZE), BF16)] * 2,
        in_specs=[SMEM, VMEM, VMEM, VMEM],
        out_specs=[VMEM, VMEM],
    )(swapped[0, 0], key_rows[0], value_rows[0], documents)
    from_side = to_side(payload_side)

    def rows_of(other, queries, out_grad):
        return pl.pallas_call(
            functools.partial(rows_kernel, other),
            out_shape=pltpu.VMEM((2 * rows, HALF), BF16),
            in_specs=[HBM, HBM],
            out_specs=VMEM,
            scratch_shapes=[pltpu.SemaphoreType.DMA((2,))],
            compiler_params=None if other else SMALL,
        )(queries, out_grad)

    both = jnp.concatenate([payload, from_side], axis=0)
    rows_side = rows_of(True, queries, out_grad)
    both, rows_side = lax.optimization_barrier((both, rows_side))
    rows_got = to_side(rows_side)
    home = [both] + [up(both, k) for k in range(1, count)]
    away = [to_partner(block) for block in home]
    *early, home[hops], queries, out_grad = lax.optimization_barrier(
        (*home[:hops], *away[:hops], home[hops], queries, out_grad)
    )
    rows_all = jnp.concatenate([rows_of(False, queries, out_grad), rows_got], axis=0)
    ready = pl.pallas_call(
        functools.partial(prepare_kernel, hops),
        out_shape=[pltpu.VMEM((2, 2 * rows * hops, HEAD_SIZE), BF16)] * 2
        + [pltpu.VMEM((2, HEAD_SIZE, 2 * rows * hops), BF16)] * 2,
        in_specs=[VMEM] * (2 * hops),
        out_specs=[VMEM] * 4,
        compiler_params=SMALL,
        cost_estimate=pl.CostEstimate(flops=0, bytes_accessed=4 * 1024 * 1024, transcendentals=0),
    )(*early)
    chunk = pltpu.VMEM((4 * rows, HEAD_SIZE), BF16)
    outs = pl.pallas_call(
        functools.partial(attention_kernel, hops),
        out_shape=[pltpu.VMEM((4 * rows, HALF), BF16)] + [chunk] * (2 * count),
        in_specs=[VMEM] * (5 + 2 * count),
        out_specs=[VMEM] * (1 + 2 * count),
        scratch_shapes=[
            pltpu.VMEM((2, keys, HEAD_SIZE), BF16),
            pltpu.VMEM((2, keys, HEAD_SIZE), BF16),
            pltpu.VMEM((2, HEAD_SIZE, keys), BF16),
            pltpu.VMEM((2, HEAD_SIZE, keys), BF16),
            pltpu.VMEM((2, 16, rows), F32),
            pltpu.VMEM((2, 8, rows), I32),
            pltpu.VMEM((8, rows), F32),
            pltpu.VMEM((2, keys, HEAD_SIZE), F32),
            pltpu.VMEM((2, keys, HEAD_SIZE), F32),
            pltpu.SMEM((2 * NBLK,), I32),
            pltpu.SMEM((2 * NBLK,), I32),
            pltpu.SMEM((2 * NBLK,), I32),
        ],
        compiler_params=pltpu.CompilerParams(vmem_limit_bytes=32 * 1024 * 1024),
        cost_estimate=pl.CostEstimate(
            flops=12 * rows * keys * 2048,
            bytes_accessed=4 * 1024 * 1024,
            transcendentals=rows * keys * 16,
        ),
    )(rows_all, *home, *away, *ready)
    home_sum, away_sum = outs[1 : 1 + count], outs[1 + count :]
    side_out = outs[0][2 * rows :]
    out, query_grad = pl.pallas_call(
        own_kernel,
        out_shape=[jax.ShapeDtypeStruct(queries.shape, BF16)] * 2,
        in_specs=[VMEM],
        out_specs=[HBM] * 2,
        compiler_params=SMALL,
        scratch_shapes=[pltpu.SemaphoreType.DMA((2,))],
        cost_estimate=pl.CostEstimate(flops=0, bytes_accessed=4 * 1024 * 1024, transcendentals=0),
    )(outs[0])

    parts = []
    for k in reversed(range(count)):
        crossed = to_partner(away_sum[k])
        part = home_sum[k].astype(F32) + crossed.astype(F32)
        if k:
            part = part.astype(BF16)
            part = down(part, k)
        parts.append(part)
    out_got = to_side(side_out)
    out, query_grad = pl.pallas_call(
        finish_kernel,
        out_shape=[jax.ShapeDtypeStruct(queries.shape, BF16)] * 2,
        in_specs=[VMEM, HBM, HBM],
        out_specs=[HBM] * 2,
        compiler_params=SMALL,
        input_output_aliases={1: 0, 2: 1},
        scratch_shapes=[pltpu.SemaphoreType.DMA((2,))],
    )(out_got, out, query_grad)
    parts[0], out, query_grad = lax.optimization_barrier((parts[0], out, query_grad))
    total = sum(part.astype(F32) for part in parts).astype(BF16)
    grads_got = to_side(total[2 * rows :])
    grads = total[: 2 * rows]
    first = core_index() == 0
    grads = jnp.concatenate(
        [jnp.where(first, grads, grads_got), jnp.where(first, grads_got, grads)], axis=1
    )
    return (out[None], query_grad[None], grads[None, :rows], grads[None, rows:])


def solution(mesh):
    groups, ranks = mesh.devices.shape
    wide = Mesh(mesh.devices.reshape(2, groups // 2, ranks), ("half", "pair", "ctx"))
    spec3 = P(("half", "pair"), "ctx", None)
    in_specs = (spec3, spec3, spec3, spec3, P(("half", "pair"), "ctx"), spec3)
    return jax.shard_map(
        local, mesh=wide, in_specs=in_specs, out_specs=(spec3,) * 4, check_vma=False
    )
```

```python
import functools
import math

import jax
import jax.numpy as jnp
from jax import lax
from jax.experimental import pallas as pl
from jax.experimental.pallas import tpu as pltpu
from jax.sharding import Mesh
from jax.sharding import PartitionSpec as P

HEAD_SIZE = 128
QUERY_PER_KEY = 8
NBLK = 4
META = 16
DOC_ROW = NBLK
DOC_VALUES = 16
GROUPED = 2
HALF = QUERY_PER_KEY * HEAD_SIZE
NEG = -1e30
F32, BF16, I32 = jnp.float32, jnp.bfloat16, jnp.int32
NT = (((1,), (1,)), ((), ()))
VMEM = pl.BlockSpec(memory_space=pltpu.VMEM)
SMEM = pl.BlockSpec(memory_space=pltpu.SMEM)
HBM = pl.BlockSpec(memory_space=pltpu.HBM)
SMALL = pltpu.CompilerParams(vmem_limit_bytes=8 * 1024 * 1024)


def core_index():
    return lax.rem(lax.axis_index("ctx"), 2)


def payload_kernel(swap_ref, key_ref, value_ref, docs_ref, own_ref, side_ref):
    rows = key_ref.shape[0]
    core = core_index()
    docs = jnp.broadcast_to(docs_ref[...].astype(F32), (META, rows))
    place = lax.broadcasted_iota(I32, docs.shape, 0)
    meta = jnp.where(place == DOC_ROW, docs, 0.0)
    for block in range(NBLK):
        meta = jnp.where(place == block, swap_ref[block].astype(F32), meta)
    meta = meta.astype(BF16)
    for ref, head in ((own_ref, core), (side_ref, 1 - core)):
        lane = pl.ds(pl.multiple_of(head * HEAD_SIZE, HEAD_SIZE), HEAD_SIZE)
        ref[:rows, :] = key_ref[:, lane]
        ref[rows : 2 * rows, :] = value_ref[:, lane]
        ref[2 * rows :, :] = meta


def rows_kernel(other, query_ref, grad_ref, rows_ref, sems):
    rows = query_ref.shape[0]
    core = core_index()
    head = 1 - core if other else core
    lanes = pl.ds(pl.multiple_of(head * HALF, HALF), HALF)
    copies = [
        pltpu.make_async_copy(
            source.at[:, lanes], rows_ref.at[pl.ds(part * rows, rows), :], sems.at[part]
        )
        for part, source in enumerate((query_ref, grad_ref))
    ]
    for copy in copies:
        copy.start()
    for copy in copies:
        copy.wait()


def write_heads(source_ref, head, out_ref, query_grad_ref, sems):
    rows = out_ref.shape[0]
    lanes = pl.ds(pl.multiple_of(head * HALF, HALF), HALF)
    copies = [
        pltpu.make_async_copy(
            source_ref.at[pl.ds(part * rows, rows), :], target.at[:, lanes], sems.at[part]
        )
        for part, target in enumerate((out_ref, query_grad_ref))
    ]
    for copy in copies:
        copy.start()
    for copy in copies:
        copy.wait()


def own_kernel(own_ref, out_ref, query_grad_ref, sems):
    write_heads(own_ref, core_index(), out_ref, query_grad_ref, sems)


def finish_kernel(side_ref, out_held, query_grad_held, out_ref, query_grad_ref, sems):
    write_heads(side_ref, 1 - core_index(), out_ref, query_grad_ref, sems)


def merge_hop(home, away, slots_at, rows, logs):
    key_log, value_log, key_turned, value_turned = logs
    per_block = rows // NBLK
    size = 2 * rows + META
    for who in range(2):
        base = pl.multiple_of(slots_at[who] * rows, rows)
        flags = home[who * size + 2 * rows : (who + 1) * size, :].astype(F32)
        for which, log, turned in ((0, key_log, key_turned), (1, value_log, value_turned)):
            merged = ([], [])
            for block in range(NBLK):
                mask = (
                    jnp.broadcast_to(flags[block : block + 1, :], (per_block, HEAD_SIZE)).astype(BF16)
                    > 0.5
                )
                first = who * size + which * rows + block * per_block
                own = home[first : first + per_block, :]
                other = away[first : first + per_block, :]
                merged[0].append(jnp.where(mask, other, own))
                merged[1].append(jnp.where(mask, own, other))
            for logical in range(2):
                whole = jnp.concatenate(merged[logical], axis=0)
                log[logical, pl.ds(base, rows), :] = whole
                turned[logical, :, pl.ds(base, rows)] = whole.T


def prepare_kernel(hops, *refs):
    homes, aways = refs[:hops], refs[hops : 2 * hops]
    logs = refs[2 * hops :]
    rows = (homes[0].shape[0] // 2 - META) // 2
    core = core_index()
    parity = (core, 1 - core)
    for k in range(hops):
        slots_at = [2 * (hops - 1 - k) + parity[who] for who in range(2)]
        merge_hop(homes[k], aways[k], slots_at, rows, logs)


def attention_kernel(hops, rows_ref, *refs):
    count = hops + 1
    slots = 2 * count
    window = slots - 1
    homes, aways = refs[:count], refs[count : 2 * count]
    ready = refs[2 * count : 2 * count + 4]
    out_all = refs[2 * count + 4]
    home_outs = refs[2 * count + 5 : 3 * count + 5]
    away_outs = refs[3 * count + 5 : 4 * count + 5]
    (
        key_log,
        value_log,
        key_turned,
        value_turned,
        doc_window,
        starts,
        flag_rows,
        key_total,
        value_total,
        logical_of,
        needed_of,
        order_of,
    ) = refs[4 * count + 5 :]
    rows = rows_ref.shape[0] // 4
    per_block = rows // NBLK
    lanes = QUERY_PER_KEY * per_block
    size = 2 * rows + META
    core = core_index()
    chip = lax.axis_index("ctx") // 2
    parity = (core, 1 - core)
    scale = 1.0 / math.sqrt(HEAD_SIZE)
    factor = scale * math.log2(math.e)

    key_total[...] = jnp.zeros_like(key_total)
    value_total[...] = jnp.zeros_like(value_total)
    doc_window[...] = jnp.full_like(doc_window, 1e4)

    def meta_of(ref, who):
        return ref[who * size + 2 * rows : (who + 1) * size, :].astype(F32)

    for k in range(count):
        for who in range(2):
            slot = 2 * (hops - k) + parity[who]
            base = pl.multiple_of(slot * rows, rows)
            for logical, ref in ((0, homes[k]), (1, aways[k])):
                docs = meta_of(ref, who)[DOC_ROW : DOC_ROW + 1, :]
                doc_window[logical, pl.ds(slot, 1), :] = jnp.where(chip >= k, docs, -1.0)
    logs = (key_log, value_log, key_turned, value_turned)
    for log, held in zip(logs[:2], ready[:2]):
        log[:, pl.ds(2 * rows, 2 * rows * hops), :] = held[...]
    for log, held in zip(logs[2:], ready[2:]):
        log[:, :, pl.ds(2 * rows, 2 * rows * hops)] = held[...]
    merge_hop(homes[hops], aways[hops], parity, rows, logs)

    values_down = lax.broadcasted_iota(I32, (DOC_VALUES, rows), 0).astype(F32)
    group = lax.broadcasted_iota(I32, (8, rows), 1) // per_block
    meta_rows = [meta_of(homes[0], who) for who in range(2)]
    for logical in range(2):
        lower = jnp.zeros((DOC_VALUES, rows), F32)
        for slot in range(slots):
            docs = jnp.broadcast_to(doc_window[logical, slot : slot + 1, :], lower.shape)
            lower = lower + jnp.where(docs < values_down, 1.0, 0.0)
        lower = jnp.broadcast_to(jnp.sum(lower, axis=1, keepdims=True), lower.shape)
        for who in range(2):
            docs = meta_of((homes, aways)[logical][0], who)[DOC_ROW : DOC_ROW + 1, :]
            docs = jnp.broadcast_to(docs, (8, rows))
            turns = [docs] + [pltpu.roll(docs, t * per_block, 1) for t in range(1, NBLK)]
            for block in range(NBLK):
                tiled = turns[0]
                for t in range(1, NBLK):
                    tiled = jnp.where(group == (block + t) % NBLK, turns[t], tiled)
                tiled = jnp.broadcast_to(tiled[:1], lower.shape)
                start = jnp.sum(jnp.where(tiled == values_down, lower, 0.0), axis=0, keepdims=True)
                starts[logical, who * NBLK + block : who * NBLK + block + 1, :] = start.astype(I32)
    for who in range(2):
        flag_rows[who * NBLK : (who + 1) * NBLK, :] = meta_rows[who][:NBLK, :]
    flags = flag_rows[...]
    firsts = [
        jnp.broadcast_to(
            jnp.min(starts[logical].astype(F32), axis=1, keepdims=True), flags.shape
        )
        for logical in range(2)
    ]
    first = jnp.where(flags > 0.5, firsts[1], firsts[0]).astype(I32)
    flags = flags.astype(I32)
    needs = [
        window + parity[index // NBLK] - first[index, 0] // rows for index in range(2 * NBLK)
    ]
    for index, need in enumerate(needs):
        place = jnp.int32(0)
        for other, its_need in enumerate(needs):
            if other != index:
                ahead = its_need >= need if other < index else its_need > need
                place = place + ahead.astype(I32)
        order_of[place] = index
        logical_of[index] = flags[index, 0]
        needed_of[index] = need

    def unit(unit_index, chunks):
        who, block = unit_index // NBLK, lax.rem(unit_index, NBLK)
        logical = logical_of[unit_index]
        row_parity = jnp.where(who == 0, core, 1 - core)
        first_slot = window + row_parity - chunks
        first = pl.multiple_of(first_slot * rows, rows)
        span = pl.ds(first, chunks * rows)
        columns = [slice(h * HEAD_SIZE, (h + 1) * HEAD_SIZE) for h in range(QUERY_PER_KEY)]
        query_at = pl.ds(pl.multiple_of(2 * who * rows + block * per_block, per_block), per_block)
        grad_at = pl.ds(
            pl.multiple_of((2 * who + 1) * rows + block * per_block, per_block), per_block
        )
        query = jnp.concatenate([rows_ref[query_at, column] for column in columns], axis=0)
        grad = jnp.concatenate([rows_ref[grad_at, column] for column in columns], axis=0)
        scores = lax.dot_general(key_log[logical, span, :], query, NT, preferred_element_type=F32)
        shape = (chunks * rows, HEAD_SIZE)
        key_place = lax.broadcasted_iota(I32, shape, 0)
        row_first = starts[logical, pl.ds(unit_index, 1), :] - first
        row_last = (
            (chunks - 1) * rows
            + block * per_block
            + lax.rem(lax.broadcasted_iota(I32, (1, HEAD_SIZE), 1), per_block)
        )
        allowed = (key_place >= row_first) & (key_place <= row_last)
        scores = jnp.concatenate(
            [
                jnp.where(allowed, scores[:, lane : lane + HEAD_SIZE], NEG)
                for lane in range(0, lanes, HEAD_SIZE)
            ],
            axis=1,
        )
        peak = jnp.max(scores, axis=0, keepdims=True)
        powers = jnp.exp2((scores - peak) * factor)
        inverse = 1.0 / jnp.sum(powers, axis=0, keepdims=True)
        probs = powers * inverse
        weights = probs.astype(BF16)
        out_turned = jnp.dot(
            value_turned[logical, :, span], weights, preferred_element_type=F32
        ).astype(BF16)
        delta = jnp.sum(grad.T.astype(F32) * out_turned.astype(F32), axis=0, keepdims=True)
        prob_grad = lax.dot_general(
            value_log[logical, span, :], grad, NT, preferred_element_type=F32
        )
        score_grad = (probs * (prob_grad - delta)).astype(BF16)
        query_grad_turned = jnp.dot(
            key_turned[logical, :, span], score_grad, preferred_element_type=F32
        )
        key_add = jnp.dot(score_grad, query, preferred_element_type=F32)
        value_add = jnp.dot(weights, grad, preferred_element_type=F32)
        out = out_turned.T
        query_grad = (query_grad_turned * scale).astype(BF16).T
        return query_at, grad_at, logical, span, out, query_grad, key_add, value_add

    def step(pair, carry):
        members = [order_of[pair * GROUPED + m] for m in range(GROUPED)]
        needed = needed_of[members[0]]
        for chunks in range(1, window + 1):

            @pl.when(needed == chunks)
            def _(chunks=chunks):
                results = [unit(member, chunks) for member in members]
                for query_at, grad_at, logical, span, out, query_grad, key_add, value_add in results:
                    key_total[logical, span, :] += key_add
                    value_total[logical, span, :] += value_add
                    for h in range(QUERY_PER_KEY):
                        column = slice(h * HEAD_SIZE, (h + 1) * HEAD_SIZE)
                        part = slice(h * per_block, (h + 1) * per_block)
                        out_all[query_at, column] = out[part, :]
                        out_all[grad_at, column] = query_grad[part, :]

        return carry

    lax.fori_loop(0, 2 * NBLK // GROUPED, step, 0)
    for k in range(count):
        for who in range(2):
            base = pl.multiple_of((2 * (hops - k) + parity[who]) * rows, rows)
            flags = meta_of(homes[k], who)
            for block in range(NBLK):
                at = pl.ds(base + block * per_block, per_block)
                mask = jnp.broadcast_to(flags[block : block + 1, :], (per_block, HEAD_SIZE)) > 0.5
                for which, total, gain in ((0, key_total, scale), (1, value_total, 1.0)):
                    part = (2 * who + which) * rows + block * per_block
                    first = total[0, at, :] * gain
                    second = total[1, at, :] * gain
                    home_outs[k][part : part + per_block, :] = jnp.where(mask, second, first).astype(BF16)
                    away_outs[k][part : part + per_block, :] = jnp.where(mask, first, second).astype(BF16)


def local(queries, key_rows, value_rows, out_grad, documents, swapped):
    ranks = lax.axis_size("ctx")
    hops = ranks // 4
    count = hops + 1
    slots = 2 * count
    rows, width = key_rows.shape[1:]
    keys = slots * rows
    size = 2 * rows + META
    queries, out_grad = queries[0], out_grad[0]

    def up(block, k):
        return lax.ppermute(block, "ctx", [(i, i + 2 * k) for i in range(ranks - 2 * k)])

    def down(block, k):
        return lax.ppermute(block, "ctx", [(i + 2 * k, i) for i in range(ranks - 2 * k)])

    def to_partner(block):
        return lax.ppermute(block, "half", [(0, 1), (1, 0)])

    def to_side(block):
        return lax.ppermute(block, "ctx", [(i, i ^ 1) for i in range(ranks)])

    payload, payload_side = pl.pallas_call(
        payload_kernel,
        out_shape=[pltpu.VMEM((size, HEAD_SIZE), BF16)] * 2,
        in_specs=[SMEM, VMEM, VMEM, VMEM],
        out_specs=[VMEM, VMEM],
    )(swapped[0, 0], key_rows[0], value_rows[0], documents)
    from_side = to_side(payload_side)

    def rows_of(other, queries, out_grad):
        return pl.pallas_call(
            functools.partial(rows_kernel, other),
            out_shape=pltpu.VMEM((2 * rows, HALF), BF16),
            in_specs=[HBM, HBM],
            out_specs=VMEM,
            scratch_shapes=[pltpu.SemaphoreType.DMA((2,))],
            compiler_params=None if other else SMALL,
        )(queries, out_grad)

    both = jnp.concatenate([payload, from_side], axis=0)
    rows_side = rows_of(True, queries, out_grad)
    both, rows_side = lax.optimization_barrier((both, rows_side))
    rows_got = to_side(rows_side)
    home = [both] + [up(both, k) for k in range(1, count)]
    away = [to_partner(block) for block in home]
    *early, home[hops], queries, out_grad = lax.optimization_barrier(
        (*home[:hops], *away[:hops], home[hops], queries, out_grad)
    )
    rows_all = jnp.concatenate([rows_of(False, queries, out_grad), rows_got], axis=0)
    ready = pl.pallas_call(
        functools.partial(prepare_kernel, hops),
        out_shape=[pltpu.VMEM((2, 2 * rows * hops, HEAD_SIZE), BF16)] * 2
        + [pltpu.VMEM((2, HEAD_SIZE, 2 * rows * hops), BF16)] * 2,
        in_specs=[VMEM] * (2 * hops),
        out_specs=[VMEM] * 4,
        compiler_params=SMALL,
        cost_estimate=pl.CostEstimate(flops=0, bytes_accessed=4 * 1024 * 1024, transcendentals=0),
    )(*early)
    chunk = pltpu.VMEM((4 * rows, HEAD_SIZE), BF16)
    outs = pl.pallas_call(
        functools.partial(attention_kernel, hops),
        out_shape=[pltpu.VMEM((4 * rows, HALF), BF16)] + [chunk] * (2 * count),
        in_specs=[VMEM] * (5 + 2 * count),
        out_specs=[VMEM] * (1 + 2 * count),
        scratch_shapes=[
            pltpu.VMEM((2, keys, HEAD_SIZE), BF16),
            pltpu.VMEM((2, keys, HEAD_SIZE), BF16),
            pltpu.VMEM((2, HEAD_SIZE, keys), BF16),
            pltpu.VMEM((2, HEAD_SIZE, keys), BF16),
            pltpu.VMEM((2, 16, rows), F32),
            pltpu.VMEM((2, 8, rows), I32),
            pltpu.VMEM((8, rows), F32),
            pltpu.VMEM((2, keys, HEAD_SIZE), F32),
            pltpu.VMEM((2, keys, HEAD_SIZE), F32),
            pltpu.SMEM((2 * NBLK,), I32),
            pltpu.SMEM((2 * NBLK,), I32),
            pltpu.SMEM((2 * NBLK,), I32),
        ],
        compiler_params=pltpu.CompilerParams(vmem_limit_bytes=32 * 1024 * 1024),
        cost_estimate=pl.CostEstimate(
            flops=12 * rows * keys * 2048,
            bytes_accessed=4 * 1024 * 1024,
            transcendentals=rows * keys * 16,
        ),
    )(rows_all, *home, *away, *ready)
    home_sum, away_sum = outs[1 : 1 + count], outs[1 + count :]
    side_out = outs[0][2 * rows :]
    out, query_grad = pl.pallas_call(
        own_kernel,
        out_shape=[jax.ShapeDtypeStruct(queries.shape, BF16)] * 2,
        in_specs=[VMEM],
        out_specs=[HBM] * 2,
        compiler_params=SMALL,
        scratch_shapes=[pltpu.SemaphoreType.DMA((2,))],
        cost_estimate=pl.CostEstimate(flops=0, bytes_accessed=4 * 1024 * 1024, transcendentals=0),
    )(outs[0])

    parts = []
    for k in reversed(range(count)):
        crossed = to_partner(away_sum[k])
        part = home_sum[k].astype(F32) + crossed.astype(F32)
        if k:
            part = part.astype(BF16)
            part = down(part, k)
        parts.append(part)
    out_got = to_side(side_out)
    out, query_grad = pl.pallas_call(
        finish_kernel,
        out_shape=[jax.ShapeDtypeStruct(queries.shape, BF16)] * 2,
        in_specs=[VMEM, HBM, HBM],
        out_specs=[HBM] * 2,
        compiler_params=SMALL,
        input_output_aliases={1: 0, 2: 1},
        scratch_shapes=[pltpu.SemaphoreType.DMA((2,))],
    )(out_got, out, query_grad)
    parts[0], out, query_grad = lax.optimization_barrier((parts[0], out, query_grad))
    total = sum(part.astype(F32) for part in parts).astype(BF16)
    grads_got = to_side(total[2 * rows :])
    grads = total[: 2 * rows]
    first = core_index() == 0
    grads = jnp.concatenate(
        [jnp.where(first, grads, grads_got), jnp.where(first, grads_got, grads)], axis=1
    )
    return (out[None], query_grad[None], grads[None, :rows], grads[None, rows:])


def solution(mesh):
    groups, ranks = mesh.devices.shape
    wide = Mesh(mesh.devices.reshape(2, groups // 2, ranks), ("half", "pair", "ctx"))
    spec3 = P(("half", "pair"), "ctx", None)
    in_specs = (spec3, spec3, spec3, spec3, P(("half", "pair"), "ctx"), spec3)
    return jax.shard_map(
        local, mesh=wide, in_specs=in_specs, out_specs=(spec3,) * 4, check_vma=False
    )
```
